32 devices in a mesh: dp: 4 (over z), fsdp: 8 (over y, x, core).
Axes of the slice: x: 2, y: 2, z: 4, core: 2. Of those that a mesh axis runs over, the one named last changes fastest.
Arguments:
- frames: bfloat16 [2, 32, 384, 512], P(None, ('dp', 'fsdp')), may hold values from -6 to 6
- upstream: bfloat16 [2, 32, 384, 512], P(None, ('dp', 'fsdp')), may hold values from -6 to 6
- utterance: int32 [2, 32, 24], P(None, ('dp', 'fsdp')), may hold values from 0 to 5, never falling along the last dimension, each value on 1 to 8 neighbouring positions
- first_gain: bfloat16 [512], P('fsdp'), may hold values from 0.099609375 to 1.8984375
- first_shift: bfloat16 [512], P('fsdp'), may hold values from -3 to 3
- project_in: bfloat16 [512, 1536], P('fsdp'), may hold values from -0.25 to 0.25
- query_bias: bfloat16 [512], P('fsdp'), may hold values from -3 to 3
- value_bias: bfloat16 [512], P('fsdp'), may hold values from -3 to 3
- project_out: bfloat16 [512, 512], P('fsdp'), may hold values from -0.75 to 0.75
- out_bias: bfloat16 [512], P('fsdp'), may hold values from -3 to 3
- second_gain: bfloat16 [512], P('fsdp'), may hold values from 0.099609375 to 1.8984375
- second_shift: bfloat16 [512], P('fsdp'), may hold values from -3 to 3
- up_weight: bfloat16 [512, 2048], P('fsdp'), may hold values from -0.25 to 0.25
- up_bias: bfloat16 [2048], P('fsdp'), may hold values from -3 to 3
- down_weight: bfloat16 [2048, 512], P('fsdp'), may hold values from -0.1875 to 0.1875
- down_bias: bfloat16 [512], P('fsdp'), may hold values from -3 to 3
Outputs:
- output: bfloat16 [2, 32, 384, 512], P(None, ('dp', 'fsdp'))
- grad_frames: float32 [2, 32, 384, 512], P(None, ('dp', 'fsdp'))
- grad_first_gain: float32 [512], P('fsdp')
- grad_first_shift: float32 [512], P('fsdp')
- grad_project_in: float32 [512, 1536], P('fsdp')
- grad_query_bias: float32 [512], P('fsdp')
- grad_value_bias: float32 [512], P('fsdp')
- grad_project_out: float32 [512, 512], P('fsdp')
- grad_out_bias: float32 [512], P('fsdp')
- grad_second_gain: float32 [512], P('fsdp')
- grad_second_shift: float32 [512], P('fsdp')
- grad_up_weight: float32 [512, 2048], P('fsdp')
- grad_up_bias: float32 [2048], P('fsdp')
- grad_down_weight: float32 [2048, 512], P('fsdp')
- grad_down_bias: float32 [512], P('fsdp')
The draws below stay inside these ranges and needn't reach their ends.
Inputs may be any that keep to these rules, and one draw needn't show every extreme that they name: In each packed row the utterance numbers never fall, every utterance covers 1 to 8 consecutive segments, and some utterance covers exactly 8.
All inputs are finite; a program needn't handle non-finite values.
Results may differ from the reference program's by a relative error of at most 0.023.
Values may be sent and summed in bfloat16 or wider, within the bound.
No kernel may reach another device: no remote copies, remote signals or barrier semaphores. Data moves between devices by JAX's collectives and lax.ppermute only.
A program may use at most 192 MiB of HBM per device.

```python
import math
import jax
import jax.numpy as jnp
import numpy as np
from jax import lax

D = 512
HEADS = 8
FF = 2048
SEG = 16
RIGHT = 4
LEFT = 30
MEMS = 4
MB = 2
ROW_LEN = 384
SEGS = 24
UTTS = 6
UTT_MOST = 8
ROWS = 32
N_DP = 4


def levels(own_key, shape, pieces, smallest, high):
    factor_of = 1.0
    for axis_at, parts in pieces:
        draws = jax.random.uniform(jax.random.fold_in(jax.random.fold_in(own_key, 6), axis_at), (parts,), jnp.float32, smallest / len(pieces), high / len(pieces))
        factor_of = factor_of * jnp.repeat(jnp.exp(draws), shape[axis_at] // parts).reshape((-1,) + (1,) * (len(shape) - 1 - axis_at))
    return factor_of


def split_up(number_of, total, reach, skew):
    weights = [(1 << 20) // math.isqrt(grade ** skew) + 1 for grade in range(2, number_of + 1)]
    rest, given = total - reach - (number_of - 1), [1] * (number_of - 1)
    while rest > 0:
        free = [i for i in range(number_of - 1) if given[i] < reach]
        whole, remaining = sum([weights[i] for i in free]), rest
        for i in free:
            addition = min(reach - given[i], max(1, remaining * weights[i] // whole), rest)
            given[i] = given[i] + addition
            rest = rest - addition
    return np.array([reach] + given)


def uneven(key, amount, total, most, skew):
    if amount == 2:
        one = jax.random.randint(key, (), max(1, total - most), min(most, total - 1) + 1)
        return jnp.stack([one, total - one])
    tallies = jnp.asarray(split_up(amount, total, most, skew), jnp.int32)
    couples = (amount - 1) // 2
    source_of, taker = tallies[1:1 + 2 * couples:2], tallies[2:2 + 2 * couples:2]
    room = jnp.minimum(source_of - 1, most - taker)
    shifted = jax.random.randint(jax.random.fold_in(key, 1), (couples,), 0, 1 << 20) % (room + 1)
    tallies = tallies.at[1:1 + 2 * couples:2].set(source_of - shifted).at[2:2 + 2 * couples:2].set(taker + shifted)
    return tallies[jax.random.permutation(jax.random.fold_in(key, 2), amount)]


def normal_values(own_key, extent, scale, bound, shards=(), kind=jnp.bfloat16):
    drawn = scale * jax.random.normal(own_key, extent, jnp.float32)
    if shards:
        drawn = drawn * levels(own_key, extent, shards, -0.22, 0.18)
    return jnp.clip(drawn, -bound, bound).astype(kind)


def setup_inputs(seed: int = 0) -> dict:
    streams_of = jax.random.split(jax.random.key(seed), 17)
    frames = normal_values(streams_of[0], (MB, ROWS, ROW_LEN, D), 1.0, 6.0, ((1, 32),))
    upstream = normal_values(streams_of[1], (MB, ROWS, ROW_LEN, D), 1.0, 6.0, ((1, 32),))
    utterance = jax.vmap(lambda own: jnp.searchsorted(jnp.cumsum(uneven(own, UTTS, SEGS, UTT_MOST, 2)), jnp.arange(SEGS), side="right"))(jax.random.split(streams_of[2], MB * ROWS)).reshape((MB, ROWS, SEGS)).astype(jnp.int32)
    first_gain = jnp.clip(1.0 + 0.18 * jax.random.normal(streams_of[3], (D,), jnp.float32), 0.099609375, 1.8984375).astype(jnp.bfloat16)
    first_shift = normal_values(streams_of[4], (D,), 0.5, 3.0, ((0, 8),))
    project_in = normal_values(streams_of[5], (D, 3 * D), D ** -0.5, 0.25, ((0, 8),))
    query_bias = normal_values(streams_of[6], (D,), 0.5, 3.0, ((0, 8),))
    value_bias = normal_values(streams_of[7], (D,), 0.5, 3.0, ((0, 8),))
    project_out = normal_values(streams_of[8], (D, D), (D // 8) ** -0.5, 0.75, ((0, 8),))
    out_bias = normal_values(streams_of[9], (D,), 0.5, 3.0, ((0, 8),))
    second_gain = jnp.clip(1.0 + 0.18 * jax.random.normal(streams_of[10], (D,), jnp.float32), 0.099609375, 1.8984375).astype(jnp.bfloat16)
    second_shift = normal_values(streams_of[11], (D,), 0.5, 3.0, ((0, 8),))
    up_weight = normal_values(streams_of[12], (D, FF), D ** -0.5, 0.25, ((0, 8),))
    up_bias = normal_values(streams_of[13], (FF,), 0.5, 3.0, ((0, 8),))
    down_weight = normal_values(streams_of[14], (FF, D), (FF // 2) ** -0.5, 0.1875, ((0, 8),))
    down_bias = normal_values(streams_of[15], (D,), 0.5, 3.0, ((0, 8),))
    return {"frames": frames, "upstream": upstream, "utterance": utterance, "first_gain": first_gain, "first_shift": first_shift, "project_in": project_in, "query_bias": query_bias, "value_bias": value_bias, "project_out": project_out, "out_bias": out_bias, "second_gain": second_gain, "second_shift": second_shift, "up_weight": up_weight, "up_bias": up_bias, "down_weight": down_weight, "down_bias": down_bias}


@jax.custom_vjp
def low(v):
    return lax.optimization_barrier(v.astype(jnp.bfloat16)).astype(jnp.float32)

@jax.custom_vjp
def low_back(v):
    return v

def low_keep(v):
    return (low(v), None)

def low_pass(kept, grad):
    return (grad,)

def back_keep(v):
    return (v, None)

def back_low(kept, grad):
    return (low(grad),)
low.defvjp(low_keep, low_pass)
low_back.defvjp(back_keep, back_low)

def layer_norm(value, gain, shift):
    center = lax.optimization_barrier(jnp.mean(value, axis=-1, keepdims=True))
    offset = value - center
    spread = lax.optimization_barrier(jnp.mean(offset * offset, axis=-1, keepdims=True))
    return offset * lax.rsqrt(spread + 1e-05) * gain + shift

def matmul(left, right):
    return jnp.dot(left, right, precision=lax.Precision.HIGHEST)

def row_attention(query, keys, values, mem_keys, mem_values, utter):
    length, width = query.shape
    head_width = width // HEADS
    nsegs = utter.shape[0]
    block = min(512, length)
    frame_utt = jnp.repeat(utter, SEG)
    padded_keys = jnp.pad(keys, ((64, 64), (0, 0)))
    padded_vals = jnp.pad(values, ((64, 64), (0, 0)))
    padded_utt = jnp.pad(frame_utt, (64, 64), constant_values=-1)
    memory_key_rows = mem_keys.reshape(nsegs, HEADS, head_width)
    memory_value_rows = mem_values.reshape(nsegs, HEADS, head_width)
    seg_index = jnp.arange(nsegs, dtype=jnp.int32)
    score_scale = 1.0 / head_width ** 0.5

    def one_block(index):
        start = (index * block).astype(jnp.int32)
        query_tile = lax.dynamic_slice_in_dim(query, start, block, 0).reshape(block, HEADS, head_width)
        k_block = lax.dynamic_slice_in_dim(padded_keys, start, block + 128, 0).reshape(block + 128, HEADS, head_width)
        v_block = lax.dynamic_slice_in_dim(padded_vals, start, block + 128, 0).reshape(block + 128, HEADS, head_width)
        k_utter = lax.dynamic_slice_in_dim(padded_utt, start, block + 128, 0)
        q_utter = lax.dynamic_slice_in_dim(frame_utt, start, block, 0)
        q_place = start + jnp.arange(block, dtype=jnp.int32)
        k_place = start - 64 + jnp.arange(block + 128, dtype=jnp.int32)
        q_seg = q_place // SEG
        lower = q_seg * SEG - LEFT
        upper = q_seg * SEG + SEG + RIGHT
        allowed = (k_utter[None, :] == q_utter[:, None]) & (k_place[None, :] >= lower[:, None]) & (k_place[None, :] < upper[:, None])
        mem_ok = (utter[None, :] == q_utter[:, None]) & (seg_index[None, :] >= q_seg[:, None] - MEMS) & (seg_index[None, :] < q_seg[:, None])
        s_frames = jnp.einsum('qhd,khd->hqk', query_tile, k_block, precision=lax.Precision.HIGHEST) * score_scale
        summary_memory = jnp.einsum('wbt,ubt->bwu', query_tile, memory_key_rows, precision=lax.Precision.HIGHEST) * score_scale
        s_frames = jnp.where(allowed[None], s_frames, -1000000000.0)
        summary_memory = jnp.where(mem_ok[None], summary_memory, -1000000000.0)
        top = jnp.maximum(lax.optimization_barrier(jnp.max(s_frames, axis=-1, keepdims=True)), lax.optimization_barrier(jnp.max(summary_memory, axis=-1, keepdims=True)))
        e_frames = jnp.exp(s_frames - top)
        e_memory = jnp.exp(summary_memory - top)
        total = lax.optimization_barrier(jnp.sum(e_frames, axis=-1, keepdims=True)) + lax.optimization_barrier(jnp.sum(e_memory, axis=-1, keepdims=True))
        p_frames = low(e_frames / total)
        previous_memory = low(e_memory / total)
        layer_result = jnp.einsum('hqk,khd->qhd', p_frames, v_block, precision=lax.Precision.HIGHEST)
        layer_result = layer_result + jnp.einsum('elv,vew->lew', previous_memory, memory_value_rows, precision=lax.Precision.HIGHEST)
        return layer_result.reshape(block, width)
    blocks = lax.map(jax.checkpoint(one_block), jnp.arange(length // block, dtype=jnp.int32))
    return blocks.reshape(length, width)

def forward(inputs, utter, params):
    first_gain, first_shift, project_in, query_bias, value_bias, project_out, out_bias, second_gain, second_shift, up_weight, up_bias, down_weight, down_bias = params
    width = inputs.shape[-1]
    nrows = inputs.shape[0]
    nsegs = inputs.shape[1] // SEG
    normed = low(layer_norm(inputs, first_gain, first_shift))
    mixed = matmul(normed, project_in)
    query = low(low_back(mixed[..., :width] + query_bias))
    keys = low(low_back(mixed[..., width:2 * width]))
    values = low(low_back(mixed[..., 2 * width:] + value_bias))
    summary = low(lax.optimization_barrier(jnp.mean(normed.reshape(nrows, nsegs, SEG, width), axis=2)))
    mem_mixed = matmul(summary, project_in[:, width:])
    mem_keys = low(low_back(mem_mixed[..., :width]))
    mem_values = low(low_back(mem_mixed[..., width:] + value_bias))
    attended = jax.vmap(row_attention)(query, keys, values, mem_keys, mem_values, utter)
    attended = low(low_back(attended))
    resid = inputs + matmul(attended, project_out) + out_bias
    normed2 = low(layer_norm(resid, second_gain, second_shift))
    hidden = low(low_back(jax.nn.gelu(matmul(normed2, up_weight) + up_bias)))
    return resid + matmul(hidden, down_weight) + down_bias

def reference(frames, upstream, utterance, first_gain, first_shift, project_in, query_bias, value_bias, project_out, out_bias, second_gain, second_shift, up_weight, up_bias, down_weight, down_bias):
    params = tuple((p.astype(jnp.float32) for p in (first_gain, first_shift, project_in, query_bias, value_bias, project_out, out_bias, second_gain, second_shift, up_weight, up_bias, down_weight, down_bias)))
    group = ROWS // N_DP
    grads = tuple((jnp.zeros_like(p) for p in params))
    outputs = []
    grad_inputs = []
    for micro in range(MB):
        inputs = frames[micro].astype(jnp.float32).reshape(N_DP, group, ROW_LEN, D)
        cotangent = upstream[micro].astype(jnp.float32).reshape(N_DP, group, ROW_LEN, D)
        utters = utterance[micro].reshape(N_DP, group, SEGS)

        def step(carry, item):
            rows_in, rows_cot, rows_utt = item
            layer_result, pull = jax.vjp(lambda value, weights: forward(value, rows_utt, weights), rows_in, params)
            grad_in, grad_w = pull(rows_cot)
            return (tuple((c + g for c, g in zip(carry, grad_w))), (layer_result, grad_in))
        grads, (results, grad_ins) = lax.scan(step, grads, (inputs, cotangent, utters))
        outputs.append(results.reshape(ROWS, ROW_LEN, D))
        grad_inputs.append(grad_ins.reshape(ROWS, ROW_LEN, D))
    output = jnp.stack(outputs).astype(jnp.bfloat16)
    grad_frames = jnp.stack(grad_inputs)
    return (output, grad_frames, grads[0], grads[1], grads[2], grads[3], grads[4], grads[5], grads[6], grads[7], grads[8], grads[9], grads[10], grads[11], grads[12])
```

```python
import functools

import jax
import jax.numpy as jnp
from jax import lax
from jax.experimental import pallas as pl
from jax.experimental.pallas import tpu as pltpu
from jax.sharding import PartitionSpec as P

HEADS = 8
SEG = 16
RIGHT = 4
LEFT = 30
MEMS = 4
QB = 128
WIN = 176
SLOTS = 16
KEYS = WIN + SLOTS
TILE = 512
EXTRA = 16
BF = jnp.bfloat16
F32 = jnp.float32
HBM = pl.BlockSpec(memory_space=pl.ANY)
VMEM = pl.BlockSpec(memory_space=pltpu.VMEM)
LIMIT = 56 * 2**20


def nn(a, b):
    return lax.dot_general(a, b, (((1,), (0,)), ((), ())), preferred_element_type=F32)


def nt(a, b):
    return lax.dot_general(a, b, (((1,), (1,)), ((), ())), preferred_element_type=F32)


def tn(a, b):
    return lax.dot_general(a, b, (((0,), (0,)), ((), ())), preferred_element_type=F32)


def params(**more):
    return pltpu.CompilerParams(vmem_limit_bytes=LIMIT, **more)


def window(block, length):
    first = min(max(block * QB - 32, 0), length - WIN)
    slot = min(max(block * QB // SEG - MEMS, 0), length // SEG - SLOTS)
    return first, slot


def pieces_of(parts, width):
    plan = []
    for number, (offset, relative, first, rows, count) in enumerate(parts):
        for each in range(count):
            plan.append((number, each * rows, rows, offset + each, relative, first))
    return plan


def start_copies(copies):
    for copy in copies:
        copy.start()


def wait_copies(copies):
    for copy in copies:
        copy.wait()


def stats(value):
    mean = jnp.mean(value, axis=-1, keepdims=True)
    offset = value - mean
    spread = jnp.mean(offset * offset, axis=-1, keepdims=True)
    scale = lax.rsqrt(spread + 1e-05)
    return offset * scale, scale


def averages(length):
    blocks = length // QB
    rows = blocks * SLOTS
    row = lax.broadcasted_iota(jnp.int32, (rows, length), 0)
    seg = lax.broadcasted_iota(jnp.int32, (rows, length), 1) // SEG
    slot = row % SLOTS
    for block in range(blocks):
        first = window(block, length)[1]
        slot = slot + jnp.where(row // SLOTS == block, first, 0)
    return jnp.where(slot == seg, 1.0 / SEG, 0.0).astype(BF)


def head_pair(value):
    lane = lax.broadcasted_iota(jnp.int32, value.shape, 1)
    zero = jnp.zeros_like(value)
    half = value.shape[1] // 2
    return jnp.concatenate(
        [jnp.where(lane < half, value, zero), jnp.where(lane >= half, value, zero)], axis=0
    )


def diagonal(value):
    half = value.shape[0] // 2
    return jnp.concatenate([value[:half, :QB], value[half:, QB:]], axis=0)


def visible_bias(bias_ref, utter_ref, row, nsegs):
    length = nsegs * SEG
    key = lax.broadcasted_iota(jnp.int32, (KEYS, QB), 0)
    query = lax.broadcasted_iota(jnp.int32, (KEYS, QB), 1)
    segs = QB // SEG
    starts = [jnp.int32(0)]
    for seg in range(1, nsegs):
        same = utter_ref[row, seg] == utter_ref[row, seg - 1]
        starts.append(jnp.where(same, starts[-1], seg))
    for block in range(length // QB):
        first, slot = window(block, length)
        lower = jnp.zeros((KEYS, QB), jnp.int32)
        upper = jnp.zeros((KEYS, QB), jnp.int32)
        for part in range(segs):
            seg = block * segs + part
            more = jnp.int32(0)
            if seg + 1 < nsegs:
                more = jnp.where(utter_ref[row, seg + 1] == utter_ref[row, seg], RIGHT, 0)
            frame_low = jnp.maximum(seg * SEG - LEFT, starts[seg] * SEG) - first
            frame_high = seg * SEG + SEG + more - first
            slot_low = jnp.maximum(seg - MEMS, starts[seg]) - slot + WIN
            slot_high = jnp.int32(seg - slot + WIN)
            here = query // SEG == part
            lower = jnp.where(here, jnp.where(key < WIN, frame_low, slot_low), lower)
            upper = jnp.where(here, jnp.where(key < WIN, frame_high, slot_high), upper)
        seen = (key >= lower) & (key < upper)
        bias_ref[block] = jnp.where(seen, 0.0, -1e9)


def front_body(plan, width, nparts, utter, x, *refs):
    parts = refs[:nparts]
    (vecs, q_out, k_out, v_out, p_out, att_out, resid_out, n2_out) = refs[nparts : nparts + 8]
    (w_in, w_out, small, bias, att, sem) = refs[nparts + 8 :]
    row = pl.program_id(0)
    length, model = x.shape[1], x.shape[2]
    pieces = small.shape[0]
    blocks = length // QB
    me = lax.axis_index("fsdp")

    @pl.when(row == 0)
    def _():
        copies = []
        for number, at, rows, offset, relative, first in plan:
            device = jnp.bitwise_xor(me, offset) if relative else offset
            for band in range(5):
                low, high = band * width, (band + 1) * width if band < 4 else 4 * width + EXTRA
                low, high = max(low, first), min(high, first + rows)
                if low >= high:
                    continue
                source = parts[number].at[pl.ds(at + low - first, high - low), :]
                if band == 4:
                    target = small.at[device]
                else:
                    place = pl.multiple_of(device * width, width) + low - band * width
                    if band < 3:
                        target = w_in.at[pl.ds(place, high - low), pl.ds(band * model, model)]
                    else:
                        target = w_out.at[pl.ds(place, high - low), :]
                copies.append(pltpu.make_async_copy(source, target, sem))
        start_copies(copies)
        wait_copies(copies)
        total = jnp.zeros((8, model), F32)
        ups = [jnp.zeros((1, model), F32) for _ in range(4)]
        for piece in range(pieces):
            found = small[piece].astype(F32)
            total = total + pltpu.roll(found, piece * width, 1)[:8]
            for part in range(4):
                place = (piece * 4 + part) * width
                ups[place // model] += pltpu.roll(found, place % model, 1)[8 + part : 9 + part]
        vecs[0:8] = total
        for part in range(4):
            vecs[8 + part : 9 + part] = ups[part]
        vecs[12:16] = jnp.zeros((4, model), F32)

    visible_bias(bias, utter, row, length // SEG)
    value = x[0].astype(F32)
    unit, _ = stats(value)
    normed = (unit * vecs[0:1] + vecs[1:2]).astype(BF)
    summary = nn(averages(length), normed).astype(BF)
    wide = jnp.concatenate([normed, summary], axis=0)
    q_out[0] = ((nn(normed, w_in[:, :model]) + vecs[2:3]).astype(BF).astype(F32) * 0.125).astype(BF)
    k_out[0] = nn(wide, w_in[:, model : 2 * model]).astype(BF)
    v_out[0] = (nn(wide, w_in[:, 2 * model :]) + vecs[3:4]).astype(BF)
    for block in range(blocks):
        first, _ = window(block, length)
        rows = slice(block * QB, (block + 1) * QB)
        own = slice(length + block * SLOTS, length + (block + 1) * SLOTS)
        for pair in range(HEADS // 2):
            lanes = slice(pair * 128, (pair + 1) * 128)
            keys = jnp.concatenate([k_out[0, first : first + WIN, lanes], k_out[0, own, lanes]], axis=0)
            vals = jnp.concatenate([v_out[0, first : first + WIN, lanes], v_out[0, own, lanes]], axis=0)
            seen = bias[block]
            scores = nt(keys, head_pair(q_out[0, rows, lanes]))
            scores = scores + jnp.concatenate([seen, seen], axis=1)
            top = jnp.max(scores, axis=0, keepdims=True)
            raised = jnp.exp(scores - top)
            probs = (raised * (1.0 / jnp.sum(raised, axis=0, keepdims=True))).astype(BF)
            p_out[0, block, pair] = probs
            found = diagonal(tn(vals, probs))
            att_out[0, lanes, rows] = found.astype(BF)
            att[rows, lanes] = found.T.astype(BF)
    resid = value + nn(att[...], w_out[...]) + vecs[4:5]
    resid_out[0] = resid
    unit, _ = stats(resid)
    n2_out[0] = (unit * vecs[5:6] + vecs[6:7]).astype(BF)


def front(x, utter, parts, plan, width, pieces):
    rows, length, model = x.shape
    blocks = length // QB
    wide = length + blocks * SLOTS
    body = functools.partial(front_body, plan, width, len(parts))

    def by_row(*shape):
        zeros = (0,) * len(shape)
        return pl.BlockSpec((1,) + shape, lambda r, *_: (r,) + zeros)

    return pl.pallas_call(
        body,
        grid=(rows,),
        in_specs=[pl.BlockSpec(memory_space=pltpu.SMEM), by_row(length, model)] + [HBM] * len(parts),
        out_specs=[
            pl.BlockSpec((16, model), lambda r: (0, 0)),
            by_row(length, model),
            by_row(wide, model),
            by_row(wide, model),
            by_row(blocks, HEADS // 2, KEYS, 2 * QB),
            by_row(model, length),
            by_row(length, model),
            by_row(length, model),
        ],
        out_shape=[
            jax.ShapeDtypeStruct((16, model), F32),
            jax.ShapeDtypeStruct((rows, length, model), BF),
            jax.ShapeDtypeStruct((rows, wide, model), BF),
            jax.ShapeDtypeStruct((rows, wide, model), BF),
            jax.ShapeDtypeStruct((rows, blocks, HEADS // 2, KEYS, 2 * QB), BF),
            jax.ShapeDtypeStruct((rows, model, length), BF),
            jax.ShapeDtypeStruct((rows, length, model), F32),
            jax.ShapeDtypeStruct((rows, length, model), BF),
        ],
        scratch_shapes=[
            pltpu.VMEM((model, 3 * model), BF),
            pltpu.VMEM((model, model), BF),
            pltpu.VMEM((pieces, EXTRA, model), BF),
            pltpu.VMEM((blocks, KEYS, QB), F32),
            pltpu.VMEM((length, model), BF),
            pltpu.SemaphoreType.DMA,
        ],
        compiler_params=params(),
        name="front",
    )(utter, x, *parts)


def assemble(plan, parts, target, height, sem):
    me = lax.axis_index("fsdp")
    copies = []
    for number, at, rows, offset, relative, first in plan:
        device = jnp.bitwise_xor(me, offset) if relative else offset
        place = pl.multiple_of(device * height, height) + first
        copies.append(
            pltpu.make_async_copy(
                parts[number].at[pl.ds(at, rows), :], target.at[pl.ds(place, rows), :], sem
            )
        )
    return copies


def gelu_both(v):
    c = 0.7978845608028654
    square = v * v
    bent = jnp.tanh(c * v * (1.0 + 0.044715 * square))
    half = 0.5 + 0.5 * bent
    slope = half + 0.5 * v * (1.0 - bent * bent) * (c * (1.0 + 3 * 0.044715 * square))
    return v * half, slope


def middle_body(up_plan, down_plan, n_up, n_down, n2, dy, vecs, *refs):
    up_parts = refs[:n_up]
    down_parts = refs[n_up : n_up + n_down]
    hidden, du, grad, ub = refs[n_up + n_down : n_up + n_down + 4]
    up, down, dyt, sem = refs[n_up + n_down + 4 :]
    model = n2.shape[1]
    tokens = n2.shape[0]
    pieces = up.shape[0] // up_plan[1]
    copies = assemble(up_plan[0], up_parts, up, up_plan[1], sem.at[0])
    later = assemble(down_plan[0], down_parts, down, down_plan[1], sem.at[1])
    start_copies(copies)
    start_copies(later)
    dyt[...] = dy[...].T
    wait_copies(copies)
    wait_copies(later)
    step = 128
    for tile in range(up.shape[1] // TILE):
        cols = slice(tile * TILE, (tile + 1) * TILE)
        sums = jnp.zeros((1, TILE), F32)
        for chunk in range(tokens // step):
            rows = slice(chunk * step, (chunk + 1) * step)
            u = nn(n2[rows], up[:, cols]) + vecs[8 + tile : 9 + tile]
            value, slope = gelu_both(u)
            hidden[rows, cols] = value.astype(BF)
            back = nt(dy[rows], down[cols]).astype(BF).astype(F32) * slope
            du[rows, cols] = back.astype(BF)
            sums = sums + jnp.sum(back, axis=0, keepdims=True)
        ub[tile : tile + 1] = sums
        grad[:, cols] = nn(dyt[...], hidden[:, cols]).astype(BF)


def middle(n2, dy, vecs, up_parts, up_plan, down_parts, down_plan):
    tokens, model = n2.shape
    ff = up_parts[0].shape[1]
    body = functools.partial(middle_body, up_plan, down_plan, len(up_parts), len(down_parts))
    return pl.pallas_call(
        body,
        in_specs=[VMEM] * 3 + [HBM] * (len(up_parts) + len(down_parts)),
        out_specs=[VMEM] * 4,
        out_shape=[
            jax.ShapeDtypeStruct((tokens, ff), BF),
            jax.ShapeDtypeStruct((tokens, ff), BF),
            jax.ShapeDtypeStruct((model, ff), BF),
            jax.ShapeDtypeStruct((ff // TILE, TILE), F32),
        ],
        scratch_shapes=[
            pltpu.VMEM((model, ff), BF),
            pltpu.VMEM((ff, model), BF),
            pltpu.VMEM((model, tokens), BF),
            pltpu.SemaphoreType.DMA((2,)),
        ],
        compiler_params=params(),
        name="middle",
    )(n2, dy, vecs, *up_parts, *down_parts)


def norm_back(grad, unit, scale):
    first = jnp.mean(grad, axis=-1, keepdims=True)
    second = jnp.mean(grad * unit, axis=-1, keepdims=True)
    return scale * (grad - first - unit * second)


def back_body(up_plan, n_up, out_plan, width, n_out, n2, du, resid, dy, att, vecs, *refs):
    up_parts = refs[:n_up]
    out_parts = refs[n_up : n_up + n_out]
    gup, gout, dresid, datt, sums = refs[n_up + n_out : n_up + n_out + 5]
    up, w_out, n2t, sem = refs[n_up + n_out + 5 :]
    me = lax.axis_index("fsdp")
    tokens, model = n2.shape
    copies = assemble(up_plan[0], up_parts, up, up_plan[1], sem)
    for number, at, rows, offset, relative, first in out_plan:
        low, high = max(first, 3 * width), min(first + rows, 4 * width)
        if low < high:
            device = jnp.bitwise_xor(me, offset) if relative else offset
            place = pl.multiple_of(device * width, width) + low - 3 * width
            copies.append(
                pltpu.make_async_copy(
                    out_parts[number].at[pl.ds(at + low - first, high - low), :],
                    w_out.at[pl.ds(place, high - low), :],
                    sem,
                )
            )
    start_copies(copies)
    n2t[...] = n2[...].T
    for tile in range(du.shape[1] // TILE):
        cols = slice(tile * TILE, (tile + 1) * TILE)
        gup[:, cols] = nn(n2t[...], du[:, cols]).astype(BF)
    wait_copies(copies)
    step = 128
    per_row = att.shape[2] // step
    gains = jnp.zeros((1, model), F32)
    shifts = jnp.zeros((1, model), F32)
    biases = jnp.zeros((1, model), F32)
    downs = jnp.zeros((1, model), F32)
    for chunk in range(tokens // step):
        rows = slice(chunk * step, (chunk + 1) * step)
        grad = nt(du[rows], up[...])
        unit, scale = stats(resid[rows])
        gains = gains + jnp.sum(grad * unit, axis=0, keepdims=True)
        shifts = shifts + jnp.sum(grad, axis=0, keepdims=True)
        top = dy[rows].astype(F32)
        downs = downs + jnp.sum(top, axis=0, keepdims=True)
        total = top + norm_back(grad * vecs[5:6], unit, scale)
        biases = biases + jnp.sum(total, axis=0, keepdims=True)
        dresid[rows] = total
        datt[rows] = nt(total.astype(BF), w_out[...]).astype(BF)
    full = jnp.zeros((model, model), F32)
    length = att.shape[2]
    for row in range(att.shape[0]):
        rows = slice(row * length, (row + 1) * length)
        full = full + nn(att[row], dresid[rows].astype(BF))
    gout[...] = full.astype(BF)
    sums[0:1] = gains
    sums[1:2] = shifts
    sums[2:3] = biases
    sums[3:4] = downs


def back(n2, du, resid, dy, att, vecs, up_parts, up_plan, out_parts, out_plan, width):
    tokens, model = n2.shape
    ff = du.shape[1]
    body = functools.partial(back_body, up_plan, len(up_parts), out_plan, width, len(out_parts))
    return pl.pallas_call(
        body,
        in_specs=[VMEM] * 6 + [HBM] * (len(up_parts) + len(out_parts)),
        out_specs=[VMEM] * 5,
        out_shape=[
            jax.ShapeDtypeStruct((model, ff), BF),
            jax.ShapeDtypeStruct((model, model), BF),
            jax.ShapeDtypeStruct((tokens, model), F32),
            jax.ShapeDtypeStruct((tokens, model), BF),
            jax.ShapeDtypeStruct((4, model), F32),
        ],
        scratch_shapes=[
            pltpu.VMEM((model, ff), BF),
            pltpu.VMEM((model, model), BF),
            pltpu.VMEM((model, tokens), BF),
            pltpu.SemaphoreType.DMA,
        ],
        compiler_params=params(),
        name="back",
    )(n2, du, resid, dy, att, vecs, *up_parts, *out_parts)


def rear_body(plan, width, nparts, q, k, v, p, datt, x, dresid, vecs, *refs):
    parts = refs[:nparts]
    gin, dx, sums = refs[nparts : nparts + 3]
    (w_in, wide_all, mixed_all, dk, dv, sem) = refs[nparts + 3 :]
    row = pl.program_id(0)
    count = pl.num_programs(0)
    length, model = x.shape[1], x.shape[2]
    extent = k.shape[1]
    blocks = length // QB
    me = lax.axis_index("fsdp")

    copies = []
    for number, at, rows, offset, relative, first in plan:
        device = jnp.bitwise_xor(me, offset) if relative else offset
        for band in range(3):
            low, high = max(band * width, first), min((band + 1) * width, first + rows)
            if low < high:
                place = pl.multiple_of(device * width, width) + low - band * width
                copies.append(
                    pltpu.make_async_copy(
                        parts[number].at[pl.ds(at + low - first, high - low), :],
                        w_in.at[pl.ds(place, high - low), pl.ds(band * model, model)],
                        sem,
                    )
                )

    @pl.when(row == 0)
    def _():
        start_copies(copies)

    base = pl.multiple_of(row * extent, extent)
    value = x[0].astype(F32)
    unit, scale = stats(value)
    normed = (unit * vecs[0:1] + vecs[1:2]).astype(BF)
    average = averages(length)
    wide_all[pl.ds(base, length), :] = normed
    wide_all[pl.ds(base + length, extent - length), :] = nn(average, normed).astype(BF)
    dk[...] = jnp.zeros_like(dk)
    dv[...] = jnp.zeros_like(dv)
    mixed_all[pl.ds(base + length, extent - length), 0:model] = jnp.zeros((extent - length, model), BF)
    for block in range(blocks):
        first, _ = window(block, length)
        rows = slice(block * QB, (block + 1) * QB)
        own = slice(length + block * SLOTS, length + (block + 1) * SLOTS)
        span = slice(first, first + WIN)
        for pair in range(HEADS // 2):
            lanes = slice(pair * 128, (pair + 1) * 128)
            keys = jnp.concatenate([k[0, span, lanes], k[0, own, lanes]], axis=0)
            vals = jnp.concatenate([v[0, span, lanes], v[0, own, lanes]], axis=0)
            queries = head_pair(q[0, rows, lanes])
            tops = head_pair(datt[0, rows, lanes])
            probs = p[0, block, pair]
            wides = probs.astype(F32)
            back = nt(vals, tops)
            inner = jnp.sum(wides * back, axis=0, keepdims=True)
            dscores = (wides * (back - inner)).astype(BF)
            gv = nn(probs, tops)
            gk = nn(dscores, queries)
            dv[span, lanes] += gv[:WIN]
            dv[own, lanes] = gv[WIN:]
            dk[span, lanes] += gk[:WIN]
            dk[own, lanes] = gk[WIN:]
            gq = diagonal(tn(keys, dscores)).T * 0.125
            mixed_all[pl.ds(base + block * QB, QB), lanes] = gq.astype(BF)
    mixed_all[pl.ds(base, extent), model : 2 * model] = dk[...].astype(BF)
    mixed_all[pl.ds(base, extent), 2 * model :] = dv[...].astype(BF)

    @pl.when(row == 0)
    def _():
        wait_copies(copies)

    grad = nt(mixed_all[pl.ds(base, extent), :], w_in[...])
    grad = grad[:length] + tn(average, grad[length:].astype(BF))
    add = jnp.concatenate(
        [
            jnp.sum(grad * unit, axis=0, keepdims=True),
            jnp.sum(grad, axis=0, keepdims=True),
            jnp.sum(mixed_all[pl.ds(base, length), 0:model].astype(F32), axis=0, keepdims=True),
            jnp.sum(mixed_all[pl.ds(base, extent), 2 * model :].astype(F32), axis=0, keepdims=True),
        ],
        axis=0,
    )

    @pl.when(row == 0)
    def _():
        sums[...] = add

    @pl.when(row > 0)
    def _():
        sums[...] += add

    dx[0] = dresid[0] + norm_back(grad * vecs[0:1], unit, scale)

    @pl.when(row == count - 1)
    def _():
        for tile in range(3):
            cols = slice(tile * model, (tile + 1) * model)
            gin[:, cols] = tn(wide_all[...], mixed_all[:, cols]).astype(BF)


def rear(q, k, v, p, datt, x, dresid, vecs, parts, plan, width):
    rows, length, model = x.shape
    extent = k.shape[1]
    blocks = length // QB
    body = functools.partial(rear_body, plan, width, len(parts))

    def by_row(*shape):
        zeros = (0,) * len(shape)
        return pl.BlockSpec((1,) + shape, lambda r: (r,) + zeros)

    def whole(*shape):
        return pl.BlockSpec(shape, lambda r: (0,) * len(shape))

    return pl.pallas_call(
        body,
        grid=(rows,),
        in_specs=[
            by_row(length, model),
            by_row(extent, model),
            by_row(extent, model),
            by_row(blocks, HEADS // 2, KEYS, 2 * QB),
            by_row(length, model),
            by_row(length, model),
            by_row(length, model),
            whole(16, model),
        ]
        + [HBM] * len(parts),
        out_specs=[whole(model, 3 * model), by_row(length, model), whole(4, model)],
        out_shape=[
            jax.ShapeDtypeStruct((model, 3 * model), BF),
            jax.ShapeDtypeStruct((rows, length, model), F32),
            jax.ShapeDtypeStruct((4, model), F32),
        ],
        scratch_shapes=[
            pltpu.VMEM((model, 3 * model), BF),
            pltpu.VMEM((rows * extent, model), BF),
            pltpu.VMEM((rows * extent, 3 * model), BF),
            pltpu.VMEM((extent, model), F32),
            pltpu.VMEM((extent, model), F32),
            pltpu.SemaphoreType.DMA,
        ],
        compiler_params=params(),
        name="rear",
    )(q, k, v, p, datt, x, dresid, vecs, *parts)


def finish_body(plan, nparts, hidden, resid, vecs, *refs):
    parts = refs[:nparts]
    out, down, sem = refs[nparts:]
    copies = assemble(plan[0], parts, down, plan[1], sem)
    start_copies(copies)
    wait_copies(copies)
    step = 128
    for chunk in range(hidden.shape[0] // step):
        rows = slice(chunk * step, (chunk + 1) * step)
        out[rows] = (resid[rows] + nn(hidden[rows], down[...]) + vecs[7:8]).astype(BF)


def finish(hidden, resid, vecs, parts, plan):
    tokens, ff = hidden.shape
    model = resid.shape[1]
    return pl.pallas_call(
        functools.partial(finish_body, plan, len(parts)),
        in_specs=[VMEM] * 3 + [HBM] * len(parts),
        out_specs=VMEM,
        out_shape=jax.ShapeDtypeStruct((tokens, model), BF),
        scratch_shapes=[pltpu.VMEM((ff, model), BF), pltpu.SemaphoreType.DMA],
        compiler_params=params(),
        name="finish",
    )(hidden, resid, vecs, *parts)


def gather(piece, size):
    rows = piece.shape[0]
    whole = lax.all_gather(piece, "fsdp", axis=0, tiled=True)
    return [whole], pieces_of([(0, False, 0, rows, size)], rows)


def pack(project_in, project_out, vectors, up_bias):
    width, model = project_out.shape
    rows = jnp.concatenate(
        [jnp.stack(vectors), up_bias.reshape(4, width), jnp.zeros((4, width), BF)], axis=0
    )
    rows = jnp.pad(rows, ((0, 0), (0, model - width)))
    parts = [project_in[:, at * model : (at + 1) * model] for at in range(3)]
    return jnp.concatenate(parts + [project_out, rows], axis=0)


def scatter(value):
    own = lax.psum_scatter(value, "fsdp", scatter_dimension=0, tiled=True)
    return lax.psum(own, "dp").astype(F32)


def shards(
    frames,
    upstream,
    utterance,
    first_gain,
    first_shift,
    project_in,
    query_bias,
    value_bias,
    project_out,
    out_bias,
    second_gain,
    second_shift,
    up_weight,
    up_bias,
    down_weight,
    down_bias,
):
    micro, nrows, length, model = frames.shape
    rows = micro * nrows
    size = model // project_out.shape[0]
    width = model // size
    ff = up_weight.shape[1]
    x = frames.reshape(rows, length, model)
    dy = upstream.reshape(rows * length, model)
    utter = utterance.reshape(rows, length // SEG)
    vectors = (first_gain, first_shift, query_bias, value_bias, out_bias, second_gain, second_shift, down_bias)
    packed = pack(project_in, project_out, vectors, up_bias)
    a_parts, a_plan = gather(packed, size)
    u_parts, u_plan = gather(up_weight, size)
    d_parts, d_plan = gather(down_weight, size)
    vecs, q, k, v, p, att, resid, n2 = front(x, utter, a_parts, a_plan, width, size)
    n2 = n2.reshape(rows * length, model)
    flat = resid.reshape(rows * length, model)
    hidden, du, gdown, gub = middle(n2, dy, vecs, u_parts, (u_plan, width), d_parts, (d_plan, ff // size))
    gup, gout, dresid, datt, sums2 = back(
        n2, du, flat, dy, att, vecs, u_parts, (u_plan, width), a_parts, a_plan, width
    )
    shape = (rows, length, model)
    gin, dx, sums1 = rear(
        q, k, v, p, datt.reshape(shape), x, dresid.reshape(shape), vecs, a_parts, a_plan, width
    )
    out = finish(hidden, flat, vecs, d_parts, (d_plan, ff // size))
    small = jnp.concatenate([sums1, sums2, gub], axis=0)
    small = lax.psum(small, ("dp", "fsdp"))
    me = lax.axis_index("fsdp")

    def own(row):
        return lax.dynamic_slice_in_dim(small[row], me * width, width, 0)

    gub = lax.dynamic_slice_in_dim(small[8:].reshape(-1), me * (ff // size), ff // size, 0)
    return (
        out.reshape(frames.shape),
        dx.reshape(frames.shape),
        own(0),
        own(1),
        scatter(gin),
        own(2),
        own(3),
        scatter(gout),
        own(6),
        own(4),
        own(5),
        scatter(gup),
        gub,
        scatter(gdown.T),
        own(7),
    )


def solution(mesh):
    rows = P(None, ("dp", "fsdp"), None, None)
    vector = P("fsdp")
    matrix = P("fsdp", None)
    weights = (vector, vector, matrix, vector, vector, matrix, vector, vector, vector, matrix, vector, matrix, vector)
    return jax.shard_map(
        shards,
        mesh=mesh,
        in_specs=(rows, rows, P(None, ("dp", "fsdp"), None)) + weights,
        out_specs=(rows, rows) + weights,
        check_vma=False,
    )
```

```python
import functools

import jax
import jax.numpy as jnp
from jax import lax
from jax.experimental import pallas as pl
from jax.experimental.pallas import tpu as pltpu
from jax.sharding import PartitionSpec as P

HEADS = 8
SEG = 16
RIGHT = 4
LEFT = 30
MEMS = 4
QB = 128
WIN = 176
SLOTS = 16
KEYS = WIN + SLOTS
SLOTS_OF = {(1, 0): 0, (3, 0): 1, (2, 1): 2, (3, 1): 3, (1, 1): 4, (2, 0): 5, (0, 0): 6, (0, 1): 7}
TILE = 512
EXTRA = 16
BF = jnp.bfloat16
F32 = jnp.float32
HBM = pl.BlockSpec(memory_space=pl.ANY)
VMEM = pl.BlockSpec(memory_space=pltpu.VMEM)
LIMIT = 32 * 2**20


def nn(a, b):
    return lax.dot_general(a, b, (((1,), (0,)), ((), ())), preferred_element_type=F32)


def nt(a, b):
    return lax.dot_general(a, b, (((1,), (1,)), ((), ())), preferred_element_type=F32)


def tn(a, b):
    return lax.dot_general(a, b, (((0,), (0,)), ((), ())), preferred_element_type=F32)


def params(**more):
    return pltpu.CompilerParams(vmem_limit_bytes=LIMIT, **more)


def cost(micros):
    return pl.CostEstimate(flops=int(micros * 1.15e9), bytes_accessed=0, transcendentals=0)


def window(block, length):
    first = min(max(block * QB - 32, 0), length - WIN)
    slot = min(max(block * QB // SEG - MEMS, 0), length // SEG - SLOTS)
    return first, slot


def pieces_of(parts, width):
    plan = []
    for number, (offset, relative, first, rows, count) in enumerate(parts):
        for each in range(count):
            plan.append((number, each * rows, rows, offset + each, relative, first))
    return plan


def start_copies(copies):
    for copy in copies:
        copy.start()


def wait_copies(copies):
    for copy in copies:
        copy.wait()


def stats(value):
    mean = jnp.mean(value, axis=-1, keepdims=True)
    offset = value - mean
    spread = jnp.mean(offset * offset, axis=-1, keepdims=True)
    scale = lax.rsqrt(spread + 1e-05)
    return offset * scale, scale


def averages(length):
    blocks = length // QB
    rows = blocks * SLOTS
    row = lax.broadcasted_iota(jnp.int32, (rows, length), 0)
    seg = lax.broadcasted_iota(jnp.int32, (rows, length), 1) // SEG
    slot = row % SLOTS
    for block in range(blocks):
        first = window(block, length)[1]
        slot = slot + jnp.where(row // SLOTS == block, first, 0)
    return jnp.where(slot == seg, 1.0 / SEG, 0.0).astype(BF)


def head_pair(value):
    lane = lax.broadcasted_iota(jnp.int32, value.shape, 1)
    zero = jnp.zeros_like(value)
    half = value.shape[1] // 2
    return jnp.concatenate(
        [jnp.where(lane < half, value, zero), jnp.where(lane >= half, value, zero)], axis=0
    )


def diagonal(value):
    half = value.shape[0] // 2
    return jnp.concatenate([value[:half, :QB], value[half:, QB:]], axis=0)


def visible_bias(bias_ref, utter_ref, row, nsegs):
    length = nsegs * SEG
    key = lax.broadcasted_iota(jnp.int32, (KEYS, QB), 0)
    query = lax.broadcasted_iota(jnp.int32, (KEYS, QB), 1)
    segs = QB // SEG
    starts = [jnp.int32(0)]
    for seg in range(1, nsegs):
        same = utter_ref[row, seg] == utter_ref[row, seg - 1]
        starts.append(jnp.where(same, starts[-1], seg))
    for block in range(length // QB):
        first, slot = window(block, length)
        lower = jnp.zeros((KEYS, QB), jnp.int32)
        upper = jnp.zeros((KEYS, QB), jnp.int32)
        for part in range(segs):
            seg = block * segs + part
            more = jnp.int32(0)
            if seg + 1 < nsegs:
                more = jnp.where(utter_ref[row, seg + 1] == utter_ref[row, seg], RIGHT, 0)
            frame_low = jnp.maximum(seg * SEG - LEFT, starts[seg] * SEG) - first
            frame_high = seg * SEG + SEG + more - first
            slot_low = jnp.maximum(seg - MEMS, starts[seg]) - slot + WIN
            slot_high = jnp.int32(seg - slot + WIN)
            here = query // SEG == part
            lower = jnp.where(here, jnp.where(key < WIN, frame_low, slot_low), lower)
            upper = jnp.where(here, jnp.where(key < WIN, frame_high, slot_high), upper)
        seen = (key >= lower) & (key < upper)
        bias_ref[block] = jnp.where(seen, 0.0, -1e9)


def front_body(plan, width, nparts, utter, x, *refs):
    parts = refs[:nparts]
    (vecs, q_out, k_out, v_out, p_out, att_out, resid_out, n2_out) = refs[nparts : nparts + 8]
    (w_in, w_out, small, bias, att, sem) = refs[nparts + 8 :]
    row = pl.program_id(0)
    length, model = x.shape[1], x.shape[2]
    pieces = small.shape[0]
    blocks = length // QB
    me = lax.axis_index("fsdp")

    @pl.when(row == 0)
    def _():
        copies = []
        for number, at, rows, offset, relative, first in plan:
            device = jnp.bitwise_xor(me, offset) if relative else offset
            for band in range(5):
                low, high = band * width, (band + 1) * width if band < 4 else 4 * width + EXTRA
                low, high = max(low, first), min(high, first + rows)
                if low >= high:
                    continue
                source = parts[number].at[pl.ds(at + low - first, high - low), :]
                if band == 4:
                    target = small.at[device]
                else:
                    place = pl.multiple_of(device * width, width) + low - band * width
                    if band < 3:
                        target = w_in.at[pl.ds(place, high - low), pl.ds(band * model, model)]
                    else:
                        target = w_out.at[pl.ds(place, high - low), :]
                copies.append(pltpu.make_async_copy(source, target, sem))
        start_copies(copies)
        wait_copies(copies)
        total = jnp.zeros((8, model), F32)
        ups = [jnp.zeros((1, model), F32) for _ in range(4)]
        for piece in range(pieces):
            found = small[piece].astype(F32)
            total = total + pltpu.roll(found, piece * width, 1)[:8]
            for part in range(4):
                place = (piece * 4 + part) * width
                ups[place // model] += pltpu.roll(found, place % model, 1)[8 + part : 9 + part]
        vecs[0:8] = total
        for part in range(4):
            vecs[8 + part : 9 + part] = ups[part]
        vecs[12:16] = jnp.zeros((4, model), F32)

    visible_bias(bias, utter, row, length // SEG)
    value = x[0].astype(F32)
    unit, _ = stats(value)
    normed = (unit * vecs[0:1] + vecs[1:2]).astype(BF)
    summary = nn(averages(length), normed).astype(BF)
    wide = jnp.concatenate([normed, summary], axis=0)
    q_out[0] = ((nn(normed, w_in[:, :model]) + vecs[2:3]).astype(BF).astype(F32) * 0.125).astype(BF)
    k_out[0] = nn(wide, w_in[:, model : 2 * model]).astype(BF)
    v_out[0] = (nn(wide, w_in[:, 2 * model :]) + vecs[3:4]).astype(BF)
    for block in range(blocks):
        first, _ = window(block, length)
        rows = slice(block * QB, (block + 1) * QB)
        own = slice(length + block * SLOTS, length + (block + 1) * SLOTS)
        for pair in range(HEADS // 2):
            lanes = slice(pair * 128, (pair + 1) * 128)
            keys = jnp.concatenate([k_out[0, first : first + WIN, lanes], k_out[0, own, lanes]], axis=0)
            vals = jnp.concatenate([v_out[0, first : first + WIN, lanes], v_out[0, own, lanes]], axis=0)
            seen = bias[block]
            scores = nt(keys, head_pair(q_out[0, rows, lanes]))
            scores = scores + jnp.concatenate([seen, seen], axis=1)
            top = jnp.max(scores, axis=0, keepdims=True)
            raised = jnp.exp(scores - top)
            probs = (raised * (1.0 / jnp.sum(raised, axis=0, keepdims=True))).astype(BF)
            p_out[0, block, pair] = probs
            found = diagonal(tn(vals, probs))
            att_out[0, lanes, rows] = found.astype(BF)
            att[rows, lanes] = found.T.astype(BF)
    resid = value + nn(att[...], w_out[...]) + vecs[4:5]
    resid_out[0] = resid
    unit, _ = stats(resid)
    n2_out[0] = (unit * vecs[5:6] + vecs[6:7]).astype(BF)


def front(x, utter, parts, plan, width, pieces):
    rows, length, model = x.shape
    blocks = length // QB
    wide = length + blocks * SLOTS
    body = functools.partial(front_body, plan, width, len(parts))

    def by_row(*shape):
        zeros = (0,) * len(shape)
        return pl.BlockSpec((1,) + shape, lambda r, *_: (r,) + zeros)

    return pl.pallas_call(
        body,
        grid=(rows,),
        in_specs=[pl.BlockSpec(memory_space=pltpu.SMEM), by_row(length, model)] + [HBM] * len(parts),
        out_specs=[
            pl.BlockSpec((16, model), lambda r: (0, 0)),
            by_row(length, model),
            by_row(wide, model),
            by_row(wide, model),
            by_row(blocks, HEADS // 2, KEYS, 2 * QB),
            by_row(model, length),
            by_row(length, model),
            by_row(length, model),
        ],
        out_shape=[
            jax.ShapeDtypeStruct((16, model), F32),
            jax.ShapeDtypeStruct((rows, length, model), BF),
            jax.ShapeDtypeStruct((rows, wide, model), BF),
            jax.ShapeDtypeStruct((rows, wide, model), BF),
            jax.ShapeDtypeStruct((rows, blocks, HEADS // 2, KEYS, 2 * QB), BF),
            jax.ShapeDtypeStruct((rows, model, length), BF),
            jax.ShapeDtypeStruct((rows, length, model), F32),
            jax.ShapeDtypeStruct((rows, length, model), BF),
        ],
        scratch_shapes=[
            pltpu.VMEM((model, 3 * model), BF),
            pltpu.VMEM((model, model), BF),
            pltpu.VMEM((pieces, EXTRA, model), BF),
            pltpu.VMEM((blocks, KEYS, QB), F32),
            pltpu.VMEM((length, model), BF),
            pltpu.SemaphoreType.DMA,
        ],
        compiler_params=params(),
        name="front",
        cost_estimate=cost(14),
    )(utter, x, *parts)


def assemble(plan, parts, target, height, sem):
    me = lax.axis_index("fsdp")
    copies = []
    for number, at, rows, offset, relative, first in plan:
        device = jnp.bitwise_xor(me, offset) if relative else offset
        place = pl.multiple_of(device * height, height) + first
        copies.append(
            pltpu.make_async_copy(
                parts[number].at[pl.ds(at, rows), :], target.at[pl.ds(place, rows), :], sem
            )
        )
    return copies


def emit(full, grads, part, within, sem):
    if len(grads) == 1:
        return [pltpu.make_async_copy(full, within(grads[0]), sem)]
    me = lax.axis_index("fsdp")
    copies = []
    for core in range(2):
        for (chip, top), slot in SLOTS_OF.items():
            device = jnp.bitwise_xor(me, 2 * chip + core)
            copies.append(
                pltpu.make_async_copy(part(device, top), within(grads[core].at[slot]), sem)
            )
    return copies


def gelu_both(v):
    c = 0.7978845608028654
    square = v * v
    bent = jnp.tanh(c * v * (1.0 + 0.044715 * square))
    half = 0.5 + 0.5 * bent
    slope = half + 0.5 * v * (1.0 - bent * bent) * (c * (1.0 + 3 * 0.044715 * square))
    return v * half, slope


def middle_body(up_plan, down_plan, n_up, n_down, n_grad, n2, dy, vecs, *refs):
    up_parts = refs[:n_up]
    down_parts = refs[n_up : n_up + n_down]
    hidden, du, ub, *grads = refs[n_up + n_down : n_up + n_down + 3 + n_grad]
    up, down, dyt, grad, sem = refs[n_up + n_down + 3 + n_grad :]
    model = n2.shape[1]
    tokens = n2.shape[0]
    pieces = up.shape[0] // up_plan[1]
    copies = assemble(up_plan[0], up_parts, up, up_plan[1], sem.at[0])
    later = assemble(down_plan[0], down_parts, down, down_plan[1], sem.at[1])
    start_copies(copies)
    start_copies(later)
    dyt[...] = dy[...].T
    wait_copies(copies)
    wait_copies(later)
    step = 128
    for tile in range(up.shape[1] // TILE):
        cols = slice(tile * TILE, (tile + 1) * TILE)
        sums = jnp.zeros((1, TILE), F32)
        for chunk in range(tokens // step):
            rows = slice(chunk * step, (chunk + 1) * step)
            u = nn(n2[rows], up[:, cols]) + vecs[8 + tile : 9 + tile]
            value, slope = gelu_both(u)
            hidden[rows, cols] = value.astype(BF)
            back = nt(dy[rows], down[cols]).astype(BF).astype(F32) * slope
            du[rows, cols] = back.astype(BF)
            sums = sums + jnp.sum(back, axis=0, keepdims=True)
        ub[tile : tile + 1] = sums
        grad[:, cols] = nn(dyt[...], hidden[:, cols]).astype(BF)
    half = model // 2
    copies = emit(
        grad,
        grads,
        lambda device, top: grad.at[pl.ds(top * half, half), pl.ds(pl.multiple_of(device * down_plan[1], down_plan[1]), down_plan[1])],
        lambda ref: ref,
        sem.at[0],
    )
    start_copies(copies)
    wait_copies(copies)


def middle(n2, dy, vecs, up_parts, up_plan, down_parts, down_plan, fast):
    tokens, model = n2.shape
    ff = up_parts[0].shape[1]
    shapes = [(8, model // 2, down_plan[1])] * 2 if fast else [(model, ff)]
    body = functools.partial(
        middle_body, up_plan, down_plan, len(up_parts), len(down_parts), len(shapes)
    )
    return pl.pallas_call(
        body,
        in_specs=[VMEM] * 3 + [HBM] * (len(up_parts) + len(down_parts)),
        out_specs=[VMEM] * 3 + [HBM] * len(shapes),
        out_shape=[
            jax.ShapeDtypeStruct((tokens, ff), BF),
            jax.ShapeDtypeStruct((tokens, ff), BF),
            jax.ShapeDtypeStruct((ff // TILE, TILE), F32),
        ]
        + [jax.ShapeDtypeStruct(shape, BF) for shape in shapes],
        scratch_shapes=[
            pltpu.VMEM((model, ff), BF),
            pltpu.VMEM((ff, model), BF),
            pltpu.VMEM((model, tokens), BF),
            pltpu.VMEM((model, ff), BF),
            pltpu.SemaphoreType.DMA((2,)),
        ],
        compiler_params=params(),
        name="middle",
        cost_estimate=cost(16),
    )(n2, dy, vecs, *up_parts, *down_parts)


def norm_back(grad, unit, scale):
    first = jnp.mean(grad, axis=-1, keepdims=True)
    second = jnp.mean(grad * unit, axis=-1, keepdims=True)
    return scale * (grad - first - unit * second)


def back_body(up_plan, n_up, out_plan, width, n_out, n_grad, n2, du, resid, dy, att, vecs, *refs):
    up_parts = refs[:n_up]
    out_parts = refs[n_up : n_up + n_out]
    dresid, datt, sums, *grads = refs[n_up + n_out : n_up + n_out + 3 + n_grad]
    up, w_out, n2t, gup, gout, sem = refs[n_up + n_out + 3 + n_grad :]
    me = lax.axis_index("fsdp")
    tokens, model = n2.shape
    copies = assemble(up_plan[0], up_parts, up, up_plan[1], sem)
    for number, at, rows, offset, relative, first in out_plan:
        low, high = max(first, 3 * width), min(first + rows, 4 * width)
        if low < high:
            device = jnp.bitwise_xor(me, offset) if relative else offset
            place = pl.multiple_of(device * width, width) + low - 3 * width
            copies.append(
                pltpu.make_async_copy(
                    out_parts[number].at[pl.ds(at + low - first, high - low), :],
                    w_out.at[pl.ds(place, high - low), :],
                    sem,
                )
            )
    start_copies(copies)
    n2t[...] = n2[...].T
    for tile in range(du.shape[1] // TILE):
        cols = slice(tile * TILE, (tile + 1) * TILE)
        gup[:, cols] = nn(n2t[...], du[:, cols]).astype(BF)
    wait_copies(copies)
    step = 128
    per_row = att.shape[2] // step
    gains = jnp.zeros((1, model), F32)
    shifts = jnp.zeros((1, model), F32)
    biases = jnp.zeros((1, model), F32)
    downs = jnp.zeros((1, model), F32)
    for chunk in range(tokens // step):
        rows = slice(chunk * step, (chunk + 1) * step)
        grad = nt(du[rows], up[...])
        unit, scale = stats(resid[rows])
        gains = gains + jnp.sum(grad * unit, axis=0, keepdims=True)
        shifts = shifts + jnp.sum(grad, axis=0, keepdims=True)
        top = dy[rows].astype(F32)
        downs = downs + jnp.sum(top, axis=0, keepdims=True)
        total = top + norm_back(grad * vecs[5:6], unit, scale)
        biases = biases + jnp.sum(total, axis=0, keepdims=True)
        dresid[rows] = total
        datt[rows] = nt(total.astype(BF), w_out[...]).astype(BF)
    full = jnp.zeros((model, model), F32)
    length = att.shape[2]
    for row in range(att.shape[0]):
        rows = slice(row * length, (row + 1) * length)
        full = full + nn(att[row], dresid[rows].astype(BF))
    gout[...] = full.astype(BF)
    half = width // 2
    ff = gup.shape[1]

    def part_of(full):
        return lambda device, top: full.at[pl.ds(pl.multiple_of(device * width, width) + top * half, half), :]

    copies = emit(gup, grads, part_of(gup), lambda ref: ref.at[:, 0:ff], sem)
    copies += emit(gout, grads, part_of(gout), lambda ref: ref.at[:, ff : ff + model], sem)
    start_copies(copies)
    wait_copies(copies)
    sums[0:1] = gains
    sums[1:2] = shifts
    sums[2:3] = biases
    sums[3:4] = downs


def back(n2, du, resid, dy, att, vecs, up_parts, up_plan, out_parts, out_plan, width, fast):
    tokens, model = n2.shape
    ff = du.shape[1]
    shapes = [(8, width // 2, ff + model)] * 2 if fast else [(model, ff + model)]
    body = functools.partial(
        back_body, up_plan, len(up_parts), out_plan, width, len(out_parts), len(shapes)
    )
    return pl.pallas_call(
        body,
        in_specs=[VMEM] * 6 + [HBM] * (len(up_parts) + len(out_parts)),
        out_specs=[VMEM] * 3 + [HBM] * len(shapes),
        out_shape=[
            jax.ShapeDtypeStruct((tokens, model), F32),
            jax.ShapeDtypeStruct((tokens, model), BF),
            jax.ShapeDtypeStruct((4, model), F32),
        ]
        + [jax.ShapeDtypeStruct(shape, BF) for shape in shapes],
        scratch_shapes=[
            pltpu.VMEM((model, ff), BF),
            pltpu.VMEM((model, model), BF),
            pltpu.VMEM((model, tokens), BF),
            pltpu.VMEM((model, ff), BF),
            pltpu.VMEM((model, model), BF),
            pltpu.SemaphoreType.DMA,
        ],
        compiler_params=params(),
        name="back",
        cost_estimate=cost(13),
    )(n2, du, resid, dy, att, vecs, *up_parts, *out_parts)


def rear_body(plan, width, nparts, n_grad, q, k, v, p, datt, x, dresid, vecs, *refs):
    parts = refs[:nparts]
    dx, sums, *grads = refs[nparts : nparts + 2 + n_grad]
    (w_in, wide_all, mixed_all, dk, dv, gin, sem) = refs[nparts + 2 + n_grad :]
    row = pl.program_id(0)
    count = pl.num_programs(0)
    length, model = x.shape[1], x.shape[2]
    extent = k.shape[1]
    blocks = length // QB
    me = lax.axis_index("fsdp")

    copies = []
    for number, at, rows, offset, relative, first in plan:
        device = jnp.bitwise_xor(me, offset) if relative else offset
        for band in range(3):
            low, high = max(band * width, first), min((band + 1) * width, first + rows)
            if low < high:
                place = pl.multiple_of(device * width, width) + low - band * width
                copies.append(
                    pltpu.make_async_copy(
                        parts[number].at[pl.ds(at + low - first, high - low), :],
                        w_in.at[pl.ds(place, high - low), pl.ds(band * model, model)],
                        sem,
                    )
                )

    @pl.when(row == 0)
    def _():
        start_copies(copies)

    base = pl.multiple_of(row * extent, extent)
    value = x[0].astype(F32)
    unit, scale = stats(value)
    normed = (unit * vecs[0:1] + vecs[1:2]).astype(BF)
    average = averages(length)
    wide_all[pl.ds(base, length), :] = normed
    wide_all[pl.ds(base + length, extent - length), :] = nn(average, normed).astype(BF)
    dk[...] = jnp.zeros_like(dk)
    dv[...] = jnp.zeros_like(dv)
    mixed_all[pl.ds(base + length, extent - length), 0:model] = jnp.zeros((extent - length, model), BF)
    for block in range(blocks):
        first, _ = window(block, length)
        rows = slice(block * QB, (block + 1) * QB)
        own = slice(length + block * SLOTS, length + (block + 1) * SLOTS)
        span = slice(first, first + WIN)
        for pair in range(HEADS // 2):
            lanes = slice(pair * 128, (pair + 1) * 128)
            keys = jnp.concatenate([k[0, span, lanes], k[0, own, lanes]], axis=0)
            vals = jnp.concatenate([v[0, span, lanes], v[0, own, lanes]], axis=0)
            queries = head_pair(q[0, rows, lanes])
            tops = head_pair(datt[0, rows, lanes])
            probs = p[0, block, pair]
            wides = probs.astype(F32)
            back = nt(vals, tops)
            inner = jnp.sum(wides * back, axis=0, keepdims=True)
            dscores = (wides * (back - inner)).astype(BF)
            gv = nn(probs, tops)
            gk = nn(dscores, queries)
            dv[span, lanes] += gv[:WIN]
            dv[own, lanes] = gv[WIN:]
            dk[span, lanes] += gk[:WIN]
            dk[own, lanes] = gk[WIN:]
            gq = diagonal(tn(keys, dscores)).T * 0.125
            mixed_all[pl.ds(base + block * QB, QB), lanes] = gq.astype(BF)
    mixed_all[pl.ds(base, extent), model : 2 * model] = dk[...].astype(BF)
    mixed_all[pl.ds(base, extent), 2 * model :] = dv[...].astype(BF)

    @pl.when(row == 0)
    def _():
        wait_copies(copies)

    grad = nt(mixed_all[pl.ds(base, extent), :], w_in[...])
    grad = grad[:length] + tn(average, grad[length:].astype(BF))
    add = jnp.concatenate(
        [
            jnp.sum(grad * unit, axis=0, keepdims=True),
            jnp.sum(grad, axis=0, keepdims=True),
            jnp.sum(mixed_all[pl.ds(base, length), 0:model].astype(F32), axis=0, keepdims=True),
            jnp.sum(mixed_all[pl.ds(base, extent), 2 * model :].astype(F32), axis=0, keepdims=True),
        ],
        axis=0,
    )

    @pl.when(row == 0)
    def _():
        sums[...] = add

    @pl.when(row > 0)
    def _():
        sums[...] += add

    dx[0] = dresid[0] + norm_back(grad * vecs[0:1], unit, scale)

    @pl.when(row == count - 1)
    def _():
        for tile in range(3):
            cols = slice(tile * model, (tile + 1) * model)
            gin[:, cols] = tn(wide_all[...], mixed_all[:, cols]).astype(BF)
        half = width // 2
        sends = emit(
            gin,
            grads,
            lambda device, top: gin.at[pl.ds(pl.multiple_of(device * width, width) + top * half, half), :],
            lambda ref: ref,
            sem,
        )
        start_copies(sends)
        wait_copies(sends)


def rear(q, k, v, p, datt, x, dresid, vecs, parts, plan, width, fast):
    rows, length, model = x.shape
    extent = k.shape[1]
    blocks = length // QB
    shapes = [(8, width // 2, 3 * model)] * 2 if fast else [(model, 3 * model)]
    body = functools.partial(rear_body, plan, width, len(parts), len(shapes))

    def by_row(*shape):
        zeros = (0,) * len(shape)
        return pl.BlockSpec((1,) + shape, lambda r: (r,) + zeros)

    def whole(*shape):
        return pl.BlockSpec(shape, lambda r: (0,) * len(shape))

    return pl.pallas_call(
        body,
        grid=(rows,),
        in_specs=[
            by_row(length, model),
            by_row(extent, model),
            by_row(extent, model),
            by_row(blocks, HEADS // 2, KEYS, 2 * QB),
            by_row(length, model),
            by_row(length, model),
            by_row(length, model),
            whole(16, model),
        ]
        + [HBM] * len(parts),
        out_specs=[by_row(length, model), whole(4, model)] + [HBM] * len(shapes),
        out_shape=[
            jax.ShapeDtypeStruct((rows, length, model), F32),
            jax.ShapeDtypeStruct((4, model), F32),
        ]
        + [jax.ShapeDtypeStruct(shape, BF) for shape in shapes],
        scratch_shapes=[
            pltpu.VMEM((model, 3 * model), BF),
            pltpu.VMEM((rows * extent, model), BF),
            pltpu.VMEM((rows * extent, 3 * model), BF),
            pltpu.VMEM((extent, model), F32),
            pltpu.VMEM((extent, model), F32),
            pltpu.VMEM((model, 3 * model), BF),
            pltpu.SemaphoreType.DMA,
        ],
        compiler_params=params(),
        name="rear",
        cost_estimate=cost(17),
    )(q, k, v, p, datt, x, dresid, vecs, *parts)


def finish_body(plan, nparts, hidden, resid, vecs, *refs):
    parts = refs[:nparts]
    out, down, sem = refs[nparts:]
    copies = assemble(plan[0], parts, down, plan[1], sem)
    start_copies(copies)
    wait_copies(copies)
    step = 128
    for chunk in range(hidden.shape[0] // step):
        rows = slice(chunk * step, (chunk + 1) * step)
        out[rows] = (resid[rows] + nn(hidden[rows], down[...]) + vecs[7:8]).astype(BF)


def finish(hidden, resid, vecs, parts, plan):
    tokens, ff = hidden.shape
    model = resid.shape[1]
    return pl.pallas_call(
        functools.partial(finish_body, plan, len(parts)),
        in_specs=[VMEM] * 3 + [HBM] * len(parts),
        out_specs=VMEM,
        out_shape=jax.ShapeDtypeStruct((tokens, model), BF),
        scratch_shapes=[pltpu.VMEM((ff, model), BF), pltpu.SemaphoreType.DMA],
        compiler_params=params(),
        name="finish",
        cost_estimate=cost(6),
    )(hidden, resid, vecs, *parts)


def along(value, offset):
    return lax.ppermute(value, "fsdp", [(i, i ^ offset) for i in range(8)])


def across(value, offset, size):
    return lax.ppermute(value, "dp", [(i, i ^ offset) for i in range(size)])


def gather(piece, size, cut):
    rows = piece.shape[0]
    if size != 8:
        whole = lax.all_gather(piece, "fsdp", axis=0, tiled=True)
        return [whole], pieces_of([(0, False, 0, rows, size)], rows)
    along_x = along(piece, 2)
    along_y = along(piece, 4)
    core = along(piece, 1)
    top = along(along_x[:cut], 4)
    bottom = along(along_y[cut:], 2)
    parts = [piece, core, along_x, along_y]
    parts += [along(along_x, 1), along(along_y, 1), top, bottom, along(top, 1), along(bottom, 1)]
    whole = [(offset, True, 0, rows, 1) for offset in (0, 1, 2, 4, 3, 5)]
    halves = [(offset, True, first, count, 1) for offset in (6, 7) for first, count in ((0, cut), (cut, rows - cut))]
    return parts, pieces_of(whole + halves, rows)


def pack_body(w_in, w_out, *refs):
    vectors = refs[:8]
    up_bias, out = refs[8:]
    width, model = w_out.shape
    for band in range(3):
        out[band * width : (band + 1) * width] = w_in[:, band * model : (band + 1) * model]
    out[3 * width : 4 * width] = w_out[...]
    rows = [vector[...].astype(F32).reshape(1, width) for vector in vectors]
    bias = up_bias[...].astype(F32).reshape(1, 4 * width)
    rows += [bias[:, at * width : (at + 1) * width] for at in range(4)]
    rows += [jnp.zeros((4, width), F32)]
    out[4 * width :] = jnp.zeros((EXTRA, model), BF)
    out[4 * width :, 0:width] = jnp.concatenate(rows, axis=0).astype(BF)


def pack(project_in, project_out, vectors, up_bias):
    width, model = project_out.shape
    return pl.pallas_call(
        pack_body,
        in_specs=[VMEM] * 11,
        out_specs=VMEM,
        out_shape=jax.ShapeDtypeStruct((4 * width + EXTRA, model), BF),
        compiler_params=params(),
        name="pack",
        cost_estimate=cost(3),
    )(project_in, project_out, *vectors, up_bias)


def plus(*values):
    total = values[0].astype(F32)
    for value in values[1:]:
        total = total + value.astype(F32)
    return total


def scatter(grads, size, dims):
    if len(grads) == 1:
        own = lax.psum_scatter(grads[0], "fsdp", scatter_dimension=dims, tiled=True)
        return lax.psum(own, "dp").astype(F32)
    here, there = grads
    held = plus(here, along(there, 1)).astype(BF)
    from_x = along(held[0:2], 2)
    from_y = along(held[2:4], 4)
    next_x = along(plus(held[4], from_y[1]).astype(BF), 2)
    next_y = along(plus(held[5], from_x[1]).astype(BF), 4)
    top = plus(held[6], from_x[0], next_y).astype(BF)
    bottom = plus(held[7], from_y[0], next_x).astype(BF)
    own = jnp.stack([top, bottom])
    own = plus(own, across(own, 1, size)).astype(BF)
    own = plus(own, across(own, 2, size))
    return own.reshape(-1, own.shape[2])


def reduce_small(value, size, fast):
    if not fast:
        return lax.psum(value, ("dp", "fsdp"))
    for offset in (1, 2, 4):
        value = value + along(value, offset)
    for offset in (1, 2):
        value = value + across(value, offset, size)
    return value


def shards(
    group,
    frames,
    upstream,
    utterance,
    first_gain,
    first_shift,
    project_in,
    query_bias,
    value_bias,
    project_out,
    out_bias,
    second_gain,
    second_shift,
    up_weight,
    up_bias,
    down_weight,
    down_bias,
):
    micro, nrows, length, model = frames.shape
    rows = micro * nrows
    size = model // project_out.shape[0]
    width = model // size
    ff = up_weight.shape[1]
    x = frames.reshape(rows, length, model)
    dy = upstream.reshape(rows * length, model)
    utter = utterance.reshape(rows, length // SEG)
    vectors = (first_gain, first_shift, query_bias, value_bias, out_bias, second_gain, second_shift, down_bias)
    fast = size == 8 and group == 4
    packed = pack(project_in, project_out, vectors, up_bias)
    a_parts, a_plan = gather(packed, size, 2 * width)
    u_parts, u_plan = gather(up_weight, size, width // 2)
    d_parts, d_plan = gather(down_weight, size, ff // size // 2)
    vecs, q, k, v, p, att, resid, n2 = front(x, utter, a_parts, a_plan, width, size)
    n2 = n2.reshape(rows * length, model)
    flat = resid.reshape(rows * length, model)
    hidden, du, gub, *gdown = middle(
        n2, dy, vecs, u_parts, (u_plan, width), d_parts, (d_plan, ff // size), fast
    )
    dresid, datt, sums2, *gup = back(
        n2, du, flat, dy, att, vecs, u_parts, (u_plan, width), a_parts, a_plan, width, fast
    )
    shape = (rows, length, model)
    dx, sums1, *gin = rear(
        q, k, v, p, datt.reshape(shape), x, dresid.reshape(shape), vecs, a_parts, a_plan, width, fast
    )
    out = finish(hidden, flat, vecs, d_parts, (d_plan, ff // size))
    small = jnp.concatenate([sums1, sums2, gub], axis=0)
    small = reduce_small(small, group, fast)
    me = lax.axis_index("fsdp")

    def own(row):
        return lax.dynamic_slice_in_dim(small[row], me * width, width, 0)

    gub = lax.dynamic_slice_in_dim(small[8:].reshape(-1), me * (ff // size), ff // size, 0)
    gdown = scatter(gdown, group, 1).T
    gup = scatter(gup, group, 0)
    gin = scatter(gin, group, 0)
    return (
        out.reshape(frames.shape),
        dx.reshape(frames.shape),
        own(0),
        own(1),
        gin,
        own(2),
        own(3),
        gup[:, ff:],
        own(6),
        own(4),
        own(5),
        gup[:, :ff],
        gub,
        gdown,
        own(7),
    )


def solution(mesh):
    rows = P(None, ("dp", "fsdp"), None, None)
    vector = P("fsdp")
    matrix = P("fsdp", None)
    weights = (vector, vector, matrix, vector, vector, matrix, vector, vector, vector, matrix, vector, matrix, vector)
    return jax.shard_map(
        functools.partial(shards, mesh.shape["dp"]),
        mesh=mesh,
        in_specs=(rows, rows, P(None, ("dp", "fsdp"), None)) + weights,
        out_specs=(rows, rows) + weights,
        check_vma=False,
    )
```

```python
import functools

import jax
import jax.numpy as jnp
from jax import lax
from jax.experimental import pallas as pl
from jax.experimental.pallas import tpu as pltpu
from jax.sharding import PartitionSpec as P

HEADS = 8
SEG = 16
RIGHT = 4
LEFT = 30
MEMS = 4
QB = 128
WIN = 176
SLOTS = 16
KEYS = WIN + SLOTS
SLOTS_OF = {(1, 0): 0, (3, 0): 1, (2, 1): 2, (3, 1): 3, (1, 1): 4, (2, 0): 5, (0, 0): 6, (0, 1): 7}
TILE = 512
EXTRA = 16
BF = jnp.bfloat16
F32 = jnp.float32
HBM = pl.BlockSpec(memory_space=pl.ANY)
VMEM = pl.BlockSpec(memory_space=pltpu.VMEM)
LIMIT = 16 * 2**20


def nn(a, b):
    return lax.dot_general(a, b, (((1,), (0,)), ((), ())), preferred_element_type=F32)


def nt(a, b):
    return lax.dot_general(a, b, (((1,), (1,)), ((), ())), preferred_element_type=F32)


def tn(a, b):
    return lax.dot_general(a, b, (((0,), (0,)), ((), ())), preferred_element_type=F32)


def params(limit=LIMIT):
    return pltpu.CompilerParams(vmem_limit_bytes=limit)


def cost(micros):
    return pl.CostEstimate(flops=int(micros * 1.15e9), bytes_accessed=0, transcendentals=0)


def window(block, length):
    first = min(max(block * QB - 32, 0), length - WIN)
    slot = min(max(block * QB // SEG - MEMS, 0), length // SEG - SLOTS)
    return first, slot


def start_copies(copies):
    for copy in copies:
        copy.start()


def wait_copies(copies):
    for copy in copies:
        copy.wait()


def full(shape, dtype):
    return jax.ShapeDtypeStruct(shape, dtype)


def assemble(plan, parts, segments, sem):
    me = lax.axis_index("fsdp")
    copies = []
    for number, (offset, relative, first, rows, count) in enumerate(plan):
        for each in range(count):
            device = jnp.bitwise_xor(me, offset) if relative else each
            for start, height, target, column in segments:
                low, high = max(first, start), min(first + rows, start + height)
                if low < high:
                    place = pl.multiple_of(device * height, height) + low - start
                    source = parts[number].at[pl.ds(each * rows + low - first, high - low), :]
                    wide = source.shape[1]
                    copies.append(
                        pltpu.make_async_copy(
                            source, target.at[pl.ds(place, high - low), pl.ds(column, wide)], sem
                        )
                    )
    return copies


def emit(whole, grads, part, within, sem):
    if len(grads) == 1:
        return [pltpu.make_async_copy(whole, within(grads[0]), sem)]
    me = lax.axis_index("fsdp")
    copies = []
    for core in range(2):
        for (chip, top), slot in SLOTS_OF.items():
            device = jnp.bitwise_xor(me, 2 * chip + core)
            copies.append(
                pltpu.make_async_copy(part(device, top), within(grads[core].at[slot]), sem)
            )
    return copies


def row_part(whole, width):
    half = width // 2
    return lambda device, top: whole.at[
        pl.ds(pl.multiple_of(device * width, width) + top * half, half), :
    ]


def stats(value):
    mean = jnp.mean(value, axis=-1, keepdims=True)
    offset = value - mean
    spread = jnp.mean(offset * offset, axis=-1, keepdims=True)
    scale = lax.rsqrt(spread + 1e-05)
    return offset * scale, scale


def averages(length):
    blocks = length // QB
    rows = blocks * SLOTS
    row = lax.broadcasted_iota(jnp.int32, (rows, length), 0)
    seg = lax.broadcasted_iota(jnp.int32, (rows, length), 1) // SEG
    slot = row % SLOTS
    for block in range(blocks):
        first = window(block, length)[1]
        slot = slot + jnp.where(row // SLOTS == block, first, 0)
    return jnp.where(slot == seg, 1.0 / SEG, 0.0).astype(BF)


def head_pair(value):
    lane = lax.broadcasted_iota(jnp.int32, value.shape, 1)
    zero = jnp.zeros_like(value)
    half = value.shape[1] // 2
    return jnp.concatenate(
        [jnp.where(lane < half, value, zero), jnp.where(lane >= half, value, zero)], axis=0
    )


def diagonal(value):
    half = value.shape[0] // 2
    return jnp.concatenate([value[:half, :QB], value[half:, QB:]], axis=0)


def visible_bias(bias_ref, utter_ref, row, nsegs):
    length = nsegs * SEG
    key = lax.broadcasted_iota(jnp.int32, (KEYS, QB), 0)
    query = lax.broadcasted_iota(jnp.int32, (KEYS, QB), 1)
    segs = QB // SEG
    starts = [jnp.int32(0)]
    for seg in range(1, nsegs):
        same = utter_ref[row, seg] == utter_ref[row, seg - 1]
        starts.append(jnp.where(same, starts[-1], seg))
    for block in range(length // QB):
        first, slot = window(block, length)
        lower = jnp.zeros((KEYS, QB), jnp.int32)
        upper = jnp.zeros((KEYS, QB), jnp.int32)
        for part in range(segs):
            seg = block * segs + part
            more = jnp.int32(0)
            if seg + 1 < nsegs:
                more = jnp.where(utter_ref[row, seg + 1] == utter_ref[row, seg], RIGHT, 0)
            frame_low = jnp.maximum(seg * SEG - LEFT, starts[seg] * SEG) - first
            frame_high = seg * SEG + SEG + more - first
            slot_low = jnp.maximum(seg - MEMS, starts[seg]) - slot + WIN
            slot_high = jnp.int32(seg - slot + WIN)
            here = query // SEG == part
            lower = jnp.where(here, jnp.where(key < WIN, frame_low, slot_low), lower)
            upper = jnp.where(here, jnp.where(key < WIN, frame_high, slot_high), upper)
        seen = (key >= lower) & (key < upper)
        bias_ref[block] = jnp.where(seen, 0.0, -1e9)


def call(body, name, micros, ins, outs, scratch, args, limit=LIMIT):
    kinds = [HBM if by_copy else VMEM for _, by_copy in outs]
    return pl.pallas_call(
        body,
        in_specs=[VMEM] * ins + [HBM] * (len(args) - ins),
        out_specs=kinds,
        out_shape=[shape for shape, _ in outs],
        scratch_shapes=scratch,
        compiler_params=params(limit),
        name=name,
        cost_estimate=cost(micros),
    )(*args)


def attention(q_ref, k_ref, v_ref, p_ref, bias, att_ref, att, length):
    for block in range(length // QB):
        first, _ = window(block, length)
        rows = slice(block * QB, (block + 1) * QB)
        own = slice(length + block * SLOTS, length + (block + 1) * SLOTS)
        for pair in range(HEADS // 2):
            lanes = slice(pair * 128, (pair + 1) * 128)
            keys = jnp.concatenate([k_ref[first : first + WIN, lanes], k_ref[own, lanes]], axis=0)
            vals = jnp.concatenate([v_ref[first : first + WIN, lanes], v_ref[own, lanes]], axis=0)
            seen = bias[block]
            scores = nt(keys, head_pair(q_ref[rows, lanes]))
            scores = scores + jnp.concatenate([seen, seen], axis=1)
            top = jnp.max(scores, axis=0, keepdims=True)
            raised = jnp.exp(scores - top)
            probs = (raised * (1.0 / jnp.sum(raised, axis=0, keepdims=True))).astype(BF)
            p_ref[block, pair] = probs
            found = diagonal(tn(vals, probs))
            att_ref[lanes, rows] = found.astype(BF)
            att[rows, lanes] = found.T.astype(BF)


def front_body(row, first_call, plan, width, utter, x, vecs_in, w_in_in, w_out_in, *refs):
    nparts = len(plan) if first_call else 0
    parts = refs[:nparts]
    outs = refs[nparts:]
    if first_call:
        vecs, w_in, w_out, *outs = outs
    else:
        vecs, w_in, w_out = vecs_in, w_in_in, w_out_in
    (q_out, k_out, v_out, wide_out, p_out, att_out, resid_out, n2_out, bias, att, *outs) = outs
    length, model = x.shape[1], x.shape[2]
    value = x[row].astype(F32)
    if first_call:
        small, sem = outs
        segments = [(band * width, width, w_in, band * model) for band in range(3)]
        segments += [(3 * width, width, w_out, 0), (4 * width, EXTRA, small, 0)]
        copies = assemble(plan, parts, segments, sem)
        start_copies(copies)
    visible_bias(bias, utter, row, length // SEG)
    unit, _ = stats(value)
    if first_call:
        wait_copies(copies)
        total = jnp.zeros((8, model), F32)
        ups = [jnp.zeros((1, model), F32) for _ in range(4)]
        for piece in range(model // width):
            found = small[piece * EXTRA : (piece + 1) * EXTRA].astype(F32)
            total = total + pltpu.roll(found, piece * width, 1)[:8]
            for part in range(4):
                place = (piece * 4 + part) * width
                ups[place // model] += pltpu.roll(found, place % model, 1)[8 + part : 9 + part]
        vecs[0:8] = total
        for part in range(4):
            vecs[8 + part : 9 + part] = ups[part]
        vecs[12:16] = jnp.zeros((4, model), F32)
    normed = (unit * vecs[0:1] + vecs[1:2]).astype(BF)
    summary = nn(averages(length), normed).astype(BF)
    wide = jnp.concatenate([normed, summary], axis=0)
    wide_out[...] = wide.T
    q_out[...] = ((nn(normed, w_in[:, :model]) + vecs[2:3]).astype(BF).astype(F32) * 0.125).astype(BF)
    k_out[...] = nn(wide, w_in[:, model : 2 * model]).astype(BF)
    v_out[...] = (nn(wide, w_in[:, 2 * model :]) + vecs[3:4]).astype(BF)
    attention(q_out, k_out, v_out, p_out, bias, att_out, att, length)
    resid = value + nn(att[...], w_out[...]) + vecs[4:5]
    resid_out[...] = resid
    unit, _ = stats(resid)
    n2_out[...] = (unit * vecs[5:6] + vecs[6:7]).astype(BF)


def front(row, x, utter, vecs, w_in, w_out, plan, parts, width):
    _, length, model = x.shape
    blocks = length // QB
    wide = length + blocks * SLOTS
    first_call = vecs is None
    outs = [
        full((length, model), BF),
        full((wide, model), BF),
        full((wide, model), BF),
        full((model, wide), BF),
        full((blocks, HEADS // 2, KEYS, 2 * QB), BF),
        full((model, length), BF),
        full((length, model), F32),
        full((length, model), BF),
    ]
    scratch = [pltpu.VMEM((blocks, KEYS, QB), F32), pltpu.VMEM((length, model), BF)]
    if first_call:
        outs = [full((16, model), F32), full((model, 3 * model), BF), full((model, model), BF)] + outs
        pieces = model // width
        scratch += [pltpu.VMEM((pieces * EXTRA, model), BF), pltpu.SemaphoreType.DMA]
        args = [utter, x] + list(parts)
        specs = [pl.BlockSpec(memory_space=pltpu.SMEM), VMEM] + [HBM] * len(parts)

        def body(utter, x, *refs):
            front_body(row, True, plan, width, utter, x, None, None, None, *refs)
    else:
        args = [utter, x, vecs, w_in, w_out]
        specs = [pl.BlockSpec(memory_space=pltpu.SMEM)] + [VMEM] * 4
        body = functools.partial(front_body, row, False, plan, width)
    return pl.pallas_call(
        body,
        in_specs=specs,
        out_specs=[VMEM] * len(outs),
        out_shape=outs,
        scratch_shapes=scratch,
        compiler_params=params(),
        name=f"front{row}",
        cost_estimate=cost(7),
    )(*args)


def gelu_both(v):
    c = 0.7978845608028654
    square = v * v
    bent = jnp.tanh(c * v * (1.0 + 0.044715 * square))
    half = 0.5 + 0.5 * bent
    slope = half + 0.5 * v * (1.0 - bent * bent) * (c * (1.0 + 3 * 0.044715 * square))
    return v * half, slope


def middle_body(rows, plan, width, n_grad, *refs):
    n2s = refs[:rows]
    dy, vecs, *refs = refs[rows:]
    parts = refs[: len(plan)]
    hidden, slopes, up, *grads = refs[len(plan) : len(plan) + 3 + n_grad]
    dyt, grad, sem = refs[len(plan) + 3 + n_grad :]
    tokens, model = dy.shape
    ff = up.shape[1]
    tall = ff * width // model
    copies = assemble(plan, parts, [(0, width, up, 0)], sem)
    start_copies(copies)
    dyt[...] = dy[...].T
    wait_copies(copies)
    length = n2s[0].shape[0]
    step = 128
    for tile in range(ff // TILE):
        cols = slice(tile * TILE, (tile + 1) * TILE)
        for chunk in range(tokens // step):
            rows = slice(chunk * step, (chunk + 1) * step)
            at = chunk * step % length
            u = nn(n2s[chunk * step // length][at : at + step], up[:, cols]) + vecs[8 + tile : 9 + tile]
            value, slope = gelu_both(u)
            hidden[rows, cols] = value.astype(BF)
            slopes[rows, cols] = slope.astype(BF)
        grad[:, cols] = nn(dyt[...], hidden[:, cols]).astype(BF)
    half = model // 2
    copies = emit(
        grad,
        grads,
        lambda device, top: grad.at[pl.ds(top * half, half), pl.ds(pl.multiple_of(device * tall, tall), tall)],
        lambda ref: ref,
        sem,
    )
    start_copies(copies)
    wait_copies(copies)


def middle(n2s, dy, vecs, parts, plan, width, ff, fast):
    tokens, model = dy.shape
    tall = ff * width // model
    shapes = [(8, model // 2, tall)] * 2 if fast else [(model, ff)]
    outs = [
        (full((tokens, ff), BF), False),
        (full((tokens, ff), BF), False),
        (full((model, ff), BF), False),
    ]
    outs += [(full(shape, BF), True) for shape in shapes]
    scratch = [pltpu.VMEM((model, tokens), BF), pltpu.VMEM((model, ff), BF), pltpu.SemaphoreType.DMA]
    body = functools.partial(middle_body, len(n2s), plan, width, len(shapes))
    return call(body, "middle", 8, len(n2s) + 2, outs, scratch, [*n2s, dy, vecs, *parts])


def turn_body(plan, dy, slopes, *refs):
    parts = refs[: len(plan)]
    du, ub, down, sem = refs[len(plan) :]
    tokens, model = dy.shape
    ff = down.shape[0]
    tall = plan[0][3]
    copies = assemble(plan, parts, [(0, tall, down, 0)], sem)
    start_copies(copies)
    wait_copies(copies)
    step = 128
    for tile in range(ff // TILE):
        cols = slice(tile * TILE, (tile + 1) * TILE)
        sums = jnp.zeros((1, TILE), F32)
        for chunk in range(tokens // step):
            rows = slice(chunk * step, (chunk + 1) * step)
            back = nt(dy[rows], down[cols]).astype(BF).astype(F32) * slopes[rows, cols].astype(F32)
            du[rows, cols] = back.astype(BF)
            sums = sums + jnp.sum(back, axis=0, keepdims=True)
        ub[tile : tile + 1] = sums


def turn(dy, slopes, parts, plan):
    tokens, model = dy.shape
    ff = slopes.shape[1]
    outs = [
        (full((tokens, ff), BF), False),
        (full((ff // TILE, TILE), F32), False),
        (full((ff, model), BF), False),
    ]
    args = [dy, slopes, *parts]
    return call(functools.partial(turn_body, plan), "turn", 5, 2, outs, [pltpu.SemaphoreType.DMA], args)


def rise_body(rows, width, *refs):
    n2s = refs[:rows]
    du, *grads = refs[rows:-3]
    n2t, gup, sem = refs[-3:]
    length = n2s[0].shape[0]
    for row in range(rows):
        n2t[:, row * length : (row + 1) * length] = n2s[row][...].T
    for tile in range(du.shape[1] // TILE):
        cols = slice(tile * TILE, (tile + 1) * TILE)
        gup[:, cols] = nn(n2t[...], du[:, cols]).astype(BF)
    copies = emit(gup, grads, row_part(gup, width), lambda ref: ref, sem)
    start_copies(copies)
    wait_copies(copies)


def rise(n2s, du, width, fast):
    model = n2s[0].shape[1]
    tokens, ff = du.shape
    shapes = [(8, width // 2, ff)] * 2 if fast else [(model, ff)]
    outs = [(full(shape, BF), True) for shape in shapes]
    scratch = [pltpu.VMEM((model, tokens), BF), pltpu.VMEM((model, ff), BF), pltpu.SemaphoreType.DMA]
    body = functools.partial(rise_body, len(n2s), width)
    return call(body, "rise", 4, len(n2s) + 1, outs, scratch, [*n2s, du])


def norm_back(grad, unit, scale):
    first = jnp.mean(grad, axis=-1, keepdims=True)
    second = jnp.mean(grad * unit, axis=-1, keepdims=True)
    return scale * (grad - first - unit * second)


def back_body(rows, *refs):
    resids = refs[:rows]
    du, dy, vecs, up, w_out, dresid, datt, sums = refs[rows:]
    tokens, model = dy.shape
    length = resids[0].shape[0]
    step = 128
    gains = jnp.zeros((1, model), F32)
    shifts = jnp.zeros((1, model), F32)
    biases = jnp.zeros((1, model), F32)
    downs = jnp.zeros((1, model), F32)
    for chunk in range(tokens // step):
        rows = slice(chunk * step, (chunk + 1) * step)
        at = chunk * step % length
        grad = nt(du[rows], up[...])
        unit, scale = stats(resids[chunk * step // length][at : at + step])
        gains = gains + jnp.sum(grad * unit, axis=0, keepdims=True)
        shifts = shifts + jnp.sum(grad, axis=0, keepdims=True)
        top = dy[rows].astype(F32)
        downs = downs + jnp.sum(top, axis=0, keepdims=True)
        total = top + norm_back(grad * vecs[5:6], unit, scale)
        biases = biases + jnp.sum(total, axis=0, keepdims=True)
        dresid[rows] = total
        datt[rows] = nt(total.astype(BF), w_out[...]).astype(BF)
    sums[0:1] = gains
    sums[1:2] = shifts
    sums[2:3] = biases
    sums[3:4] = downs


def back(resids, du, dy, vecs, up, w_out):
    tokens, model = dy.shape
    outs = [
        (full((tokens, model), F32), False),
        (full((tokens, model), BF), False),
        (full((4, model), F32), False),
    ]
    args = [*resids, du, dy, vecs, up, w_out]
    return call(functools.partial(back_body, len(resids)), "back", 8, len(args), outs, [], args)


def rear_body(row, q, k, v, p, datt, mixed, sums, dk, dv):
    length, model = q.shape
    extent = k.shape[0]
    base = row * length
    dk[...] = jnp.zeros_like(dk)
    dv[...] = jnp.zeros_like(dv)
    mixed[length:extent, 0:model] = jnp.zeros((extent - length, model), BF)
    for block in range(length // QB):
        first, _ = window(block, length)
        rows = slice(block * QB, (block + 1) * QB)
        own = slice(length + block * SLOTS, length + (block + 1) * SLOTS)
        span = slice(first, first + WIN)
        for pair in range(HEADS // 2):
            lanes = slice(pair * 128, (pair + 1) * 128)
            keys = jnp.concatenate([k[span, lanes], k[own, lanes]], axis=0)
            vals = jnp.concatenate([v[span, lanes], v[own, lanes]], axis=0)
            queries = head_pair(q[rows, lanes])
            tops = head_pair(datt[base + block * QB : base + (block + 1) * QB, lanes])
            probs = p[block, pair]
            wides = probs.astype(F32)
            back = nt(vals, tops)
            inner = jnp.sum(wides * back, axis=0, keepdims=True)
            dscores = (wides * (back - inner)).astype(BF)
            gv = nn(probs, tops)
            gk = nn(dscores, queries)
            dv[span, lanes] += gv[:WIN]
            dv[own, lanes] = gv[WIN:]
            dk[span, lanes] += gk[:WIN]
            dk[own, lanes] = gk[WIN:]
            gq = diagonal(tn(keys, dscores)).T * 0.125
            mixed[rows, lanes] = gq.astype(BF)
    mixed[:, model : 2 * model] = dk[...].astype(BF)
    mixed[:, 2 * model :] = dv[...].astype(BF)
    sums[0:1] = jnp.sum(mixed[:, 0:model].astype(F32), axis=0, keepdims=True)
    sums[1:2] = jnp.sum(mixed[:, 2 * model :].astype(F32), axis=0, keepdims=True)


def rear(row, q, k, v, p, datt):
    length, model = q.shape
    extent = k.shape[0]
    outs = [(full((extent, 3 * model), BF), False), (full((2, model), F32), False)]
    scratch = [pltpu.VMEM((extent, model), F32), pltpu.VMEM((extent, model), F32)]
    body = functools.partial(rear_body, row)
    return call(body, f"rear{row}", 7, 5, outs, scratch, [q, k, v, p, datt])


def inner_body(rows, width, *refs):
    wides = refs[:rows]
    mixeds = refs[rows : 2 * rows]
    atts = refs[2 * rows : 3 * rows]
    dresid, *grads = refs[3 * rows : -3]
    gin, gout, sem = refs[-3:]
    model = gout.shape[0]
    length = atts[0].shape[1]
    for tile in range(3):
        cols = slice(tile * model, (tile + 1) * model)
        total = nn(wides[0][...], mixeds[0][:, cols])
        for row in range(1, rows):
            total = total + nn(wides[row][...], mixeds[row][:, cols])
        gin[:, cols] = total.astype(BF)
    total = nn(atts[0][...], dresid[0:length].astype(BF))
    for row in range(1, rows):
        total = total + nn(atts[row][...], dresid[row * length : (row + 1) * length].astype(BF))
    gout[...] = total.astype(BF)
    copies = emit(gin, grads, row_part(gin, width), lambda ref: ref.at[:, 0 : 3 * model], sem)
    copies += emit(gout, grads, row_part(gout, width), lambda ref: ref.at[:, 3 * model :], sem)
    start_copies(copies)
    wait_copies(copies)


def inner(wides, mixeds, atts, dresid, width, fast):
    model = dresid.shape[1]
    shapes = [(8, width // 2, 4 * model)] * 2 if fast else [(model, 4 * model)]
    outs = [(full(shape, BF), True) for shape in shapes]
    scratch = [pltpu.VMEM((model, 3 * model), BF), pltpu.VMEM((model, model), BF), pltpu.SemaphoreType.DMA]
    args = [*wides, *mixeds, *atts, dresid]
    body = functools.partial(inner_body, len(wides), width)
    return call(body, "inner", 4, len(args), outs, scratch, args)


def base_body(rows, x, dresid, vecs, w_in, gub, back_sums, *refs):
    mixeds = refs[:rows]
    rear_sums = refs[rows : 2 * rows]
    dx, sums = refs[2 * rows :]
    length, model = x.shape[1], x.shape[2]
    average = averages(length)
    gains = jnp.zeros((1, model), F32)
    shifts = jnp.zeros((1, model), F32)
    for row in range(rows):
        unit, scale = stats(x[row].astype(F32))
        grad = nt(mixeds[row][...], w_in[...])
        grad = grad[:length] + tn(average, grad[length:].astype(BF))
        gains = gains + jnp.sum(grad * unit, axis=0, keepdims=True)
        shifts = shifts + jnp.sum(grad, axis=0, keepdims=True)
        dx[row] = dresid[row * length : (row + 1) * length] + norm_back(grad * vecs[0:1], unit, scale)
    sums[0:1] = gains
    sums[1:2] = shifts
    sums[2:4] = wide_sum(*[part[...] for part in rear_sums])
    sums[4:8] = back_sums[...]
    sums[8:12] = gub[...]
    sums[12:16] = jnp.zeros((4, model), F32)


def base(x, dresid, vecs, w_in, gub, back_sums, mixeds, rear_sums):
    rows, length, model = x.shape
    outs = [(full((rows, length, model), F32), False), (full((16, model), F32), False)]
    args = [x, dresid, vecs, w_in, gub, back_sums, *mixeds, *rear_sums]
    return call(functools.partial(base_body, rows), "base", 5, len(args), outs, [], args)


def finish_body(rows, vecs, hidden, down, *refs):
    resids = refs[:rows]
    out = refs[rows]
    length = resids[0].shape[0]
    step = 128
    for chunk in range(hidden.shape[0] // step):
        rows = slice(chunk * step, (chunk + 1) * step)
        at = chunk * step % length
        resid = resids[chunk * step // length][at : at + step]
        out[rows] = (resid + nn(hidden[rows], down[...]) + vecs[7:8]).astype(BF)


def finish(vecs, hidden, down, resids):
    outs = [(full((hidden.shape[0], down.shape[1]), BF), False)]
    args = [vecs, hidden, down, *resids]
    return call(functools.partial(finish_body, len(resids)), "finish", 4, len(args), outs, [], args)[0]


def along(value, offset):
    return lax.ppermute(value, "fsdp", [(i, i ^ offset) for i in range(8)])


def across(value, offset, size):
    return lax.ppermute(value, "dp", [(i, i ^ offset) for i in range(size)])


def pack_body(*refs):
    sources, out = refs[:11], refs[11]
    w_in, w_out, *rows, sem = refs[12:]
    width, model = w_out.shape
    targets = [w_in, w_out, *rows]
    copies = [pltpu.make_async_copy(a, b, sem) for a, b in zip(sources, targets)]
    start_copies(copies)
    out[4 * width :] = jnp.zeros((EXTRA, model), BF)
    wait_copies(copies)
    for band in range(3):
        out[band * width : (band + 1) * width] = w_in[:, band * model : (band + 1) * model]
    out[3 * width : 4 * width] = w_out[...]
    lines = [row[...].astype(F32).reshape(1, width) for row in rows[:8]]
    bias = rows[8][...].astype(F32).reshape(1, 4 * width)
    lines += [bias[:, at * width : (at + 1) * width] for at in range(4)]
    lines += [jnp.zeros((4, width), F32)]
    out[4 * width :, 0:width] = jnp.concatenate(lines, axis=0).astype(BF)


def pack(project_in, project_out, vectors, up_bias):
    width, model = project_out.shape
    outs = [(full((4 * width + EXTRA, model), BF), False)]
    args = [project_in, project_out, *vectors, up_bias]
    scratch = [pltpu.VMEM(arg.shape, BF) for arg in args] + [pltpu.SemaphoreType.DMA]
    return call(pack_body, "pack", 2, 0, outs, scratch, args, 60 * 2**20)[0]


def settle_body(width, tall, small, *refs):
    me = lax.axis_index("fsdp")
    value = small[...]
    model = value.shape[1]
    turned = pltpu.roll(value, lax.rem(model - me * width, model), 1)
    for row, out in enumerate(refs[:8]):
        out[...] = turned[row : row + 1, 0:width].reshape(width)
    place = me * tall
    wide = jnp.zeros((1, model), F32)
    for row in range(4):
        wide = jnp.where(place // model == row, value[8 + row : 9 + row], wide)
    wide = jnp.concatenate([wide] * 8, axis=0)
    turned = pltpu.roll(wide, lax.rem(model - lax.rem(place, model), model), 1)
    refs[8][...] = turned[0:1, 0:tall].reshape(tall)


def settle(small, width, tall):
    outs = [(full((width,), F32), False)] * 8 + [(full((tall,), F32), False)]
    return call(functools.partial(settle_body, width, tall), "settle", 2, 1, outs, [], [small])


def wide_sum(*values):
    total = values[0].astype(F32)
    for value in values[1:]:
        total = total + value.astype(F32)
    return total


def plus(*values):
    def body(*refs):
        refs[-1][...] = wide_sum(*[ref[...] for ref in refs[:-1]]).astype(refs[-1].dtype)

    outs = [(full(values[0].shape, values[0].dtype), False)]
    return call(body, "plus", 1, len(values), outs, [], values)[0]


def second(held, from_x, from_y):
    def body(held, from_x, from_y, to_x, to_y):
        to_x[...] = wide_sum(held[4], from_y[1]).astype(BF)
        to_y[...] = wide_sum(held[5], from_x[1]).astype(BF)

    outs = [(full(held.shape[1:], BF), False)] * 2
    return call(body, "second", 1, 3, outs, [], [held, from_x, from_y])


def own_halves(held, from_x, from_y, last_x, last_y):
    return (
        wide_sum(held[6], from_x[0], last_y[...]).astype(BF),
        wide_sum(held[7], from_y[0], last_x[...]).astype(BF),
    )


def odd_plane():
    return lax.rem(lax.axis_index("dp"), 2) == 1


def third(*args):
    def body(held, from_x, from_y, last_x, last_y, keep, send):
        top, bottom = own_halves(held, from_x, from_y, last_x, last_y)
        odd = odd_plane()

        @pl.when(odd)
        def _():
            keep[...] = bottom
            send[...] = top

        @pl.when(jnp.logical_not(odd))
        def _():
            keep[...] = top
            send[...] = bottom

    outs = [(full(args[0].shape[1:], BF), False)] * 2
    return call(body, "third", 1, 5, outs, [], args)


def third_whole(*args):
    def body(held, from_x, from_y, last_x, last_y, out):
        out[0], out[1] = own_halves(held, from_x, from_y, last_x, last_y)

    outs = [(full((2,) + args[0].shape[1:], BF), False)]
    return call(body, "third", 1, 5, outs, [], args)[0]


def last_down(keep, other):
    def body(keep, other, out):
        half = keep.shape[0]
        odd = odd_plane()

        @pl.when(odd)
        def _():
            out[:, :half] = other[...].astype(F32).T
            out[:, half:] = keep[...].astype(F32).T

        @pl.when(jnp.logical_not(odd))
        def _():
            out[:, :half] = keep[...].astype(F32).T
            out[:, half:] = other[...].astype(F32).T

    half, tall = keep.shape
    return call(body, "last_down", 1, 2, [(full((tall, 2 * half), F32), False)], [], [keep, other])[0]


def last_up(keep, other):
    def body(keep, other, out):
        half = keep.shape[0]
        odd = odd_plane()

        @pl.when(odd)
        def _():
            out[:half] = other[...].astype(F32)
            out[half:] = keep[...].astype(F32)

        @pl.when(jnp.logical_not(odd))
        def _():
            out[:half] = keep[...].astype(F32)
            out[half:] = other[...].astype(F32)

    half, ff = keep.shape
    return call(body, "last_up", 1, 2, [(full((2 * half, ff), F32), False)], [], [keep, other])[0]


def last_in(own, other, model):
    def body(own, other, g_in, g_out):
        half = own.shape[1]
        for part in range(2):
            rows = slice(part * half, (part + 1) * half)
            total = wide_sum(own[part], other[part])
            g_in[rows] = total[:, : 3 * model]
            g_out[rows] = total[:, 3 * model :]

    rows = 2 * own.shape[1]
    outs = [(full((rows, 3 * model), F32), False), (full((rows, model), F32), False)]
    return call(body, "last_in", 1, 2, outs, [], [own, other])


def after(value, *others):
    return lax.optimization_barrier((value,) + others)[0]


def whole_plan(rows, size):
    return [(0, False, 0, rows, size)]


def near_plan(rows, cut):
    plan = [(offset, True, 0, rows, 1) for offset in (0, 1, 2, 4, 3, 5)]
    for offset in (6, 7):
        plan += [(offset, True, 0, cut, 1), (offset, True, cut, rows - cut, 1)]
    return plan


def shards(
    group,
    frames,
    upstream,
    utterance,
    first_gain,
    first_shift,
    project_in,
    query_bias,
    value_bias,
    project_out,
    out_bias,
    second_gain,
    second_shift,
    up_weight,
    up_bias,
    down_weight,
    down_bias,
):
    micro, nrows, length, model = frames.shape
    rows = micro * nrows
    width = project_out.shape[0]
    size = model // width
    ff = up_weight.shape[1]
    tall = ff // size
    x = frames.reshape(rows, length, model)
    dy = upstream.reshape(rows * length, model)
    utter = utterance.reshape(rows, length // SEG)
    vectors = (first_gain, first_shift, query_bias, value_bias, out_bias, second_gain, second_shift, down_bias)
    fast = size == 8 and group == 4 and rows == 2
    packed = pack(project_in, project_out, vectors, up_bias)
    if fast:
        cut_a, cut_u, cut_d = 2 * width, width // 2, tall // 2
        plan_a, plan_u, plan_d = (
            near_plan(packed.shape[0], cut_a),
            near_plan(width, cut_u),
            near_plan(tall, cut_d),
        )
        a2, a4, a1 = along(packed, 2), along(packed, 4), along(packed, 1)
        up_piece = after(up_weight, a1)
        u2, u4, u1 = along(up_piece, 2), along(up_piece, 4), along(up_piece, 1)
        a_top, a_bottom = along(a2[:cut_a], 4), along(a4[cut_a:], 2)
        parts_a = [packed, a1, a2, a4, along(a2, 1), along(a4, 1), a_top, a_bottom]
        parts_a += [along(a_top, 1), along(a_bottom, 1)]
        u3, u5 = along(u2, 1), along(u4, 1)
        u_top, u_bottom = along(u2[:cut_u], 4), along(u4[cut_u:], 2)
        down_piece = after(down_weight, a_top, a_bottom)
        d2, d4 = along(down_piece, 2), along(down_piece, 4)
        first_utter = after(utter, u3, u5, u1)
    else:
        plan_a, plan_u, plan_d = whole_plan(packed.shape[0], size), whole_plan(width, size), whole_plan(tall, size)
        parts_a = [lax.all_gather(packed, "fsdp", axis=0, tiled=True)]
        parts_u = [lax.all_gather(up_weight, "fsdp", axis=0, tiled=True)]
        parts_d = [lax.all_gather(down_weight, "fsdp", axis=0, tiled=True)]
        first_utter = utter
    saved = []
    vecs, w_in, w_out, *first = front(0, x, first_utter, None, None, None, plan_a, parts_a, width)
    saved.append(first)
    held = vecs
    if fast:
        held = after(vecs, u_top, u_bottom, d2, d4)
    for row in range(1, rows):
        saved.append(front(row, x, utter, held, w_in, w_out, plan_a, None, width))
    qs, ks, vs, wides, ps, atts, resids, n2s = zip(*saved)
    if fast:
        done = n2s[0]
        parts_u = [up_piece, u1, u2, u4, u3, u5, u_top, u_bottom]
        parts_u += [along(after(u_top, done), 1), along(after(u_bottom, done), 1)]
        d_top, d_bottom = along(after(d2, done)[:cut_d], 4), along(after(d4, done)[cut_d:], 2)
        d1 = along(after(down_piece, done), 1)
        done = n2s[1]
        parts_d = [down_piece, d1, d2, d4]
        parts_d += [along(after(d2, done), 1), along(after(d4, done), 1), d_top, d_bottom]
        parts_d += [along(after(d_top, done), 1), along(after(d_bottom, done), 1)]
    hidden, slopes, up, *gdown = middle(n2s, dy, vecs, parts_u, plan_u, width, ff, fast)
    if fast:
        d_core = along(gdown[1], 1)
        du, gub, down = turn(dy, slopes, parts_d, plan_d)
        d_core = after(d_core, gub)
        d_sum = plus(gdown[0], d_core)
        d_x, d_y = along(d_sum[0:2], 2), along(d_sum[2:4], 4)
        gup = rise(n2s, after(du, d_core), width, fast)
        d_x, d_y, u_part = lax.optimization_barrier((d_x, d_y, gup[1]))
        to_x, to_y = second(d_sum, d_x, d_y)
        d_x2, d_y2 = along(to_x, 2), along(to_y, 4)
        u_core = along(u_part, 1)
        dresid, datt, sums2 = back(resids, after(du, d_x, d_y), dy, vecs, up, w_out)
        d_x2, d_y2, u_core, done = lax.optimization_barrier((d_x2, d_y2, u_core, sums2))
        u_sum = plus(gup[0], u_core)
        u_x, u_y = along(u_sum[0:2], 2), along(u_sum[2:4], 4)
        d_keep, d_send = third(d_sum, d_x, d_y, d_x2, d_y2)
        d_z = across(d_send, 1, group)
        mixed0, sums0 = rear(0, after(qs[0], d_x2, d_y2, u_core), ks[0], vs[0], ps[0], datt)
        mixed1, sums1 = rear(1, after(qs[1], sums0), ks[1], vs[1], ps[1], datt)
        mixeds = (mixed0, mixed1)
        u_x, u_y, d_z, done = lax.optimization_barrier((u_x, u_y, d_z, sums1))
        to_x, to_y = second(u_sum, u_x, u_y)
        u_x2, u_y2 = along(to_x, 2), along(to_y, 4)
        d_keep = plus(d_keep, d_z)
        d_z2 = across(d_keep, 2, group)
        gin = inner(wides, mixeds, atts, after(dresid, u_x, u_y, d_z), width, fast)
        u_x2, u_y2, d_z2, i_part = lax.optimization_barrier((u_x2, u_y2, d_z2, gin[1]))
        i_core = along(i_part, 1)
        d_keep = plus(d_keep, d_z2)
        d_other = across(d_keep, 1, group)
        u_keep, u_send = third(u_sum, u_x, u_y, u_x2, u_y2)
        u_z = across(u_send, 1, group)
        dx, small = base(
            x, after(dresid, u_x2, u_y2, d_z2, gin[0]), vecs, w_in, gub, sums2, mixeds, (sums0, sums1)
        )
        i_core, u_z, d_other, small = lax.optimization_barrier((i_core, u_z, d_other, small))
        i_sum = plus(gin[0], i_core)
        i_x, i_y = along(i_sum[0:2], 2), along(i_sum[2:4], 4)
        u_keep = plus(u_keep, u_z)
        u_z2 = across(u_keep, 2, group)
        small1 = along(small, 1)
        out = finish(after(vecs, i_core, u_z, d_other, small), hidden, down, resids)
        i_x, i_y, u_z2, small1, out = lax.optimization_barrier((i_x, i_y, u_z2, small1, out))
        to_x, to_y = second(i_sum, i_x, i_y)
        i_x2, i_y2 = along(to_x, 2), along(to_y, 4)
        small = plus(small, small1)
        small2 = along(small, 2)
        u_keep = plus(u_keep, u_z2)
        u_other = across(u_keep, 1, group)
        gdown = last_down(after(d_keep, to_x), d_other)
        small = plus(small, small2)
        small4 = along(small, 4)
        i_own = third_whole(i_sum, i_x, i_y, i_x2, i_y2)
        i_z = across(i_own, 1, group)
        small = plus(small, small4)
        small_z = across(small, 1, group)
        gup = last_up(after(u_keep, i_own), u_other)
        i_own = plus(i_own, i_z)
        i_z2 = across(i_own, 2, group)
        small = plus(small, small_z)
        small_z2 = across(small, 2, group)
        small = plus(small, small_z2)
        g_in, g_out = last_in(i_own, i_z2, model)
    else:
        du, gub, down = turn(dy, slopes, parts_d, plan_d)
        gup = rise(n2s, du, width, fast)
        dresid, datt, sums2 = back(resids, du, dy, vecs, up, w_out)
        pairs = [rear(row, qs[row], ks[row], vs[row], ps[row], datt) for row in range(rows)]
        mixeds = [pair[0] for pair in pairs]
        gin = inner(wides, mixeds, atts, dresid, width, fast)
        dx, small = base(x, dresid, vecs, w_in, gub, sums2, mixeds, [pair[1] for pair in pairs])
        out = finish(vecs, hidden, down, resids)

        def total(value, dim):
            own = lax.psum_scatter(value, "fsdp", scatter_dimension=dim, tiled=True)
            return lax.psum(own, "dp").astype(F32)

        gdown = total(gdown[0], 1).T
        gup = total(gup[0], 0)
        gin = total(gin[0], 0)
        g_in, g_out = gin[:, : 3 * model], gin[:, 3 * model :]
        small = lax.psum(small, ("dp", "fsdp"))
    vectors = settle(small, width, tall)
    return (
        out.reshape(frames.shape),
        dx.reshape(frames.shape),
        vectors[0],
        vectors[1],
        g_in,
        vectors[2],
        vectors[3],
        g_out,
        vectors[6],
        vectors[4],
        vectors[5],
        gup,
        vectors[8],
        gdown,
        vectors[7],
    )


def solution(mesh):
    rows = P(None, ("dp", "fsdp"), None, None)
    vector = P("fsdp")
    matrix = P("fsdp", None)
    weights = (vector, vector, matrix, vector, vector, matrix, vector, vector, vector, matrix, vector, matrix, vector)
    return jax.shard_map(
        functools.partial(shards, mesh.shape["dp"]),
        mesh=mesh,
        in_specs=(rows, rows, P(None, ("dp", "fsdp"), None)) + weights,
        out_specs=(rows, rows) + weights,
        check_vma=False,
    )
```

```python
import functools

import jax
import jax.numpy as jnp
from jax import lax
from jax.experimental import pallas as pl
from jax.experimental.pallas import tpu as pltpu
from jax.sharding import PartitionSpec as P

HEADS = 8
SEG = 16
RIGHT = 4
LEFT = 30
MEMS = 4
QB = 128
WIN = 176
SLOTS = 16
KEYS = WIN + SLOTS
TILE = 512
EXTRA = 16
BF = jnp.bfloat16
F32 = jnp.float32
HBM = pl.BlockSpec(memory_space=pl.ANY)
VMEM = pl.BlockSpec(memory_space=pltpu.VMEM)
LIMIT = 16 * 2**20


def nn(a, b):
    return lax.dot_general(a, b, (((1,), (0,)), ((), ())), preferred_element_type=F32)


def nt(a, b):
    return lax.dot_general(a, b, (((1,), (1,)), ((), ())), preferred_element_type=F32)


def tn(a, b):
    return lax.dot_general(a, b, (((0,), (0,)), ((), ())), preferred_element_type=F32)


def params(limit=LIMIT):
    return pltpu.CompilerParams(vmem_limit_bytes=limit)


def cost(micros):
    return pl.CostEstimate(flops=int(micros * 0.1e9), bytes_accessed=0, transcendentals=0)


def window(block, length):
    first = min(max(block * QB - 32, 0), length - WIN)
    slot = min(max(block * QB // SEG - MEMS, 0), length // SEG - SLOTS)
    return first, slot


def start_copies(copies):
    for copy in copies:
        copy.start()


def wait_copies(copies):
    for copy in copies:
        copy.wait()


def full(shape, dtype):
    return jax.ShapeDtypeStruct(shape, dtype)


def assemble(plan, parts, segments, sem):
    me = lax.axis_index("fsdp")
    copies = []
    for number, (offset, relative, first, rows, count) in enumerate(plan):
        for each in range(count):
            device = jnp.bitwise_xor(me, offset) if relative else each
            for start, height, target, column in segments:
                low, high = max(first, start), min(first + rows, start + height)
                if low < high:
                    place = pl.multiple_of(device * height, height) + low - start
                    source = parts[number].at[pl.ds(each * rows + low - first, high - low), :]
                    wide = source.shape[1]
                    copies.append(
                        pltpu.make_async_copy(
                            source, target.at[pl.ds(place, high - low), pl.ds(column, wide)], sem
                        )
                    )
    return copies


def pieces_into(grads):
    if len(grads.shape) == 2:

        def put_whole(rows, columns, value, device, within):
            grads[rows, columns] = value

        return put_whole
    me = lax.axis_index("fsdp")
    chips = [jnp.bitwise_xor(me // 2, chip) for chip in range(4)]
    cores = [jnp.bitwise_xor(lax.rem(me, 2), core) for core in range(2)]

    def put(rows, columns, value, device, within):
        grads[cores[device % 2], chips[device // 2], within[0], within[1]] = value

    return put


def put_rows(put, value, width, columns):
    for device in range(value.shape[0] // width):
        rows = slice(device * width, (device + 1) * width)
        put(rows, columns, value[rows], device, (slice(0, width), columns))


def stats(value):
    mean = jnp.mean(value, axis=-1, keepdims=True)
    offset = value - mean
    spread = jnp.mean(offset * offset, axis=-1, keepdims=True)
    scale = lax.rsqrt(spread + 1e-05)
    return offset * scale, scale


def averages(length):
    blocks = length // QB
    rows = blocks * SLOTS
    row = lax.broadcasted_iota(jnp.int32, (rows, length), 0)
    seg = lax.broadcasted_iota(jnp.int32, (rows, length), 1) // SEG
    slot = row % SLOTS
    for block in range(blocks):
        first = window(block, length)[1]
        slot = slot + jnp.where(row // SLOTS == block, first, 0)
    return jnp.where(slot == seg, 1.0 / SEG, 0.0).astype(BF)


def head_pair(value):
    lane = lax.broadcasted_iota(jnp.int32, value.shape, 1)
    zero = jnp.zeros_like(value)
    half = value.shape[1] // 2
    return jnp.concatenate(
        [jnp.where(lane < half, value, zero), jnp.where(lane >= half, value, zero)], axis=0
    )


def diagonal(value):
    half = value.shape[0] // 2
    return jnp.concatenate([value[:half, :QB], value[half:, QB:]], axis=0)


def visible_bias(bias_ref, utter_ref, row, nsegs):
    length = nsegs * SEG
    key = lax.broadcasted_iota(jnp.int32, (KEYS, QB), 0)
    query = lax.broadcasted_iota(jnp.int32, (KEYS, QB), 1)
    segs = QB // SEG
    starts = [jnp.int32(0)]
    for seg in range(1, nsegs):
        same = utter_ref[row, seg] == utter_ref[row, seg - 1]
        starts.append(jnp.where(same, starts[-1], seg))
    for block in range(length // QB):
        first, slot = window(block, length)
        lower = jnp.zeros((KEYS, QB), jnp.int32)
        upper = jnp.zeros((KEYS, QB), jnp.int32)
        for part in range(segs):
            seg = block * segs + part
            more = jnp.int32(0)
            if seg + 1 < nsegs:
                more = jnp.where(utter_ref[row, seg + 1] == utter_ref[row, seg], RIGHT, 0)
            frame_low = jnp.maximum(seg * SEG - LEFT, starts[seg] * SEG) - first
            frame_high = seg * SEG + SEG + more - first
            slot_low = jnp.maximum(seg - MEMS, starts[seg]) - slot + WIN
            slot_high = jnp.int32(seg - slot + WIN)
            here = query // SEG == part
            lower = jnp.where(here, jnp.where(key < WIN, frame_low, slot_low), lower)
            upper = jnp.where(here, jnp.where(key < WIN, frame_high, slot_high), upper)
        seen = (key >= lower) & (key < upper)
        bias_ref[block] = jnp.where(seen, 0.0, -1e9)


def call(body, name, micros, ins, outs, scratch, args, limit=LIMIT):
    kinds = [HBM if by_copy else VMEM for _, by_copy in outs]
    return pl.pallas_call(
        body,
        in_specs=[VMEM] * ins + [HBM] * (len(args) - ins),
        out_specs=kinds,
        out_shape=[shape for shape, _ in outs],
        scratch_shapes=scratch,
        compiler_params=params(limit),
        name=name,
        cost_estimate=cost(micros),
    )(*args)


def attention(q_ref, k_ref, v_ref, p_ref, bias, att_ref, att, length):
    for block in range(length // QB):
        first, _ = window(block, length)
        rows = slice(block * QB, (block + 1) * QB)
        own = slice(length + block * SLOTS, length + (block + 1) * SLOTS)
        for pair in range(HEADS // 2):
            lanes = slice(pair * 128, (pair + 1) * 128)
            keys = jnp.concatenate([k_ref[first : first + WIN, lanes], k_ref[own, lanes]], axis=0)
            vals = jnp.concatenate([v_ref[first : first + WIN, lanes], v_ref[own, lanes]], axis=0)
            seen = bias[block]
            scores = nt(keys, head_pair(q_ref[rows, lanes]))
            scores = scores + jnp.concatenate([seen, seen], axis=1)
            top = jnp.max(scores, axis=0, keepdims=True)
            raised = jnp.exp(scores - top)
            probs = (raised * (1.0 / jnp.sum(raised, axis=0, keepdims=True))).astype(BF)
            p_ref[block, pair] = probs
            found = diagonal(tn(vals, probs))
            att_ref[lanes, rows] = found.astype(BF)
            att[rows, lanes] = found.T.astype(BF)


def early_body(utter, x, dy, units, biases, dyt):
    rows, length, _ = x.shape
    for row in range(rows):
        units[row] = stats(x[row].astype(F32))[0]
        visible_bias(biases.at[row], utter, row, length // SEG)
    dyt[...] = dy[...].T


def early(utter, x, dy):
    rows, length, model = x.shape
    return pl.pallas_call(
        early_body,
        in_specs=[pl.BlockSpec(memory_space=pltpu.SMEM), VMEM, VMEM],
        out_specs=[VMEM] * 3,
        out_shape=[
            full((rows, length, model), F32),
            full((rows, length // QB, KEYS, QB), F32),
            full((model, rows * length), BF),
        ],
        compiler_params=params(),
        name="early",
        cost_estimate=cost(2),
    )(utter, x, dy)


def front_body(row, first_call, plan, width, x, units, biases, vecs_in, w_in_in, w_out_in, *refs):
    nparts = len(plan) if first_call else 0
    parts = refs[:nparts]
    outs = refs[nparts:]
    if first_call:
        vecs, w_in, w_out, *outs = outs
    else:
        vecs, w_in, w_out = vecs_in, w_in_in, w_out_in
    (q_out, k_out, v_out, wide_out, p_out, att_out, resid_out, n2_out, att, *outs) = outs
    length, model = x.shape[1], x.shape[2]
    value = x[row].astype(F32)
    if first_call:
        small, sem = outs
        segments = [(band * width, width, w_in, band * model) for band in range(3)]
        segments += [(3 * width, width, w_out, 0), (4 * width, EXTRA, small, 0)]
        copies = assemble(plan, parts, segments, sem)
        start_copies(copies)
    unit = units[row]
    if first_call:
        wait_copies(copies)
        total = jnp.zeros((8, model), F32)
        ups = [jnp.zeros((1, model), F32) for _ in range(4)]
        for piece in range(model // width):
            found = small[piece * EXTRA : (piece + 1) * EXTRA].astype(F32)
            total = total + pltpu.roll(found, piece * width, 1)[:8]
            for part in range(4):
                place = (piece * 4 + part) * width
                ups[place // model] += pltpu.roll(found, place % model, 1)[8 + part : 9 + part]
        vecs[0:8] = total
        for part in range(4):
            vecs[8 + part : 9 + part] = ups[part]
        vecs[12:16] = jnp.zeros((4, model), F32)
    normed = (unit * vecs[0:1] + vecs[1:2]).astype(BF)
    summary = nn(averages(length), normed).astype(BF)
    wide = jnp.concatenate([normed, summary], axis=0)
    wide_out[...] = wide.T
    q_out[...] = ((nn(normed, w_in[:, :model]) + vecs[2:3]).astype(BF).astype(F32) * 0.125).astype(BF)
    k_out[...] = nn(wide, w_in[:, model : 2 * model]).astype(BF)
    v_out[...] = (nn(wide, w_in[:, 2 * model :]) + vecs[3:4]).astype(BF)
    attention(q_out, k_out, v_out, p_out, biases.at[row], att_out, att, length)
    resid = value + nn(att[...], w_out[...]) + vecs[4:5]
    resid_out[...] = resid
    unit, _ = stats(resid)
    n2_out[...] = (unit * vecs[5:6] + vecs[6:7]).astype(BF)


def front(row, x, units, biases, vecs, w_in, w_out, plan, parts, width):
    _, length, model = x.shape
    blocks = length // QB
    wide = length + blocks * SLOTS
    first_call = vecs is None
    outs = [
        full((length, model), BF),
        full((wide, model), BF),
        full((wide, model), BF),
        full((model, wide), BF),
        full((blocks, HEADS // 2, KEYS, 2 * QB), BF),
        full((model, length), BF),
        full((length, model), F32),
        full((length, model), BF),
    ]
    scratch = [pltpu.VMEM((length, model), BF)]
    if first_call:
        outs = [full((16, model), F32), full((model, 3 * model), BF), full((model, model), BF)] + outs
        pieces = model // width
        scratch += [pltpu.VMEM((pieces * EXTRA, model), BF), pltpu.SemaphoreType.DMA]
        args = [x, units, biases] + list(parts)
        specs = [VMEM] * 3 + [HBM] * len(parts)

        def body(x, units, biases, *refs):
            front_body(row, True, plan, width, x, units, biases, None, None, None, *refs)
    else:
        args = [x, units, biases, vecs, w_in, w_out]
        specs = [VMEM] * 6
        body = functools.partial(front_body, row, False, plan, width)
    return pl.pallas_call(
        body,
        in_specs=specs,
        out_specs=[VMEM] * len(outs),
        out_shape=outs,
        scratch_shapes=scratch,
        compiler_params=params(),
        name=f"front{row}",
        cost_estimate=cost(7),
    )(*args)


def gelu_both(v):
    c = 0.7978845608028654
    square = v * v
    bent = jnp.tanh(c * v * (1.0 + 0.044715 * square))
    half = 0.5 + 0.5 * bent
    slope = half + 0.5 * v * (1.0 - bent * bent) * (c * (1.0 + 3 * 0.044715 * square))
    return v * half, slope


def middle_body(rows, plan, width, *refs):
    n2s = refs[:rows]
    dyt, vecs, *refs = refs[rows:]
    parts = refs[: len(plan)]
    hidden, slopes, up, grads, sem = refs[len(plan) :]
    put = pieces_into(grads)
    model, tokens = dyt.shape
    ff = up.shape[1]
    tall = ff * width // model
    copies = assemble(plan, parts, [(0, width, up, 0)], sem)
    start_copies(copies)
    wait_copies(copies)
    length = n2s[0].shape[0]
    step = length
    for tile in range(ff // TILE):
        cols = slice(tile * TILE, (tile + 1) * TILE)
        for chunk in range(tokens // step):
            rows = slice(chunk * step, (chunk + 1) * step)
            at = chunk * step % length
            u = nn(n2s[chunk * step // length][at : at + step], up[:, cols]) + vecs[8 + tile : 9 + tile]
            value, slope = gelu_both(u)
            hidden[rows, cols] = value.astype(BF)
            slopes[rows, cols] = slope.astype(BF)
        grad = nn(dyt[...], hidden[:, cols]).astype(BF)
        for part in range(TILE // tall):
            inner_cols = slice(part * tall, (part + 1) * tall)
            outer_cols = slice(tile * TILE + part * tall, tile * TILE + (part + 1) * tall)
            device = tile * TILE // tall + part
            rows = slice(0, model)
            put(rows, outer_cols, grad[:, inner_cols], device, (rows, slice(0, tall)))


def middle(n2s, dyt, vecs, parts, plan, width, ff, fast):
    model, tokens = dyt.shape
    tall = ff * width // model
    shape = (2, 4, model, tall) if fast else (model, ff)
    outs = [
        (full((tokens, ff), BF), False),
        (full((tokens, ff), BF), False),
        (full((model, ff), BF), False),
        (full(shape, BF), False),
    ]
    scratch = [pltpu.SemaphoreType.DMA]
    body = functools.partial(middle_body, len(n2s), plan, width)
    return call(body, "middle", 8, len(n2s) + 2, outs, scratch, [*n2s, dyt, vecs, *parts])


def turn_body(plan, dy, slopes, *refs):
    parts = refs[: len(plan)]
    du, ub, down, sem = refs[len(plan) :]
    tokens, model = dy.shape
    ff = down.shape[0]
    tall = plan[0][3]
    length = dy.shape[0] // 2
    copies = assemble(plan, parts, [(0, tall, down, 0)], sem)
    start_copies(copies)
    wait_copies(copies)
    step = length
    for tile in range(ff // TILE):
        cols = slice(tile * TILE, (tile + 1) * TILE)
        sums = jnp.zeros((1, TILE), F32)
        for chunk in range(tokens // step):
            rows = slice(chunk * step, (chunk + 1) * step)
            back = nt(dy[rows], down[cols]).astype(BF).astype(F32) * slopes[rows, cols].astype(F32)
            du[rows, cols] = back.astype(BF)
            sums = sums + jnp.sum(back, axis=0, keepdims=True)
        ub[tile : tile + 1] = sums


def turn(dy, slopes, parts, plan):
    tokens, model = dy.shape
    ff = slopes.shape[1]
    outs = [
        (full((tokens, ff), BF), False),
        (full((ff // TILE, TILE), F32), False),
        (full((ff, model), BF), False),
    ]
    args = [dy, slopes, *parts]
    return call(functools.partial(turn_body, plan), "turn", 5, 2, outs, [pltpu.SemaphoreType.DMA], args)


def rise_body(rows, width, *refs):
    n2s = refs[:rows]
    du, grads, n2t = refs[rows:]
    length, model = n2s[0].shape
    ff = du.shape[1]
    put = pieces_into(grads)
    for row in range(rows):
        n2t[:, row * length : (row + 1) * length] = n2s[row][...].T
    for tile in range(ff // TILE):
        cols = slice(tile * TILE, (tile + 1) * TILE)
        put_rows(put, nn(n2t[...], du[:, cols]).astype(BF), width, cols)


def rise(n2s, du, width, fast):
    tokens, ff = du.shape
    model = n2s[0].shape[1]
    shape = (2, 4, width, ff) if fast else (model, ff)
    scratch = [pltpu.VMEM((model, tokens), BF)]
    body = functools.partial(rise_body, len(n2s), width)
    args = [*n2s, du]
    return call(body, "rise", 4, len(args), [(full(shape, BF), False)], scratch, args)[0]


def norm_back(grad, unit, scale):
    first = jnp.mean(grad, axis=-1, keepdims=True)
    second = jnp.mean(grad * unit, axis=-1, keepdims=True)
    return scale * (grad - first - unit * second)


def back_body(rows, *refs):
    resids = refs[:rows]
    du, dy, vecs, up, w_out, dresid, datt, sums = refs[rows:]
    tokens, model = dy.shape
    length = resids[0].shape[0]
    step = length
    gains = jnp.zeros((1, model), F32)
    shifts = jnp.zeros((1, model), F32)
    biases = jnp.zeros((1, model), F32)
    downs = jnp.zeros((1, model), F32)
    for chunk in range(tokens // step):
        rows = slice(chunk * step, (chunk + 1) * step)
        at = chunk * step % length
        grad = nt(du[rows], up[...])
        unit, scale = stats(resids[chunk * step // length][at : at + step])
        gains = gains + jnp.sum(grad * unit, axis=0, keepdims=True)
        shifts = shifts + jnp.sum(grad, axis=0, keepdims=True)
        top = dy[rows].astype(F32)
        downs = downs + jnp.sum(top, axis=0, keepdims=True)
        total = top + norm_back(grad * vecs[5:6], unit, scale)
        biases = biases + jnp.sum(total, axis=0, keepdims=True)
        dresid[rows] = total
        datt[rows] = nt(total.astype(BF), w_out[...]).astype(BF)
    sums[0:1] = gains
    sums[1:2] = shifts
    sums[2:3] = biases
    sums[3:4] = downs


def back(resids, du, dy, vecs, up, w_out):
    tokens, model = dy.shape
    outs = [
        (full((tokens, model), F32), False),
        (full((tokens, model), BF), False),
        (full((4, model), F32), False),
    ]
    args = [*resids, du, dy, vecs, up, w_out]
    return call(functools.partial(back_body, len(resids)), "back", 8, len(args), outs, [], args)


def rear_body(row, q, k, v, p, datt, mixed, sums, dk, dv):
    length, model = q.shape
    extent = k.shape[0]
    base = row * length
    dk[...] = jnp.zeros_like(dk)
    dv[...] = jnp.zeros_like(dv)
    mixed[length:extent, 0:model] = jnp.zeros((extent - length, model), BF)
    for block in range(length // QB):
        first, _ = window(block, length)
        rows = slice(block * QB, (block + 1) * QB)
        own = slice(length + block * SLOTS, length + (block + 1) * SLOTS)
        span = slice(first, first + WIN)
        for pair in range(HEADS // 2):
            lanes = slice(pair * 128, (pair + 1) * 128)
            keys = jnp.concatenate([k[span, lanes], k[own, lanes]], axis=0)
            vals = jnp.concatenate([v[span, lanes], v[own, lanes]], axis=0)
            queries = head_pair(q[rows, lanes])
            tops = head_pair(datt[base + block * QB : base + (block + 1) * QB, lanes])
            probs = p[block, pair]
            wides = probs.astype(F32)
            back = nt(vals, tops)
            inner = jnp.sum(wides * back, axis=0, keepdims=True)
            dscores = (wides * (back - inner)).astype(BF)
            gv = nn(probs, tops)
            gk = nn(dscores, queries)
            dv[span, lanes] += gv[:WIN]
            dv[own, lanes] = gv[WIN:]
            dk[span, lanes] += gk[:WIN]
            dk[own, lanes] = gk[WIN:]
            gq = diagonal(tn(keys, dscores)).T * 0.125
            mixed[rows, lanes] = gq.astype(BF)
    mixed[:, model : 2 * model] = dk[...].astype(BF)
    mixed[:, 2 * model :] = dv[...].astype(BF)
    sums[0:1] = jnp.sum(mixed[:, 0:model].astype(F32), axis=0, keepdims=True)
    sums[1:2] = jnp.sum(mixed[:, 2 * model :].astype(F32), axis=0, keepdims=True)


def rear(row, q, k, v, p, datt):
    length, model = q.shape
    extent = k.shape[0]
    outs = [(full((extent, 3 * model), BF), False), (full((2, model), F32), False)]
    scratch = [pltpu.VMEM((extent, model), F32), pltpu.VMEM((extent, model), F32)]
    body = functools.partial(rear_body, row)
    return call(body, f"rear{row}", 7, 5, outs, scratch, [q, k, v, p, datt])


def base_body(rows, width, x, dresid, vecs, w_in, gub, back_sums, *refs):
    mixeds = refs[:rows]
    rear_sums = refs[rows : 2 * rows]
    wides = refs[2 * rows : 3 * rows]
    atts = refs[3 * rows : 4 * rows]
    grads, dx, sums = refs[4 * rows :]
    length, model = x.shape[1], x.shape[2]
    put = pieces_into(grads)
    for tile in range(3):
        cols = slice(tile * model, (tile + 1) * model)
        total = nn(wides[0][...], mixeds[0][:, cols])
        for row in range(1, rows):
            total = total + nn(wides[row][...], mixeds[row][:, cols])
        put_rows(put, total.astype(BF), width, cols)
    total = nn(atts[0][...], dresid[0:length].astype(BF))
    for row in range(1, rows):
        total = total + nn(atts[row][...], dresid[row * length : (row + 1) * length].astype(BF))
    put_rows(put, total.astype(BF), width, slice(3 * model, 4 * model))
    average = averages(length)
    gains = jnp.zeros((1, model), F32)
    shifts = jnp.zeros((1, model), F32)
    for row in range(rows):
        unit, scale = stats(x[row].astype(F32))
        grad = nt(mixeds[row][...], w_in[...])
        grad = grad[:length] + tn(average, grad[length:].astype(BF))
        gains = gains + jnp.sum(grad * unit, axis=0, keepdims=True)
        shifts = shifts + jnp.sum(grad, axis=0, keepdims=True)
        dx[row] = dresid[row * length : (row + 1) * length] + norm_back(grad * vecs[0:1], unit, scale)
    sums[0:1] = gains
    sums[1:2] = shifts
    sums[2:4] = wide_sum(*[part[...] for part in rear_sums])
    sums[4:8] = back_sums[...]
    sums[8:12] = gub[...]
    sums[12:16] = jnp.zeros((4, model), F32)
    if len(grads.shape) == 4:
        for device in range(model // width):
            block = [sums[0:8, device * width : (device + 1) * width]]
            for part in range(4):
                place = (device * 4 + part) * width
                row, low = 8 + place // model, place % model
                block.append(sums[row : row + 1, low : low + width])
            block.append(jnp.zeros((4, width), F32))
            block = jnp.concatenate(block, axis=0)
            block = jnp.concatenate([block, jnp.zeros((16, 128 - width), F32)], axis=1)
            put(None, None, block.astype(BF), device, (slice(0, 16), slice(4 * model, 4 * model + 128)))
            put(
                None,
                None,
                jnp.zeros((width - 16, 128), BF),
                device,
                (slice(16, width), slice(4 * model, 4 * model + 128)),
            )


def base(x, dresid, vecs, w_in, gub, back_sums, mixeds, rear_sums, wides, atts, width, fast):
    rows, length, model = x.shape
    shape = (2, 4, width, 4 * model + 128) if fast else (model, 4 * model)
    outs = [
        (full(shape, BF), False),
        (full((rows, length, model), F32), False),
        (full((16, model), F32), False),
    ]
    args = [x, dresid, vecs, w_in, gub, back_sums, *mixeds, *rear_sums, *wides, *atts]
    return call(functools.partial(base_body, rows, width), "base", 6, len(args), outs, [], args)


def finish_body(rows, vecs, hidden, down, *refs):
    resids = refs[:rows]
    out = refs[rows]
    length = resids[0].shape[0]
    step = length
    for chunk in range(hidden.shape[0] // step):
        rows = slice(chunk * step, (chunk + 1) * step)
        at = chunk * step % length
        resid = resids[chunk * step // length][at : at + step]
        out[rows] = (resid + nn(hidden[rows], down[...]) + vecs[7:8]).astype(BF)


def finish(vecs, hidden, down, resids):
    outs = [(full((hidden.shape[0], down.shape[1]), BF), False)]
    args = [vecs, hidden, down, *resids]
    return call(functools.partial(finish_body, len(resids)), "finish", 4, len(args), outs, [], args)[0]


def along(value, offset):
    return lax.ppermute(value, "fsdp", [(i, i ^ offset) for i in range(8)])


def across(value, offset, size):
    return lax.ppermute(value, "dp", [(i, i ^ offset) for i in range(size)])


def pack_body(*refs):
    sources, out = refs[:11], refs[11]
    w_in, w_out, *rows, sem = refs[12:]
    width, model = w_out.shape
    targets = [w_in, w_out, *rows]
    copies = [pltpu.make_async_copy(a, b, sem) for a, b in zip(sources, targets)]
    start_copies(copies)
    out[4 * width :] = jnp.zeros((EXTRA, model), BF)
    wait_copies(copies)
    for band in range(3):
        out[band * width : (band + 1) * width] = w_in[:, band * model : (band + 1) * model]
    out[3 * width : 4 * width] = w_out[...]
    lines = [row[...].astype(F32).reshape(1, width) for row in rows[:8]]
    bias = rows[8][...].astype(F32).reshape(1, 4 * width)
    lines += [bias[:, at * width : (at + 1) * width] for at in range(4)]
    lines += [jnp.zeros((4, width), F32)]
    out[4 * width :, 0:width] = jnp.concatenate(lines, axis=0).astype(BF)


def pack(project_in, project_out, vectors, up_bias):
    width, model = project_out.shape
    outs = [(full((4 * width + EXTRA, model), BF), False)]
    args = [project_in, project_out, *vectors, up_bias]
    scratch = [pltpu.VMEM(arg.shape, BF) for arg in args] + [pltpu.SemaphoreType.DMA]
    return call(pack_body, "pack", 2, 0, outs, scratch, args, 60 * 2**20)[0]


def settle_body(width, tall, small, *refs):
    me = lax.axis_index("fsdp")
    value = small[...]
    model = value.shape[1]
    turned = pltpu.roll(value, lax.rem(model - me * width, model), 1)
    for row, out in enumerate(refs[:8]):
        out[...] = turned[row : row + 1, 0:width].reshape(width)
    place = me * tall
    wide = jnp.zeros((1, model), F32)
    for row in range(4):
        wide = jnp.where(place // model == row, value[8 + row : 9 + row], wide)
    wide = jnp.concatenate([wide] * 8, axis=0)
    turned = pltpu.roll(wide, lax.rem(model - lax.rem(place, model), model), 1)
    refs[8][...] = turned[0:1, 0:tall].reshape(tall)


def settle(small, width, tall):
    outs = [(full((width,), F32), False)] * 8 + [(full((tall,), F32), False)]
    return call(functools.partial(settle_body, width, tall), "settle", 2, 1, outs, [], [small])


def wide_sum(*values):
    total = values[0].astype(F32)
    for value in values[1:]:
        total = total + value.astype(F32)
    return total


def plus(*values):
    def body(*refs):
        refs[-1][...] = wide_sum(*[ref[...] for ref in refs[:-1]]).astype(refs[-1].dtype)

    outs = [(full(values[0].shape, values[0].dtype), False)]
    return call(body, "plus", 1, len(values), outs, [], values)[0]


def plus_here(both, there):
    def body(both, there, out):
        out[...] = wide_sum(both[0], there[...]).astype(BF)

    return call(body, "plus", 1, 2, [(full(there.shape, BF), False)], [], [both, there])[0]


def own_sum(held, *others):
    return wide_sum(held[0], *[other[...] for other in others]).astype(BF)


def cross_halves(held):
    def body(held, to_x, to_y):
        half = held.shape[1] // 2
        to_x[0] = held[1, :half]
        to_x[1] = held[3, :half]
        to_y[0] = held[2, half:]
        to_y[1] = held[3, half:]

    _, rows, columns = held.shape
    outs = [(full((2, rows // 2, columns), BF), False)] * 2
    return call(body, "cross_halves", 1, 1, outs, [], [held])


def second(held, from_x, from_y):
    def body(held, from_x, from_y, to_x, to_y):
        half = held.shape[1] // 2
        to_x[...] = wide_sum(held[1, half:], from_y[1]).astype(BF)
        to_y[...] = wide_sum(held[2, :half], from_x[1]).astype(BF)

    outs = [(full(from_x.shape[1:], BF), False)] * 2
    return call(body, "second", 1, 3, outs, [], [held, from_x, from_y])


def hop_halves(*args):
    def body(held, from_x, from_y, last_x, last_y, keep, send):
        half = keep.shape[0]
        top = wide_sum(held[0, :half], from_x[0], last_y[...]).astype(BF)
        bottom = wide_sum(held[0, half:], from_y[0], last_x[...]).astype(BF)
        odd = odd_plane()

        @pl.when(odd)
        def _():
            keep[...] = bottom
            send[...] = top

        @pl.when(jnp.logical_not(odd))
        def _():
            keep[...] = top
            send[...] = bottom

    _, rows, columns = args[0].shape
    outs = [(full((rows // 2, columns), BF), False)] * 2
    return call(body, "hop_halves", 1, 5, outs, [], args)


def odd_plane():
    return lax.rem(lax.axis_index("dp"), 2) == 1


def by_halves(*args):
    def body(*refs):
        keep, send = refs[-2:]
        total = own_sum(*refs[:-2])
        half = keep.shape[0]
        odd = odd_plane()

        @pl.when(odd)
        def _():
            keep[...] = total[half:]
            send[...] = total[:half]

        @pl.when(jnp.logical_not(odd))
        def _():
            keep[...] = total[:half]
            send[...] = total[half:]

    rows, columns = args[1].shape
    outs = [(full((rows // 2, columns), BF), False)] * 2
    return call(body, "by_halves", 1, len(args), outs, [], args)


def by_quarters(*args):
    def body(*refs):
        outs = refs[-5:-1]
        whole = refs[-1]
        whole[...] = own_sum(*refs[:-5])
        rows = outs[0].shape[0]
        me = lax.axis_index("dp")
        for offset, out in enumerate(outs):
            place = pl.multiple_of(jnp.bitwise_xor(me, offset) * rows, rows)
            out[...] = whole[pl.ds(place, rows), :]

    rows, columns = args[1].shape
    outs = [(full((rows // 4, columns), BF), False)] * 4
    scratch = [pltpu.VMEM((rows, columns), BF)]
    return call(body, "by_quarters", 1, len(args), outs, scratch, args)


def last_down(keep, other):
    def body(keep, other, out):
        half = keep.shape[0]
        odd = odd_plane()

        @pl.when(odd)
        def _():
            out[:, :half] = other[...].astype(F32).T
            out[:, half:] = keep[...].astype(F32).T

        @pl.when(jnp.logical_not(odd))
        def _():
            out[:, :half] = keep[...].astype(F32).T
            out[:, half:] = other[...].astype(F32).T

    half, tall = keep.shape
    return call(body, "last_down", 1, 2, [(full((tall, 2 * half), F32), False)], [], [keep, other])[0]


def last_up(keep, other):
    def body(keep, other, out):
        half = keep.shape[0]
        odd = odd_plane()

        @pl.when(odd)
        def _():
            out[:half] = other[...].astype(F32)
            out[half:] = keep[...].astype(F32)

        @pl.when(jnp.logical_not(odd))
        def _():
            out[:half] = keep[...].astype(F32)
            out[half:] = other[...].astype(F32)

    half, ff = keep.shape
    return call(body, "last_up", 1, 2, [(full((2 * half, ff), F32), False)], [], [keep, other])[0]


def last_in(quarters, model, width, tall):
    def body(*refs):
        parts, g_in, g_out, small = refs[:4], refs[4], refs[5], refs[15]
        vectors = refs[6:15]
        rows = parts[0].shape[0]
        me = lax.axis_index("dp")
        for offset, part in enumerate(parts):
            place = pl.multiple_of(jnp.bitwise_xor(me, offset) * rows, rows)
            g_in[pl.ds(place, rows), :] = part[:, : 3 * model].astype(F32)
            g_out[pl.ds(place, rows), :] = part[:, 3 * model : 4 * model].astype(F32)
            small[pl.ds(place, rows), :] = part[:, 4 * model :].astype(F32)
        for row in range(8):
            vectors[row][...] = small[row : row + 1, 0:width].reshape(width)
        wide = jnp.concatenate([small[8 + part : 9 + part, 0:width] for part in range(4)], axis=1)
        vectors[8][...] = wide.reshape(tall)

    outs = [(full((width, 3 * model), F32), False), (full((width, model), F32), False)]
    outs += [(full((width,), F32), False)] * 8 + [(full((tall,), F32), False)]
    scratch = [pltpu.VMEM((width, 128), F32)]
    return call(body, "last_in", 1, 4, outs, scratch, quarters)


def after(value, *others):
    return lax.optimization_barrier((value,) + others)[0]


def whole_plan(rows, size):
    return [(0, False, 0, rows, size)]


def near_plan(rows):
    return [(offset, True, 0, rows, 1) for offset in (0, 1, 2, 4, 6, 3, 5, 7)]


def shards(
    group,
    frames,
    upstream,
    utterance,
    first_gain,
    first_shift,
    project_in,
    query_bias,
    value_bias,
    project_out,
    out_bias,
    second_gain,
    second_shift,
    up_weight,
    up_bias,
    down_weight,
    down_bias,
):
    micro, nrows, length, model = frames.shape
    rows = micro * nrows
    width = project_out.shape[0]
    size = model // width
    ff = up_weight.shape[1]
    tall = ff // size
    x = frames.reshape(rows, length, model)
    dy = upstream.reshape(rows * length, model)
    utter = utterance.reshape(rows, length // SEG)
    vectors = (first_gain, first_shift, query_bias, value_bias, out_bias, second_gain, second_shift, down_bias)
    fast = size == 8 and group == 4 and rows == 2
    packed = pack(project_in, project_out, vectors, up_bias)
    if fast:
        plan_a, plan_u, plan_d = near_plan(packed.shape[0]), near_plan(width), near_plan(tall)
        a2, a4, a6, a1 = [along(packed, offset) for offset in (2, 4, 6, 1)]
        units, biases, dyt = early(after(utter, a1), x, dy)
        a2, a4, a6, dyt = lax.optimization_barrier((a2, a4, a6, dyt))
        up_piece = after(up_weight, a2, a4, a6)
        u2, u4, u1 = along(up_piece, 2), along(up_piece, 4), along(up_piece, 1)
        parts_a = [packed, a1, a2, a4, a6, along(a2, 1), along(a4, 1)] + [along(a6, 1)]
        u6 = along(up_piece, 6)
        first = x
    else:
        plan_a, plan_u, plan_d = whole_plan(packed.shape[0], size), whole_plan(width, size), whole_plan(tall, size)
        parts_a = [lax.all_gather(packed, "fsdp", axis=0, tiled=True)]
        parts_u = [lax.all_gather(up_weight, "fsdp", axis=0, tiled=True)]
        parts_d = [lax.all_gather(down_weight, "fsdp", axis=0, tiled=True)]
        first = x
        units, biases, dyt = early(utter, x, dy)
    saved = []
    vecs, w_in, w_out, *first = front(0, first, units, biases, None, None, None, plan_a, parts_a, width)
    saved.append(first)
    held = vecs
    if fast:
        held = vecs
    for row in range(1, rows):
        saved.append(front(row, x, units, biases, held, w_in, w_out, plan_a, None, width))
    qs, ks, vs, wides, ps, atts, resids, n2s = zip(*saved)
    if fast:
        down_piece = after(down_weight, n2s[0])
        d2, d4 = along(down_piece, 2), along(down_piece, 4)
        *u_got, done = lax.optimization_barrier((u2, u4, u6, n2s[1]))
        parts_u = [up_piece, u1, *u_got] + [along(part, 1) for part in u_got[:2]] + [along(u_got[2], 1)]
        d2, d4, down_piece, done = lax.optimization_barrier((d2, d4, down_piece, done))
        held = after(vecs, d2, d4)
        d3, d5, d6, d1 = along(d2, 1), along(d4, 1), along(down_piece, 6), along(down_piece, 1)
    hidden, slopes, up, gdown = middle(n2s, dyt, held, parts_u, plan_u, width, ff, fast)
    if fast:
        d6 = after(d6, slopes)
        parts_d = [down_piece, d1, d2, d4, d6, d3, d5, along(d6, 1)]
    if fast:
        du, gub, down = turn(dy, slopes, parts_d, plan_d)
        d_core = along(after(gdown, gub)[1], 1)
        gup = rise(n2s, du, width, fast)
        d_sum = plus_here(gdown, after(d_core, gup))
        to_x, to_y = cross_halves(d_sum)
        d_x, d_y = along(to_x, 2), along(to_y, 4)
        u_core = along(gup[1], 1)
        dresid, datt, sums2 = back(resids, after(du, to_x), dy, vecs, up, w_out)
        u_core, done = lax.optimization_barrier((u_core, sums2))
        u_sum = plus_here(gup, u_core)
        to_x, to_y = cross_halves(u_sum)
        u_x, u_y = along(to_x, 2), along(to_y, 4)
        mixed0, sums0 = rear(0, after(qs[0], to_x), ks[0], vs[0], ps[0], datt)
        d_x, d_y, done = lax.optimization_barrier((d_x, d_y, sums0))
        to_x, to_y = second(d_sum, d_x, d_y)
        d_x2, d_y2 = along(to_x, 2), along(to_y, 4)
        mixed1, sums1 = rear(1, after(qs[1], to_x), ks[1], vs[1], ps[1], datt)
        u_x, u_y, d_x2, d_y2, done = lax.optimization_barrier((u_x, u_y, d_x2, d_y2, sums1))
        to_x, to_y = second(u_sum, u_x, u_y)
        u_x2, u_y2 = along(to_x, 2), along(to_y, 4)
        d_keep, d_send = hop_halves(d_sum, d_x, d_y, d_x2, d_y2)
        d_z = across(d_send, 1, group)
        mixeds = (mixed0, mixed1)
        out = finish(after(vecs, sums1), hidden, down, resids)
        gin, dx, small = base(
            x,
            after(dresid, to_x, d_send, out),
            vecs,
            w_in,
            gub,
            sums2,
            mixeds,
            (sums0, sums1),
            wides,
            atts,
            width,
            fast,
        )
        u_x2, u_y2, d_z, done = lax.optimization_barrier((u_x2, u_y2, d_z, small))
        u_keep, u_send = hop_halves(u_sum, u_x, u_y, u_x2, u_y2)
        u_z = across(u_send, 1, group)
        d_keep = plus(d_keep, d_z)
        d_z2 = across(d_keep, 2, group)
        i_core = along(after(gin, u_send, d_keep)[1], 1)
        i_sum = plus_here(gin, i_core)
        i_got = [along(i_sum[1], 2), along(i_sum[2], 4), along(i_sum[3], 6)]
        u_z, d_z2, done = lax.optimization_barrier((u_z, d_z2, i_sum))
        u_keep = plus(u_keep, u_z)
        u_z2 = across(u_keep, 2, group)
        d_keep = plus(d_keep, d_z2)
        d_other = across(d_keep, 1, group)
        i_own, *i_send = by_quarters(i_sum, *i_got)
        i_got = [across(part, offset, group) for offset, part in zip((1, 2, 3), i_send)]
        u_keep = plus(u_keep, u_z2)
        u_other = across(u_keep, 1, group)
        i_own = plus(i_own, *i_got)
        i_got = [across(i_own, offset, group) for offset in (1, 2, 3)]
        gdown = last_down(after(d_keep, i_own), d_other)
        g_up = last_up(after(u_keep, i_own), u_other)
        g_in, g_out, *vectors = last_in([i_own, *i_got], model, width, tall)
    else:
        du, gub, down = turn(dy, slopes, parts_d, plan_d)
        dresid, datt, sums2 = back(resids, du, dy, vecs, up, w_out)
        gup = rise(n2s, du, width, fast)
        pairs = [rear(row, qs[row], ks[row], vs[row], ps[row], datt) for row in range(rows)]
        mixeds, rear_sums = zip(*pairs)
        gin, dx, small = base(
            x, dresid, vecs, w_in, gub, sums2, mixeds, rear_sums, wides, atts, width, fast
        )
        out = finish(vecs, hidden, down, resids)

        def total(value, dim):
            own = lax.psum_scatter(value, "fsdp", scatter_dimension=dim, tiled=True)
            return lax.psum(own, "dp").astype(F32)

        gdown = total(gdown, 1).T
        g_up = total(gup, 0)
        gin = total(gin, 0)
        g_in, g_out = gin[:, : 3 * model], gin[:, 3 * model :]
        vectors = settle(lax.psum(small, ("dp", "fsdp")), width, tall)
    return (
        out.reshape(frames.shape),
        dx.reshape(frames.shape),
        vectors[0],
        vectors[1],
        g_in,
        vectors[2],
        vectors[3],
        g_out,
        vectors[6],
        vectors[4],
        vectors[5],
        g_up,
        vectors[8],
        gdown,
        vectors[7],
    )


def solution(mesh):
    rows = P(None, ("dp", "fsdp"), None, None)
    vector = P("fsdp")
    matrix = P("fsdp", None)
    weights = (vector, vector, matrix, vector, vector, matrix, vector, vector, vector, matrix, vector, matrix, vector)
    return jax.shard_map(
        functools.partial(shards, mesh.shape["dp"]),
        mesh=mesh,
        in_specs=(rows, rows, P(None, ("dp", "fsdp"), None)) + weights,
        out_specs=(rows, rows) + weights,
        check_vma=False,
    )
```

```python
import functools

import jax
import jax.numpy as jnp
from jax import lax
from jax.experimental import pallas as pl
from jax.experimental.pallas import tpu as pltpu
from jax.sharding import PartitionSpec as P

HEADS = 8
SEG = 16
RIGHT = 4
LEFT = 30
MEMS = 4
QB = 128
WIN = 176
SLOTS = 16
KEYS = WIN + SLOTS
TILE = 512
EXTRA = 16
BF = jnp.bfloat16
F32 = jnp.float32
HBM = pl.BlockSpec(memory_space=pl.ANY)
VMEM = pl.BlockSpec(memory_space=pltpu.VMEM)
LIMIT = 16 * 2**20


def nn(a, b):
    return lax.dot_general(a, b, (((1,), (0,)), ((), ())), preferred_element_type=F32)


def nt(a, b):
    return lax.dot_general(a, b, (((1,), (1,)), ((), ())), preferred_element_type=F32)


def tn(a, b):
    return lax.dot_general(a, b, (((0,), (0,)), ((), ())), preferred_element_type=F32)


def params(limit=LIMIT):
    return pltpu.CompilerParams(vmem_limit_bytes=limit)


def cost(micros):
    return pl.CostEstimate(flops=int(micros * 0.1e9), bytes_accessed=0, transcendentals=0)


def window(block, length):
    first = min(max(block * QB - 32, 0), length - WIN)
    slot = min(max(block * QB // SEG - MEMS, 0), length // SEG - SLOTS)
    return first, slot


def full(shape, dtype):
    return jax.ShapeDtypeStruct(shape, dtype)


def assemble(plan, parts, segments):
    me = lax.axis_index("fsdp")
    for number, (offset, relative, first, rows, count) in enumerate(plan):
        for each in range(count):
            device = jnp.bitwise_xor(me, offset) if relative else each
            for start, height, target, column in segments:
                low, high = max(first, start), min(first + rows, start + height)
                if low < high:
                    place = pl.multiple_of(device * height, height) + low - start
                    at = each * rows + low - first
                    value = parts[number][at : at + high - low, :]
                    target[pl.ds(place, high - low), column : column + value.shape[1]] = value


def pieces_into(grads):
    if len(grads.shape) == 2:

        def put_whole(rows, columns, value, device, within):
            grads[rows, columns] = value

        return put_whole
    me = lax.axis_index("fsdp")
    chips = [jnp.bitwise_xor(me // 2, chip) for chip in range(4)]
    cores = [jnp.bitwise_xor(lax.rem(me, 2), core) for core in range(2)]

    def put(rows, columns, value, device, within):
        grads[cores[device % 2], chips[device // 2], within[0], within[1]] = value

    return put


def put_rows(put, value, width, columns):
    for device in range(value.shape[0] // width):
        rows = slice(device * width, (device + 1) * width)
        put(rows, columns, value[rows], device, (slice(0, width), columns))


def stats(value):
    mean = jnp.mean(value, axis=-1, keepdims=True)
    offset = value - mean
    spread = jnp.mean(offset * offset, axis=-1, keepdims=True)
    scale = lax.rsqrt(spread + 1e-05)
    return offset * scale, scale


def averages(length):
    blocks = length // QB
    rows = blocks * SLOTS
    row = lax.broadcasted_iota(jnp.int32, (rows, length), 0)
    seg = lax.broadcasted_iota(jnp.int32, (rows, length), 1) // SEG
    slot = row % SLOTS
    for block in range(blocks):
        first = window(block, length)[1]
        slot = slot + jnp.where(row // SLOTS == block, first, 0)
    return jnp.where(slot == seg, 1.0 / SEG, 0.0).astype(BF)


def head_pair(value):
    lane = lax.broadcasted_iota(jnp.int32, value.shape, 1)
    zero = jnp.zeros_like(value)
    half = value.shape[1] // 2
    return jnp.concatenate(
        [jnp.where(lane < half, value, zero), jnp.where(lane >= half, value, zero)], axis=0
    )


def diagonal(value):
    half = value.shape[0] // 2
    return jnp.concatenate([value[:half, :QB], value[half:, QB:]], axis=0)


def visible_bias(bias_ref, utter_ref, row, nsegs):
    length = nsegs * SEG
    key = lax.broadcasted_iota(jnp.int32, (KEYS, QB), 0)
    query = lax.broadcasted_iota(jnp.int32, (KEYS, QB), 1)
    segs = QB // SEG
    starts = [jnp.int32(0)]
    for seg in range(1, nsegs):
        same = utter_ref[row, seg] == utter_ref[row, seg - 1]
        starts.append(jnp.where(same, starts[-1], seg))
    for block in range(length // QB):
        first, slot = window(block, length)
        lower = jnp.zeros((KEYS, QB), jnp.int32)
        upper = jnp.zeros((KEYS, QB), jnp.int32)
        for part in range(segs):
            seg = block * segs + part
            more = jnp.int32(0)
            if seg + 1 < nsegs:
                more = jnp.where(utter_ref[row, seg + 1] == utter_ref[row, seg], RIGHT, 0)
            frame_low = jnp.maximum(seg * SEG - LEFT, starts[seg] * SEG) - first
            frame_high = seg * SEG + SEG + more - first
            slot_low = jnp.maximum(seg - MEMS, starts[seg]) - slot + WIN
            slot_high = jnp.int32(seg - slot + WIN)
            here = query // SEG == part
            lower = jnp.where(here, jnp.where(key < WIN, frame_low, slot_low), lower)
            upper = jnp.where(here, jnp.where(key < WIN, frame_high, slot_high), upper)
        seen = (key >= lower) & (key < upper)
        bias_ref[block] = jnp.where(seen, 0.0, -1e9)


def call(body, name, micros, ins, outs, scratch, args, limit=LIMIT):
    kinds = [HBM if by_copy else VMEM for _, by_copy in outs]
    return pl.pallas_call(
        body,
        in_specs=[VMEM] * ins + [HBM] * (len(args) - ins),
        out_specs=kinds,
        out_shape=[shape for shape, _ in outs],
        scratch_shapes=scratch,
        compiler_params=params(limit),
        name=name,
        cost_estimate=cost(micros),
    )(*args)


def attention(q_ref, k_ref, v_ref, p_ref, bias, att_ref, att, length):
    for block in range(length // QB):
        first, _ = window(block, length)
        rows = slice(block * QB, (block + 1) * QB)
        own = slice(length + block * SLOTS, length + (block + 1) * SLOTS)
        for pair in range(HEADS // 2):
            lanes = slice(pair * 128, (pair + 1) * 128)
            keys = jnp.concatenate([k_ref[first : first + WIN, lanes], k_ref[own, lanes]], axis=0)
            vals = jnp.concatenate([v_ref[first : first + WIN, lanes], v_ref[own, lanes]], axis=0)
            seen = bias[block]
            scores = nt(keys, head_pair(q_ref[rows, lanes]))
            scores = scores + jnp.concatenate([seen, seen], axis=1)
            top = jnp.max(scores, axis=0, keepdims=True)
            raised = jnp.exp(scores - top)
            probs = (raised * (1.0 / jnp.sum(raised, axis=0, keepdims=True))).astype(BF)
            p_ref[block, pair] = probs
            found = diagonal(tn(vals, probs))
            att_ref[lanes, rows] = found.astype(BF)
            att[rows, lanes] = found.T.astype(BF)


def early_body(utter, x, dy, units, biases, dyt):
    rows, length, _ = x.shape
    for row in range(rows):
        units[row] = stats(x[row].astype(F32))[0]
        visible_bias(biases.at[row], utter, row, length // SEG)
    dyt[...] = dy[...].T


def early(utter, x, dy):
    rows, length, model = x.shape
    return pl.pallas_call(
        early_body,
        in_specs=[pl.BlockSpec(memory_space=pltpu.SMEM), VMEM, VMEM],
        out_specs=[VMEM] * 3,
        out_shape=[
            full((rows, length, model), F32),
            full((rows, length // QB, KEYS, QB), F32),
            full((model, rows * length), BF),
        ],
        compiler_params=params(),
        name="early",
        cost_estimate=cost(2),
    )(utter, x, dy)


def front_body(row, first_call, plan, width, x, units, biases, vecs_in, w_in_in, w_out_in, *refs):
    nparts = len(plan) if first_call else 0
    parts = refs[:nparts]
    outs = refs[nparts:]
    if first_call:
        vecs, w_in, w_out, *outs = outs
    else:
        vecs, w_in, w_out = vecs_in, w_in_in, w_out_in
    (q_out, k_out, v_out, wide_out, p_out, att_out, resid_out, n2_out, att, *outs) = outs
    length, model = x.shape[1], x.shape[2]
    value = x[row].astype(F32)
    if first_call:
        (small,) = outs
        segments = [(band * width, width, w_in, band * model) for band in range(3)]
        segments += [(3 * width, width, w_out, 0), (4 * width, EXTRA, small, 0)]
        assemble(plan, parts, segments)
        total = jnp.zeros((8, model), F32)
        ups = [jnp.zeros((1, model), F32) for _ in range(4)]
        for piece in range(model // width):
            found = small[piece * EXTRA : (piece + 1) * EXTRA].astype(F32)
            total = total + pltpu.roll(found, piece * width, 1)[:8]
            for part in range(4):
                place = (piece * 4 + part) * width
                ups[place // model] += pltpu.roll(found, place % model, 1)[8 + part : 9 + part]
        vecs[0:8] = total
        for part in range(4):
            vecs[8 + part : 9 + part] = ups[part]
        vecs[12:16] = jnp.zeros((4, model), F32)
    normed = (units[row] * vecs[0:1] + vecs[1:2]).astype(BF)
    summary = nn(averages(length), normed).astype(BF)
    wide = jnp.concatenate([normed, summary], axis=0)
    wide_out[...] = wide.T
    q_out[...] = ((nn(normed, w_in[:, :model]) + vecs[2:3]).astype(BF).astype(F32) * 0.125).astype(BF)
    k_out[...] = nn(wide, w_in[:, model : 2 * model]).astype(BF)
    v_out[...] = (nn(wide, w_in[:, 2 * model :]) + vecs[3:4]).astype(BF)
    attention(q_out, k_out, v_out, p_out, biases.at[row], att_out, att, length)
    resid = value + nn(att[...], w_out[...]) + vecs[4:5]
    resid_out[...] = resid
    unit, _ = stats(resid)
    n2_out[...] = (unit * vecs[5:6] + vecs[6:7]).astype(BF)


def front(row, x, units, biases, vecs, w_in, w_out, plan, parts, width):
    _, length, model = x.shape
    blocks = length // QB
    wide = length + blocks * SLOTS
    first_call = vecs is None
    outs = [
        full((length, model), BF),
        full((wide, model), BF),
        full((wide, model), BF),
        full((model, wide), BF),
        full((blocks, HEADS // 2, KEYS, 2 * QB), BF),
        full((model, length), BF),
        full((length, model), F32),
        full((length, model), BF),
    ]
    scratch = [pltpu.VMEM((length, model), BF)]
    if first_call:
        outs = [full((16, model), F32), full((model, 3 * model), BF), full((model, model), BF)] + outs
        pieces = model // width
        scratch += [pltpu.VMEM((pieces * EXTRA, model), BF)]
        args = [x, units, biases] + list(parts)
        specs = [VMEM] * len(args)

        def body(x, units, biases, *refs):
            front_body(row, True, plan, width, x, units, biases, None, None, None, *refs)
    else:
        args = [x, units, biases, vecs, w_in, w_out]
        specs = [VMEM] * 6
        body = functools.partial(front_body, row, False, plan, width)
    return pl.pallas_call(
        body,
        in_specs=specs,
        out_specs=[VMEM] * len(outs),
        out_shape=outs,
        scratch_shapes=scratch,
        compiler_params=params(),
        name=f"front{row}",
        cost_estimate=cost(7),
    )(*args)


def gelu_both(v):
    c = 0.7978845608028654
    square = v * v
    bent = jnp.tanh(c * v * (1.0 + 0.044715 * square))
    half = 0.5 + 0.5 * bent
    slope = half + 0.5 * v * (1.0 - bent * bent) * (c * (1.0 + 3 * 0.044715 * square))
    return v * half, slope


def middle_body(rows, plan, width, *refs):
    n2s = refs[:rows]
    dyt, vecs, *refs = refs[rows:]
    parts = refs[: len(plan)]
    hidden, slopes, up, grads = refs[len(plan) :]
    put = pieces_into(grads)
    model, tokens = dyt.shape
    ff = up.shape[1]
    tall = ff * width // model
    assemble(plan, parts, [(0, width, up, 0)])
    length = n2s[0].shape[0]
    step = length
    for tile in range(ff // TILE):
        cols = slice(tile * TILE, (tile + 1) * TILE)
        for chunk in range(tokens // step):
            rows = slice(chunk * step, (chunk + 1) * step)
            at = chunk * step % length
            u = nn(n2s[chunk * step // length][at : at + step], up[:, cols]) + vecs[8 + tile : 9 + tile]
            value, slope = gelu_both(u)
            hidden[rows, cols] = value.astype(BF)
            slopes[rows, cols] = slope.astype(BF)
        grad = nn(dyt[...], hidden[:, cols]).astype(BF)
        for part in range(TILE // tall):
            inner_cols = slice(part * tall, (part + 1) * tall)
            outer_cols = slice(tile * TILE + part * tall, tile * TILE + (part + 1) * tall)
            device = tile * TILE // tall + part
            rows = slice(0, model)
            put(rows, outer_cols, grad[:, inner_cols], device, (rows, slice(0, tall)))


def middle(n2s, dyt, vecs, parts, plan, width, ff, fast):
    model, tokens = dyt.shape
    tall = ff * width // model
    shape = (2, 4, model, tall) if fast else (model, ff)
    outs = [
        (full((tokens, ff), BF), False),
        (full((tokens, ff), BF), False),
        (full((model, ff), BF), False),
        (full(shape, BF), False),
    ]
    body = functools.partial(middle_body, len(n2s), plan, width)
    args = [*n2s, dyt, vecs, *parts]
    return call(body, "middle", 8, len(args), outs, [], args)


def turn_body(plan, dy, slopes, *refs):
    parts = refs[: len(plan)]
    du, ub, down = refs[len(plan) :]
    tokens, model = dy.shape
    ff = down.shape[0]
    tall = plan[0][3]
    length = dy.shape[0] // 2
    assemble(plan, parts, [(0, tall, down, 0)])
    step = length
    for tile in range(ff // TILE):
        cols = slice(tile * TILE, (tile + 1) * TILE)
        sums = jnp.zeros((1, TILE), F32)
        for chunk in range(tokens // step):
            rows = slice(chunk * step, (chunk + 1) * step)
            back = nt(dy[rows], down[cols]).astype(BF).astype(F32) * slopes[rows, cols].astype(F32)
            du[rows, cols] = back.astype(BF)
            sums = sums + jnp.sum(back, axis=0, keepdims=True)
        ub[tile : tile + 1] = sums


def turn(dy, slopes, parts, plan):
    tokens, model = dy.shape
    ff = slopes.shape[1]
    outs = [
        (full((tokens, ff), BF), False),
        (full((ff // TILE, TILE), F32), False),
        (full((ff, model), BF), False),
    ]
    args = [dy, slopes, *parts]
    return call(functools.partial(turn_body, plan), "turn", 5, len(args), outs, [], args)


def rise_body(rows, width, *refs):
    n2s = refs[:rows]
    du, grads, n2t = refs[rows:]
    length, model = n2s[0].shape
    ff = du.shape[1]
    put = pieces_into(grads)
    for row in range(rows):
        n2t[:, row * length : (row + 1) * length] = n2s[row][...].T
    for tile in range(ff // TILE):
        cols = slice(tile * TILE, (tile + 1) * TILE)
        put_rows(put, nn(n2t[...], du[:, cols]).astype(BF), width, cols)


def rise(n2s, du, width, fast):
    tokens, ff = du.shape
    model = n2s[0].shape[1]
    shape = (2, 4, width, ff) if fast else (model, ff)
    scratch = [pltpu.VMEM((model, tokens), BF)]
    body = functools.partial(rise_body, len(n2s), width)
    args = [*n2s, du]
    return call(body, "rise", 4, len(args), [(full(shape, BF), False)], scratch, args)[0]


def norm_back(grad, unit, scale):
    first = jnp.mean(grad, axis=-1, keepdims=True)
    second = jnp.mean(grad * unit, axis=-1, keepdims=True)
    return scale * (grad - first - unit * second)


def back_body(rows, *refs):
    resids = refs[:rows]
    du, dy, vecs, up, w_out, dresid, datt, sums = refs[rows:]
    tokens, model = dy.shape
    length = resids[0].shape[0]
    step = length
    gains = jnp.zeros((1, model), F32)
    shifts = jnp.zeros((1, model), F32)
    biases = jnp.zeros((1, model), F32)
    downs = jnp.zeros((1, model), F32)
    for chunk in range(tokens // step):
        rows = slice(chunk * step, (chunk + 1) * step)
        at = chunk * step % length
        grad = nt(du[rows], up[...])
        unit, scale = stats(resids[chunk * step // length][at : at + step])
        gains = gains + jnp.sum(grad * unit, axis=0, keepdims=True)
        shifts = shifts + jnp.sum(grad, axis=0, keepdims=True)
        top = dy[rows].astype(F32)
        downs = downs + jnp.sum(top, axis=0, keepdims=True)
        total = top + norm_back(grad * vecs[5:6], unit, scale)
        biases = biases + jnp.sum(total, axis=0, keepdims=True)
        dresid[rows] = total
        datt[rows] = nt(total.astype(BF), w_out[...]).astype(BF)
    sums[0:1] = gains
    sums[1:2] = shifts
    sums[2:3] = biases
    sums[3:4] = downs


def back(resids, du, dy, vecs, up, w_out):
    tokens, model = dy.shape
    outs = [
        (full((tokens, model), F32), False),
        (full((tokens, model), BF), False),
        (full((4, model), F32), False),
    ]
    args = [*resids, du, dy, vecs, up, w_out]
    return call(functools.partial(back_body, len(resids)), "back", 8, len(args), outs, [], args)


def rear_body(row, q, k, v, p, datt, mixed, sums, dk, dv):
    length, model = q.shape
    extent = k.shape[0]
    base = row * length
    dk[...] = jnp.zeros_like(dk)
    dv[...] = jnp.zeros_like(dv)
    mixed[length:extent, 0:model] = jnp.zeros((extent - length, model), BF)
    for block in range(length // QB):
        first, _ = window(block, length)
        rows = slice(block * QB, (block + 1) * QB)
        own = slice(length + block * SLOTS, length + (block + 1) * SLOTS)
        span = slice(first, first + WIN)
        for pair in range(HEADS // 2):
            lanes = slice(pair * 128, (pair + 1) * 128)
            keys = jnp.concatenate([k[span, lanes], k[own, lanes]], axis=0)
            vals = jnp.concatenate([v[span, lanes], v[own, lanes]], axis=0)
            queries = head_pair(q[rows, lanes])
            tops = head_pair(datt[base + block * QB : base + (block + 1) * QB, lanes])
            probs = p[block, pair]
            wides = probs.astype(F32)
            back = nt(vals, tops)
            inner = jnp.sum(wides * back, axis=0, keepdims=True)
            dscores = (wides * (back - inner)).astype(BF)
            gv = nn(probs, tops)
            gk = nn(dscores, queries)
            dv[span, lanes] += gv[:WIN]
            dv[own, lanes] = gv[WIN:]
            dk[span, lanes] += gk[:WIN]
            dk[own, lanes] = gk[WIN:]
            gq = diagonal(tn(keys, dscores)).T * 0.125
            mixed[rows, lanes] = gq.astype(BF)
    mixed[:, model : 2 * model] = dk[...].astype(BF)
    mixed[:, 2 * model :] = dv[...].astype(BF)
    sums[0:1] = jnp.sum(mixed[:, 0:model].astype(F32), axis=0, keepdims=True)
    sums[1:2] = jnp.sum(mixed[:, 2 * model :].astype(F32), axis=0, keepdims=True)


def rear(row, q, k, v, p, datt):
    length, model = q.shape
    extent = k.shape[0]
    outs = [(full((extent, 3 * model), BF), False), (full((2, model), F32), False)]
    scratch = [pltpu.VMEM((extent, model), F32), pltpu.VMEM((extent, model), F32)]
    body = functools.partial(rear_body, row)
    return call(body, f"rear{row}", 7, 5, outs, scratch, [q, k, v, p, datt])


def base_body(rows, width, x, dresid, vecs, w_in, gub, back_sums, *refs):
    mixeds = refs[:rows]
    rear_sums = refs[rows : 2 * rows]
    wides = refs[2 * rows : 3 * rows]
    atts = refs[3 * rows : 4 * rows]
    grads, dx, sums = refs[4 * rows :]
    length, model = x.shape[1], x.shape[2]
    put = pieces_into(grads)
    for tile in range(3):
        cols = slice(tile * model, (tile + 1) * model)
        total = nn(wides[0][...], mixeds[0][:, cols])
        for row in range(1, rows):
            total = total + nn(wides[row][...], mixeds[row][:, cols])
        put_rows(put, total.astype(BF), width, cols)
    total = nn(atts[0][...], dresid[0:length].astype(BF))
    for row in range(1, rows):
        total = total + nn(atts[row][...], dresid[row * length : (row + 1) * length].astype(BF))
    put_rows(put, total.astype(BF), width, slice(3 * model, 4 * model))
    average = averages(length)
    gains = jnp.zeros((1, model), F32)
    shifts = jnp.zeros((1, model), F32)
    for row in range(rows):
        unit, scale = stats(x[row].astype(F32))
        grad = nt(mixeds[row][...], w_in[...])
        grad = grad[:length] + tn(average, grad[length:].astype(BF))
        gains = gains + jnp.sum(grad * unit, axis=0, keepdims=True)
        shifts = shifts + jnp.sum(grad, axis=0, keepdims=True)
        dx[row] = dresid[row * length : (row + 1) * length] + norm_back(grad * vecs[0:1], unit, scale)
    sums[0:1] = gains
    sums[1:2] = shifts
    sums[2:4] = wide_sum(*[part[...] for part in rear_sums])
    sums[4:8] = back_sums[...]
    sums[8:12] = gub[...]
    sums[12:16] = jnp.zeros((4, model), F32)
    if len(grads.shape) == 4:
        for device in range(model // width):
            block = [sums[0:8, device * width : (device + 1) * width]]
            for part in range(4):
                place = (device * 4 + part) * width
                row, low = 8 + place // model, place % model
                block.append(sums[row : row + 1, low : low + width])
            block.append(jnp.zeros((4, width), F32))
            block = jnp.concatenate(block, axis=0)
            block = jnp.concatenate([block, jnp.zeros((16, 128 - width), F32)], axis=1)
            put(None, None, block.astype(BF), device, (slice(0, 16), slice(4 * model, 4 * model + 128)))
            put(
                None,
                None,
                jnp.zeros((width - 16, 128), BF),
                device,
                (slice(16, width), slice(4 * model, 4 * model + 128)),
            )


def base(x, dresid, vecs, w_in, gub, back_sums, mixeds, rear_sums, wides, atts, width, fast):
    rows, length, model = x.shape
    shape = (2, 4, width, 4 * model + 128) if fast else (model, 4 * model)
    outs = [
        (full(shape, BF), False),
        (full((rows, length, model), F32), False),
        (full((16, model), F32), False),
    ]
    args = [x, dresid, vecs, w_in, gub, back_sums, *mixeds, *rear_sums, *wides, *atts]
    return call(functools.partial(base_body, rows, width), "base", 6, len(args), outs, [], args)


def finish_body(rows, vecs, hidden, down, *refs):
    resids = refs[:rows]
    out = refs[rows]
    length = resids[0].shape[0]
    step = length
    for chunk in range(hidden.shape[0] // step):
        rows = slice(chunk * step, (chunk + 1) * step)
        at = chunk * step % length
        resid = resids[chunk * step // length][at : at + step]
        out[rows] = (resid + nn(hidden[rows], down[...]) + vecs[7:8]).astype(BF)


def finish(vecs, hidden, down, resids):
    outs = [(full((hidden.shape[0], down.shape[1]), BF), False)]
    args = [vecs, hidden, down, *resids]
    return call(functools.partial(finish_body, len(resids)), "finish", 4, len(args), outs, [], args)[0]


def along(value, offset):
    return lax.ppermute(value, "fsdp", [(i, i ^ offset) for i in range(8)])


def across(value, offset, size):
    return lax.ppermute(value, "dp", [(i, i ^ offset) for i in range(size)])


def pack_body(*refs):
    sources, out = refs[:11], refs[11]
    w_in, w_out, *rows, sem = refs[12:]
    width, model = w_out.shape
    targets = [w_in, w_out, *rows]
    copies = [pltpu.make_async_copy(a, b, sem) for a, b in zip(sources, targets)]
    for copy in copies:
        copy.start()
    out[4 * width :] = jnp.zeros((EXTRA, model), BF)
    for copy in copies:
        copy.wait()
    for band in range(3):
        out[band * width : (band + 1) * width] = w_in[:, band * model : (band + 1) * model]
    out[3 * width : 4 * width] = w_out[...]
    lines = [row[...].astype(F32).reshape(1, width) for row in rows[:8]]
    bias = rows[8][...].astype(F32).reshape(1, 4 * width)
    lines += [bias[:, at * width : (at + 1) * width] for at in range(4)]
    lines += [jnp.zeros((4, width), F32)]
    out[4 * width :, 0:width] = jnp.concatenate(lines, axis=0).astype(BF)


def pack(project_in, project_out, vectors, up_bias):
    width, model = project_out.shape
    outs = [(full((4 * width + EXTRA, model), BF), False)]
    args = [project_in, project_out, *vectors, up_bias]
    scratch = [pltpu.VMEM(arg.shape, BF) for arg in args] + [pltpu.SemaphoreType.DMA]
    return call(pack_body, "pack", 2, 0, outs, scratch, args, 60 * 2**20)[0]


def settle_body(width, tall, small, *refs):
    me = lax.axis_index("fsdp")
    value = small[...]
    model = value.shape[1]
    turned = pltpu.roll(value, lax.rem(model - me * width, model), 1)
    for row, out in enumerate(refs[:8]):
        out[...] = turned[row : row + 1, 0:width].reshape(width)
    place = me * tall
    wide = jnp.zeros((1, model), F32)
    for row in range(4):
        wide = jnp.where(place // model == row, value[8 + row : 9 + row], wide)
    wide = jnp.concatenate([wide] * 8, axis=0)
    turned = pltpu.roll(wide, lax.rem(model - lax.rem(place, model), model), 1)
    refs[8][...] = turned[0:1, 0:tall].reshape(tall)


def settle(small, width, tall):
    outs = [(full((width,), F32), False)] * 8 + [(full((tall,), F32), False)]
    return call(functools.partial(settle_body, width, tall), "settle", 2, 1, outs, [], [small])


def wide_sum(*values):
    total = values[0].astype(F32)
    for value in values[1:]:
        total = total + value.astype(F32)
    return total


def plus(*values):
    def body(*refs):
        refs[-1][...] = wide_sum(*[ref[...] for ref in refs[:-1]]).astype(refs[-1].dtype)

    outs = [(full(values[0].shape, values[0].dtype), False)]
    return call(body, "plus", 1, len(values), outs, [], values)[0]


def plus_here(both, there):
    def body(both, there, out):
        out[...] = wide_sum(both[0], there[...]).astype(BF)

    return call(body, "plus", 1, 2, [(full(there.shape, BF), False)], [], [both, there])[0]


def own_sum(held, *others):
    return wide_sum(held[0], *[other[...] for other in others]).astype(BF)


def cross_halves(held):
    def body(held, to_x, to_y):
        half = held.shape[1] // 2
        to_x[0] = held[1, :half]
        to_x[1] = held[3, :half]
        to_y[0] = held[2, half:]
        to_y[1] = held[3, half:]

    _, rows, columns = held.shape
    outs = [(full((2, rows // 2, columns), BF), False)] * 2
    return call(body, "cross_halves", 1, 1, outs, [], [held])


def second(held, from_x, from_y):
    def body(held, from_x, from_y, to_x, to_y):
        half = held.shape[1] // 2
        to_x[...] = wide_sum(held[1, half:], from_y[1]).astype(BF)
        to_y[...] = wide_sum(held[2, :half], from_x[1]).astype(BF)

    outs = [(full(from_x.shape[1:], BF), False)] * 2
    return call(body, "second", 1, 3, outs, [], [held, from_x, from_y])


def hop_halves(*args):
    def body(held, from_x, from_y, last_x, last_y, keep, send):
        half = keep.shape[0]
        top = wide_sum(held[0, :half], from_x[0], last_y[...]).astype(BF)
        bottom = wide_sum(held[0, half:], from_y[0], last_x[...]).astype(BF)
        odd = odd_plane()

        @pl.when(odd)
        def _():
            keep[...] = bottom
            send[...] = top

        @pl.when(jnp.logical_not(odd))
        def _():
            keep[...] = top
            send[...] = bottom

    _, rows, columns = args[0].shape
    outs = [(full((rows // 2, columns), BF), False)] * 2
    return call(body, "hop_halves", 1, 5, outs, [], args)


def odd_plane():
    return lax.rem(lax.axis_index("dp"), 2) == 1


def by_halves(*args):
    def body(*refs):
        keep, send = refs[-2:]
        total = own_sum(*refs[:-2])
        half = keep.shape[0]
        odd = odd_plane()

        @pl.when(odd)
        def _():
            keep[...] = total[half:]
            send[...] = total[:half]

        @pl.when(jnp.logical_not(odd))
        def _():
            keep[...] = total[:half]
            send[...] = total[half:]

    rows, columns = args[1].shape
    outs = [(full((rows // 2, columns), BF), False)] * 2
    return call(body, "by_halves", 1, len(args), outs, [], args)


def by_quarters(*args):
    def body(*refs):
        outs = refs[-5:-1]
        whole = refs[-1]
        whole[...] = own_sum(*refs[:-5])
        rows = outs[0].shape[0]
        me = lax.axis_index("dp")
        for offset, out in enumerate(outs):
            place = pl.multiple_of(jnp.bitwise_xor(me, offset) * rows, rows)
            out[...] = whole[pl.ds(place, rows), :]

    rows, columns = args[1].shape
    outs = [(full((rows // 4, columns), BF), False)] * 4
    scratch = [pltpu.VMEM((rows, columns), BF)]
    return call(body, "by_quarters", 1, len(args), outs, scratch, args)


def last_down(keep, other):
    def body(keep, other, out):
        half = keep.shape[0]
        odd = odd_plane()

        @pl.when(odd)
        def _():
            out[:, :half] = other[...].astype(F32).T
            out[:, half:] = keep[...].astype(F32).T

        @pl.when(jnp.logical_not(odd))
        def _():
            out[:, :half] = keep[...].astype(F32).T
            out[:, half:] = other[...].astype(F32).T

    half, tall = keep.shape
    return call(body, "last_down", 1, 2, [(full((tall, 2 * half), F32), False)], [], [keep, other])[0]


def last_up(keep, other):
    def body(keep, other, out):
        half = keep.shape[0]
        odd = odd_plane()

        @pl.when(odd)
        def _():
            out[:half] = other[...].astype(F32)
            out[half:] = keep[...].astype(F32)

        @pl.when(jnp.logical_not(odd))
        def _():
            out[:half] = keep[...].astype(F32)
            out[half:] = other[...].astype(F32)

    half, ff = keep.shape
    return call(body, "last_up", 1, 2, [(full((2 * half, ff), F32), False)], [], [keep, other])[0]


def last_in(quarters, model, width, tall):
    def body(*refs):
        parts, g_in, g_out, small = refs[:4], refs[4], refs[5], refs[15]
        vectors = refs[6:15]
        rows = parts[0].shape[0]
        me = lax.axis_index("dp")
        for offset, part in enumerate(parts):
            place = pl.multiple_of(jnp.bitwise_xor(me, offset) * rows, rows)
            g_in[pl.ds(place, rows), :] = part[:, : 3 * model].astype(F32)
            g_out[pl.ds(place, rows), :] = part[:, 3 * model : 4 * model].astype(F32)
            small[pl.ds(place, rows), :] = part[:, 4 * model :].astype(F32)
        for row in range(8):
            vectors[row][...] = small[row : row + 1, 0:width].reshape(width)
        wide = jnp.concatenate([small[8 + part : 9 + part, 0:width] for part in range(4)], axis=1)
        vectors[8][...] = wide.reshape(tall)

    outs = [(full((width, 3 * model), F32), False), (full((width, model), F32), False)]
    outs += [(full((width,), F32), False)] * 8 + [(full((tall,), F32), False)]
    scratch = [pltpu.VMEM((width, 128), F32)]
    return call(body, "last_in", 1, 4, outs, scratch, quarters)


def after(value, *others):
    return lax.optimization_barrier((value,) + others)[0]


def whole_plan(rows, size):
    return [(0, False, 0, rows, size)]


def near_plan(rows):
    return [(offset, True, 0, rows, 1) for offset in (0, 1, 2, 4, 6, 3, 5, 7)]


def shards(
    group,
    frames,
    upstream,
    utterance,
    first_gain,
    first_shift,
    project_in,
    query_bias,
    value_bias,
    project_out,
    out_bias,
    second_gain,
    second_shift,
    up_weight,
    up_bias,
    down_weight,
    down_bias,
):
    micro, nrows, length, model = frames.shape
    rows = micro * nrows
    width = project_out.shape[0]
    size = model // width
    ff = up_weight.shape[1]
    tall = ff // size
    x = frames.reshape(rows, length, model)
    dy = upstream.reshape(rows * length, model)
    utter = utterance.reshape(rows, length // SEG)
    vectors = (first_gain, first_shift, query_bias, value_bias, out_bias, second_gain, second_shift, down_bias)
    fast = size == 8 and group == 4 and rows == 2
    packed = pack(project_in, project_out, vectors, up_bias)
    if fast:
        plan_a, plan_u, plan_d = near_plan(packed.shape[0]), near_plan(width), near_plan(tall)
        a2, a4, a6, a1 = [along(packed, offset) for offset in (2, 4, 6, 1)]
        units, biases, dyt = early(after(utter, a1), x, dy)
        a2, a4, a6, dyt = lax.optimization_barrier((a2, a4, a6, dyt))
        up_piece = after(up_weight, a2, a4, a6)
        u2, u4, u1 = along(up_piece, 2), along(up_piece, 4), along(up_piece, 1)
        parts_a = [packed, a1, a2, a4, a6, along(a2, 1), along(a4, 1)] + [along(a6, 1)]
        u6 = along(up_piece, 6)
        first = after(x, u1)
    else:
        plan_a, plan_u, plan_d = whole_plan(packed.shape[0], size), whole_plan(width, size), whole_plan(tall, size)
        parts_a = [lax.all_gather(packed, "fsdp", axis=0, tiled=True)]
        parts_u = [lax.all_gather(up_weight, "fsdp", axis=0, tiled=True)]
        parts_d = [lax.all_gather(down_weight, "fsdp", axis=0, tiled=True)]
        first = x
        units, biases, dyt = early(utter, x, dy)
    saved = []
    vecs, w_in, w_out, *first = front(0, first, units, biases, None, None, None, plan_a, parts_a, width)
    saved.append(first)
    held = vecs
    if fast:
        held = vecs
    for row in range(1, rows):
        saved.append(front(row, x, units, biases, held, w_in, w_out, plan_a, None, width))
    qs, ks, vs, wides, ps, atts, resids, n2s = zip(*saved)
    if fast:
        down_piece = after(down_weight, n2s[0])
        d2, d4 = along(down_piece, 2), along(down_piece, 4)
        *u_got, done = lax.optimization_barrier((u2, u4, u6, n2s[1]))
        parts_u = [up_piece, u1, *u_got] + [along(part, 1) for part in u_got[:2]] + [along(u_got[2], 1)]
        d2, d4, down_piece, done = lax.optimization_barrier((d2, d4, down_piece, done))
        held = after(vecs, d2, d4)
        d3, d5, d6, d1 = along(d2, 1), along(d4, 1), along(down_piece, 6), along(down_piece, 1)
    hidden, slopes, up, gdown = middle(n2s, dyt, held, parts_u, plan_u, width, ff, fast)
    if fast:
        d6 = after(d6, slopes)
        parts_d = [down_piece, d1, d2, d4, d6, d3, d5, along(d6, 1)]
    if fast:
        du, gub, down = turn(dy, slopes, parts_d, plan_d)
        d_core = along(after(gdown, gub)[1], 1)
        gup = rise(n2s, du, width, fast)
        d_sum = plus_here(gdown, after(d_core, gup))
        to_x, to_y = cross_halves(d_sum)
        d_x, d_y = along(to_x, 2), along(to_y, 4)
        u_core = along(gup[1], 1)
        dresid, datt, sums2 = back(resids, after(du, to_x), dy, vecs, up, w_out)
        u_core, done = lax.optimization_barrier((u_core, sums2))
        u_sum = plus_here(gup, u_core)
        to_x, to_y = cross_halves(u_sum)
        u_x, u_y = along(to_x, 2), along(to_y, 4)
        mixed0, sums0 = rear(0, after(qs[0], to_x), ks[0], vs[0], ps[0], datt)
        d_x, d_y, done = lax.optimization_barrier((d_x, d_y, sums0))
        to_x, to_y = second(d_sum, d_x, d_y)
        d_x2, d_y2 = along(to_x, 2), along(to_y, 4)
        mixed1, sums1 = rear(1, after(qs[1], to_x), ks[1], vs[1], ps[1], datt)
        u_x, u_y, d_x2, d_y2, done = lax.optimization_barrier((u_x, u_y, d_x2, d_y2, sums1))
        to_x, to_y = second(u_sum, u_x, u_y)
        u_x2, u_y2 = along(to_x, 2), along(to_y, 4)
        d_keep, d_send = hop_halves(d_sum, d_x, d_y, d_x2, d_y2)
        d_z = across(d_send, 1, group)
        mixeds = (mixed0, mixed1)
        gin, dx, small = base(
            x,
            after(dresid, to_x, d_send),
            vecs,
            w_in,
            gub,
            sums2,
            mixeds,
            (sums0, sums1),
            wides,
            atts,
            width,
            fast,
        )
        u_x2, u_y2, d_z, done = lax.optimization_barrier((u_x2, u_y2, d_z, small))
        u_keep, u_send = hop_halves(u_sum, u_x, u_y, u_x2, u_y2)
        u_z = across(u_send, 1, group)
        d_keep = plus(d_keep, d_z)
        d_z2 = across(d_keep, 2, group)
        i_core = along(after(gin, u_send, d_keep)[1], 1)
        i_sum = plus_here(gin, i_core)
        i_got = [along(i_sum[1], 2), along(i_sum[2], 4), along(i_sum[3], 6)]
        out = finish(after(vecs, i_sum), hidden, down, resids)
        *i_got, done = lax.optimization_barrier((*i_got, out))
        u_z, d_z2, done = lax.optimization_barrier((u_z, d_z2, i_sum))
        u_keep = plus(u_keep, u_z)
        u_z2 = across(u_keep, 2, group)
        d_keep = plus(d_keep, d_z2)
        d_other = across(d_keep, 1, group)
        i_own, *i_send = by_quarters(i_sum, *i_got)
        i_got = [across(i_send[offset - 1], offset, group) for offset in (3, 2, 1)]
        u_keep = plus(u_keep, u_z2)
        u_other = across(u_keep, 1, group)
        i_own = plus(i_own, *i_got)
        i_got = [across(i_own, offset, group) for offset in (3, 2, 1)][::-1]
        gdown = last_down(after(d_keep, i_own), d_other)
        g_up = last_up(after(u_keep, i_own), u_other)
        g_in, g_out, *vectors = last_in([i_own, *i_got], model, width, tall)
    else:
        du, gub, down = turn(dy, slopes, parts_d, plan_d)
        dresid, datt, sums2 = back(resids, du, dy, vecs, up, w_out)
        gup = rise(n2s, du, width, fast)
        pairs = [rear(row, qs[row], ks[row], vs[row], ps[row], datt) for row in range(rows)]
        mixeds, rear_sums = zip(*pairs)
        gin, dx, small = base(
            x, dresid, vecs, w_in, gub, sums2, mixeds, rear_sums, wides, atts, width, fast
        )
        out = finish(vecs, hidden, down, resids)

        def total(value, dim):
            own = lax.psum_scatter(value, "fsdp", scatter_dimension=dim, tiled=True)
            return lax.psum(own, "dp").astype(F32)

        gdown = total(gdown, 1).T
        g_up = total(gup, 0)
        gin = total(gin, 0)
        g_in, g_out = gin[:, : 3 * model], gin[:, 3 * model :]
        vectors = settle(lax.psum(small, ("dp", "fsdp")), width, tall)
    return (
        out.reshape(frames.shape),
        dx.reshape(frames.shape),
        vectors[0],
        vectors[1],
        g_in,
        vectors[2],
        vectors[3],
        g_out,
        vectors[6],
        vectors[4],
        vectors[5],
        g_up,
        vectors[8],
        gdown,
        vectors[7],
    )


def solution(mesh):
    rows = P(None, ("dp", "fsdp"), None, None)
    vector = P("fsdp")
    matrix = P("fsdp", None)
    weights = (vector, vector, matrix, vector, vector, matrix, vector, vector, vector, matrix, vector, matrix, vector)
    return jax.shard_map(
        functools.partial(shards, mesh.shape["dp"]),
        mesh=mesh,
        in_specs=(rows, rows, P(None, ("dp", "fsdp"), None)) + weights,
        out_specs=(rows, rows) + weights,
        check_vma=False,
    )
```

```python
import functools

import jax
import jax.numpy as jnp
from jax import lax
from jax.experimental import pallas as pl
from jax.experimental.pallas import tpu as pltpu
from jax.sharding import PartitionSpec as P

HEADS = 8
SEG = 16
RIGHT = 4
LEFT = 30
MEMS = 4
QB = 128
WIN = 176
SLOTS = 16
KEYS = WIN + SLOTS
TILE = 512
EXTRA = 16
BF = jnp.bfloat16
F32 = jnp.float32
HBM = pl.BlockSpec(memory_space=pl.ANY)
VMEM = pl.BlockSpec(memory_space=pltpu.VMEM)
LIMIT = 16 * 2**20


def nn(a, b):
    return lax.dot_general(a, b, (((1,), (0,)), ((), ())), preferred_element_type=F32)


def nt(a, b):
    return lax.dot_general(a, b, (((1,), (1,)), ((), ())), preferred_element_type=F32)


def tn(a, b):
    return lax.dot_general(a, b, (((0,), (0,)), ((), ())), preferred_element_type=F32)


def params(limit=LIMIT):
    return pltpu.CompilerParams(vmem_limit_bytes=limit)


def cost(micros):
    return pl.CostEstimate(flops=int(micros * 0.1e9), bytes_accessed=0, transcendentals=0)


def window(block, length):
    first = min(max(block * QB - 32, 0), length - WIN)
    slot = min(max(block * QB // SEG - MEMS, 0), length // SEG - SLOTS)
    return first, slot


def full(shape, dtype):
    return jax.ShapeDtypeStruct(shape, dtype)


def assemble(plan, parts, segments):
    me = lax.axis_index("fsdp")
    for number, (offset, relative, first, rows, count) in enumerate(plan):
        for each in range(count):
            device = jnp.bitwise_xor(me, offset) if relative else each
            for start, height, target, column in segments:
                low, high = max(first, start), min(first + rows, start + height)
                if low < high:
                    place = pl.multiple_of(device * height, height) + low - start
                    at = each * rows + low - first
                    value = parts[number][at : at + high - low, :]
                    target[pl.ds(place, high - low), column : column + value.shape[1]] = value


def pieces_into(grads):
    if len(grads.shape) == 2:

        def put_whole(rows, columns, value, device, within):
            grads[rows, columns] = value

        return put_whole
    me = lax.axis_index("fsdp")
    chips = [jnp.bitwise_xor(me // 2, chip) for chip in range(4)]
    cores = [jnp.bitwise_xor(lax.rem(me, 2), core) for core in range(2)]

    def put(rows, columns, value, device, within):
        grads[cores[device % 2], chips[device // 2], within[0], within[1]] = value

    return put


def put_rows(put, value, width, columns):
    for device in range(value.shape[0] // width):
        rows = slice(device * width, (device + 1) * width)
        put(rows, columns, value[rows], device, (slice(0, width), columns))


def stats(value):
    mean = jnp.mean(value, axis=-1, keepdims=True)
    offset = value - mean
    spread = jnp.mean(offset * offset, axis=-1, keepdims=True)
    scale = lax.rsqrt(spread + 1e-05)
    return offset * scale, scale


def averages(length):
    blocks = length // QB
    rows = blocks * SLOTS
    row = lax.broadcasted_iota(jnp.int32, (rows, length), 0)
    seg = lax.broadcasted_iota(jnp.int32, (rows, length), 1) // SEG
    slot = row % SLOTS
    for block in range(blocks):
        first = window(block, length)[1]
        slot = slot + jnp.where(row // SLOTS == block, first, 0)
    return jnp.where(slot == seg, 1.0 / SEG, 0.0).astype(BF)


def head_pair(value):
    lane = lax.broadcasted_iota(jnp.int32, value.shape, 1)
    zero = jnp.zeros_like(value)
    half = value.shape[1] // 2
    return jnp.concatenate(
        [jnp.where(lane < half, value, zero), jnp.where(lane >= half, value, zero)], axis=0
    )


def diagonal(value):
    half = value.shape[0] // 2
    return jnp.concatenate([value[:half, :QB], value[half:, QB:]], axis=0)


def visible_bias(bias_ref, utter_ref, row, nsegs):
    length = nsegs * SEG
    key = lax.broadcasted_iota(jnp.int32, (KEYS, QB), 0)
    query = lax.broadcasted_iota(jnp.int32, (KEYS, QB), 1)
    segs = QB // SEG
    starts = [jnp.int32(0)]
    for seg in range(1, nsegs):
        same = utter_ref[row, seg] == utter_ref[row, seg - 1]
        starts.append(jnp.where(same, starts[-1], seg))
    for block in range(length // QB):
        first, slot = window(block, length)
        lower = jnp.zeros((KEYS, QB), jnp.int32)
        upper = jnp.zeros((KEYS, QB), jnp.int32)
        for part in range(segs):
            seg = block * segs + part
            more = jnp.int32(0)
            if seg + 1 < nsegs:
                more = jnp.where(utter_ref[row, seg + 1] == utter_ref[row, seg], RIGHT, 0)
            frame_low = jnp.maximum(seg * SEG - LEFT, starts[seg] * SEG) - first
            frame_high = seg * SEG + SEG + more - first
            slot_low = jnp.maximum(seg - MEMS, starts[seg]) - slot + WIN
            slot_high = jnp.int32(seg - slot + WIN)
            here = query // SEG == part
            lower = jnp.where(here, jnp.where(key < WIN, frame_low, slot_low), lower)
            upper = jnp.where(here, jnp.where(key < WIN, frame_high, slot_high), upper)
        seen = (key >= lower) & (key < upper)
        bias_ref[block] = jnp.where(seen, 0.0, -1e9)


def call(body, name, micros, ins, outs, scratch, args, limit=LIMIT):
    kinds = [HBM if by_copy else VMEM for _, by_copy in outs]
    return pl.pallas_call(
        body,
        in_specs=[VMEM] * ins + [HBM] * (len(args) - ins),
        out_specs=kinds,
        out_shape=[shape for shape, _ in outs],
        scratch_shapes=scratch,
        compiler_params=params(limit),
        name=name,
        cost_estimate=cost(micros),
    )(*args)


def attention(q_ref, k_ref, v_ref, p_ref, bias, att_ref, att, length):
    for block in range(length // QB):
        first, _ = window(block, length)
        rows = slice(block * QB, (block + 1) * QB)
        own = slice(length + block * SLOTS, length + (block + 1) * SLOTS)
        for pair in range(HEADS // 2):
            lanes = slice(pair * 128, (pair + 1) * 128)
            keys = jnp.concatenate([k_ref[first : first + WIN, lanes], k_ref[own, lanes]], axis=0)
            vals = jnp.concatenate([v_ref[first : first + WIN, lanes], v_ref[own, lanes]], axis=0)
            seen = bias[block]
            scores = nt(keys, head_pair(q_ref[rows, lanes]))
            scores = scores + jnp.concatenate([seen, seen], axis=1)
            top = jnp.max(scores, axis=0, keepdims=True)
            raised = jnp.exp(scores - top)
            probs = (raised * (1.0 / jnp.sum(raised, axis=0, keepdims=True))).astype(BF)
            p_ref[block, pair] = probs
            found = diagonal(tn(vals, probs))
            att_ref[lanes, rows] = found.astype(BF)
            att[rows, lanes] = found.T.astype(BF)


def early_body(utter, x, units, scales, biases):
    rows, length, _ = x.shape
    for row in range(rows):
        unit, scale = stats(x[row].astype(F32))
        units[row] = unit
        scales[row] = jnp.broadcast_to(scale, scales.shape[1:])
        visible_bias(biases.at[row], utter, row, length // SEG)


def turned(dy):
    def body(dy, out):
        out[...] = dy[...].T

    return call(body, "turned", 1, 1, [(full(dy.shape[::-1], BF), False)], [], [dy])[0]


def early(utter, x):
    rows, length, model = x.shape
    return pl.pallas_call(
        early_body,
        in_specs=[pl.BlockSpec(memory_space=pltpu.SMEM), VMEM],
        out_specs=[VMEM] * 3,
        out_shape=[
            full((rows, length, model), F32),
            full((rows, length, 128), F32),
            full((rows, length // QB, KEYS, QB), F32),
        ],
        compiler_params=params(),
        name="early",
        cost_estimate=cost(2),
    )(utter, x)


def front_body(row, first_call, plan, width, x, units, biases, vecs_in, w_in_in, w_out_in, *refs):
    nparts = len(plan) if first_call else 0
    parts = refs[:nparts]
    outs = refs[nparts:]
    if first_call:
        vecs, w_in, w_out, *outs = outs
    else:
        vecs, w_in, w_out = vecs_in, w_in_in, w_out_in
    (q_out, k_out, v_out, wide_out, p_out, att_out, resid_out) = outs[:7]
    (n2_out, n2t_out, unit_out, scale_out, att, *outs) = outs[7:]
    length, model = x.shape[1], x.shape[2]
    value = x[row].astype(F32)
    if first_call:
        (small,) = outs
        segments = [(band * width, width, w_in, band * model) for band in range(3)]
        segments += [(3 * width, width, w_out, 0), (4 * width, EXTRA, small, 0)]
        assemble(plan, parts, segments)
        total = jnp.zeros((8, model), F32)
        ups = [jnp.zeros((1, model), F32) for _ in range(4)]
        for piece in range(model // width):
            found = small[piece * EXTRA : (piece + 1) * EXTRA].astype(F32)
            total = total + pltpu.roll(found, piece * width, 1)[:8]
            for part in range(4):
                place = (piece * 4 + part) * width
                ups[place // model] += pltpu.roll(found, place % model, 1)[8 + part : 9 + part]
        vecs[0:8] = total
        for part in range(4):
            vecs[8 + part : 9 + part] = ups[part]
        vecs[12:16] = jnp.zeros((4, model), F32)
    normed = (units[row] * vecs[0:1] + vecs[1:2]).astype(BF)
    summary = nn(averages(length), normed).astype(BF)
    wide = jnp.concatenate([normed, summary], axis=0)
    wide_out[...] = wide.T
    q_out[...] = ((nn(normed, w_in[:, :model]) + vecs[2:3]).astype(BF).astype(F32) * 0.125).astype(BF)
    k_out[...] = nn(wide, w_in[:, model : 2 * model]).astype(BF)
    v_out[...] = (nn(wide, w_in[:, 2 * model :]) + vecs[3:4]).astype(BF)
    attention(q_out, k_out, v_out, p_out, biases.at[row], att_out, att, length)
    resid = value + nn(att[...], w_out[...]) + vecs[4:5]
    resid_out[...] = resid
    unit, scale = stats(resid)
    unit_out[...] = unit
    scale_out[...] = jnp.broadcast_to(scale, scale_out.shape)
    normed = (unit * vecs[5:6] + vecs[6:7]).astype(BF)
    n2_out[...] = normed
    n2t_out[...] = normed.T


def front(row, x, units, biases, vecs, w_in, w_out, plan, parts, width):
    _, length, model = x.shape
    blocks = length // QB
    wide = length + blocks * SLOTS
    first_call = vecs is None
    outs = [
        full((length, model), BF),
        full((wide, model), BF),
        full((wide, model), BF),
        full((model, wide), BF),
        full((blocks, HEADS // 2, KEYS, 2 * QB), BF),
        full((model, length), BF),
        full((length, model), F32),
        full((length, model), BF),
        full((model, length), BF),
        full((length, model), F32),
        full((length, 128), F32),
    ]
    scratch = [pltpu.VMEM((length, model), BF)]
    if first_call:
        outs = [full((16, model), F32), full((model, 3 * model), BF), full((model, model), BF)] + outs
        pieces = model // width
        scratch += [pltpu.VMEM((pieces * EXTRA, model), BF)]
        args = [x, units, biases] + list(parts)
        specs = [VMEM] * len(args)

        def body(x, units, biases, *refs):
            front_body(row, True, plan, width, x, units, biases, None, None, None, *refs)
    else:
        args = [x, units, biases, vecs, w_in, w_out]
        specs = [VMEM] * 6
        body = functools.partial(front_body, row, False, plan, width)
    return pl.pallas_call(
        body,
        in_specs=specs,
        out_specs=[VMEM] * len(outs),
        out_shape=outs,
        scratch_shapes=scratch,
        compiler_params=params(),
        name=f"front{row}",
        cost_estimate=cost(7),
    )(*args)


def gelu_both(v):
    c = 0.7978845608028654
    a = 0.044715
    square = v * v
    half = 0.5 + 0.5 * jnp.tanh(v * (c + (c * a) * square))
    value = v * half
    return value, half + value * (1.0 - half) * (2 * c + (6 * c * a) * square)


def middle_body(rows, plan, width, *refs):
    n2s = refs[:rows]
    dyt, vecs, *refs = refs[rows:]
    parts = refs[: len(plan)]
    hidden, slopes, up, grads = refs[len(plan) :]
    put = pieces_into(grads)
    model, tokens = dyt.shape
    ff = up.shape[1]
    tall = ff * width // model
    assemble(plan, parts, [(0, width, up, 0)])
    length = n2s[0].shape[0]
    step = length
    for tile in range(ff // TILE):
        cols = slice(tile * TILE, (tile + 1) * TILE)
        for chunk in range(tokens // step):
            rows = slice(chunk * step, (chunk + 1) * step)
            at = chunk * step % length
            u = nn(n2s[chunk * step // length][at : at + step], up[:, cols]) + vecs[8 + tile : 9 + tile]
            value, slope = gelu_both(u)
            hidden[rows, cols] = value.astype(BF)
            slopes[rows, cols] = slope.astype(BF)
    for tile in range(ff // TILE):
        cols = slice(tile * TILE, (tile + 1) * TILE)
        grad = nn(dyt[...], hidden[:, cols]).astype(BF)
        for part in range(TILE // tall):
            inner_cols = slice(part * tall, (part + 1) * tall)
            outer_cols = slice(tile * TILE + part * tall, tile * TILE + (part + 1) * tall)
            device = tile * TILE // tall + part
            rows = slice(0, model)
            put(rows, outer_cols, grad[:, inner_cols], device, (rows, slice(0, tall)))


def middle(n2s, dyt, vecs, parts, plan, width, ff, fast):
    model, tokens = dyt.shape
    tall = ff * width // model
    shape = (2, 4, model, tall) if fast else (model, ff)
    outs = [
        (full((tokens, ff), BF), False),
        (full((tokens, ff), BF), False),
        (full((model, ff), BF), False),
        (full(shape, BF), False),
    ]
    body = functools.partial(middle_body, len(n2s), plan, width)
    args = [*n2s, dyt, vecs, *parts]
    return call(body, "middle", 8, len(args), outs, [], args)


def turn_body(plan, dy, slopes, *refs):
    parts = refs[: len(plan)]
    du, ub, down = refs[len(plan) :]
    tokens, model = dy.shape
    ff = down.shape[0]
    tall = plan[0][3]
    length = dy.shape[0] // 2
    assemble(plan, parts, [(0, tall, down, 0)])
    step = length
    for tile in range(ff // TILE):
        cols = slice(tile * TILE, (tile + 1) * TILE)
        sums = jnp.zeros((1, TILE), F32)
        for chunk in range(tokens // step):
            rows = slice(chunk * step, (chunk + 1) * step)
            back = nt(dy[rows], down[cols]).astype(BF).astype(F32) * slopes[rows, cols].astype(F32)
            du[rows, cols] = back.astype(BF)
            sums = sums + jnp.sum(back, axis=0, keepdims=True)
        ub[tile : tile + 1] = sums


def turn(dy, slopes, parts, plan):
    tokens, model = dy.shape
    ff = slopes.shape[1]
    outs = [
        (full((tokens, ff), BF), False),
        (full((ff // TILE, TILE), F32), False),
        (full((ff, model), BF), False),
    ]
    args = [dy, slopes, *parts]
    return call(functools.partial(turn_body, plan), "turn", 5, len(args), outs, [], args)


def rise_body(rows, width, *refs):
    n2ts = refs[:rows]
    du, grads, turned = refs[rows:]
    length = n2ts[0].shape[1]
    put = pieces_into(grads)
    for row in range(rows):
        turned[:, row * length : (row + 1) * length] = n2ts[row][...]
    for tile in range(du.shape[1] // TILE):
        cols = slice(tile * TILE, (tile + 1) * TILE)
        put_rows(put, nn(turned[...], du[:, cols]).astype(BF), width, cols)


def rise(n2ts, du, width, fast):
    tokens, ff = du.shape
    model = n2ts[0].shape[0]
    shape = (2, 4, width, ff) if fast else (model, ff)
    body = functools.partial(rise_body, len(n2ts), width)
    args = [*n2ts, du]
    scratch = [pltpu.VMEM((model, tokens), BF)]
    return call(body, "rise", 4, len(args), [(full(shape, BF), False)], scratch, args)[0]


def norm_back(grad, unit, scale):
    first = jnp.mean(grad, axis=-1, keepdims=True)
    second = jnp.mean(grad * unit, axis=-1, keepdims=True)
    return scale * (grad - first - unit * second)


def back_body(rows, *refs):
    units = refs[:rows]
    scales = refs[rows : 2 * rows]
    du, dy, vecs, up, w_out, dresid, datt, sums = refs[2 * rows :]
    tokens, model = dy.shape
    length = units[0].shape[0]
    step = length
    gains = jnp.zeros((1, model), F32)
    shifts = jnp.zeros((1, model), F32)
    biases = jnp.zeros((1, model), F32)
    downs = jnp.zeros((1, model), F32)
    for chunk in range(tokens // step):
        rows = slice(chunk * step, (chunk + 1) * step)
        at = chunk * step % length
        grad = nt(du[rows], up[...])
        unit = units[chunk * step // length][at : at + step]
        scale = scales[chunk * step // length][at : at + step, 0:1]
        gains = gains + jnp.sum(grad * unit, axis=0, keepdims=True)
        shifts = shifts + jnp.sum(grad, axis=0, keepdims=True)
        top = dy[rows].astype(F32)
        downs = downs + jnp.sum(top, axis=0, keepdims=True)
        total = top + norm_back(grad * vecs[5:6], unit, scale)
        biases = biases + jnp.sum(total, axis=0, keepdims=True)
        dresid[rows] = total
        datt[rows] = nt(total.astype(BF), w_out[...]).astype(BF)
    sums[0:1] = gains
    sums[1:2] = shifts
    sums[2:3] = biases
    sums[3:4] = downs


def back(units, scales, du, dy, vecs, up, w_out):
    tokens, model = dy.shape
    outs = [
        (full((tokens, model), F32), False),
        (full((tokens, model), BF), False),
        (full((4, model), F32), False),
    ]
    args = [*units, *scales, du, dy, vecs, up, w_out]
    return call(functools.partial(back_body, len(units)), "back", 8, len(args), outs, [], args)


def rear_body(row, q, k, v, p, datt, mixed, sums, dk, dv):
    length, model = q.shape
    extent = k.shape[0]
    base = row * length
    dk[...] = jnp.zeros_like(dk)
    dv[...] = jnp.zeros_like(dv)
    mixed[length:extent, 0:model] = jnp.zeros((extent - length, model), BF)
    for block in range(length // QB):
        first, _ = window(block, length)
        rows = slice(block * QB, (block + 1) * QB)
        own = slice(length + block * SLOTS, length + (block + 1) * SLOTS)
        span = slice(first, first + WIN)
        for pair in range(HEADS // 2):
            lanes = slice(pair * 128, (pair + 1) * 128)
            keys = jnp.concatenate([k[span, lanes], k[own, lanes]], axis=0)
            vals = jnp.concatenate([v[span, lanes], v[own, lanes]], axis=0)
            queries = head_pair(q[rows, lanes])
            tops = head_pair(datt[base + block * QB : base + (block + 1) * QB, lanes])
            probs = p[block, pair]
            wides = probs.astype(F32)
            back = nt(vals, tops)
            inner = jnp.sum(wides * back, axis=0, keepdims=True)
            dscores = (wides * (back - inner)).astype(BF)
            gv = nn(probs, tops)
            gk = nn(dscores, queries)
            dv[span, lanes] += gv[:WIN]
            dv[own, lanes] = gv[WIN:]
            dk[span, lanes] += gk[:WIN]
            dk[own, lanes] = gk[WIN:]
            gq = diagonal(tn(keys, dscores)).T * 0.125
            mixed[rows, lanes] = gq.astype(BF)
    mixed[:, model : 2 * model] = dk[...].astype(BF)
    mixed[:, 2 * model :] = dv[...].astype(BF)
    sums[0:1] = jnp.sum(mixed[:, 0:model].astype(F32), axis=0, keepdims=True)
    sums[1:2] = jnp.sum(mixed[:, 2 * model :].astype(F32), axis=0, keepdims=True)


def rear(row, q, k, v, p, datt):
    length, model = q.shape
    extent = k.shape[0]
    outs = [(full((extent, 3 * model), BF), False), (full((2, model), F32), False)]
    scratch = [pltpu.VMEM((extent, model), F32), pltpu.VMEM((extent, model), F32)]
    body = functools.partial(rear_body, row)
    return call(body, f"rear{row}", 7, 5, outs, scratch, [q, k, v, p, datt])


def base_body(rows, width, units, dresid, w_in, gub, back_sums, *refs):
    mixeds = refs[:rows]
    rear_sums = refs[rows : 2 * rows]
    wides = refs[2 * rows : 3 * rows]
    atts = refs[3 * rows : 4 * rows]
    grads, dnormed, sums = refs[4 * rows :]
    length, model = units.shape[1], units.shape[2]
    put = pieces_into(grads)
    for tile in range(3):
        cols = slice(tile * model, (tile + 1) * model)
        total = nn(wides[0][...], mixeds[0][:, cols])
        for row in range(1, rows):
            total = total + nn(wides[row][...], mixeds[row][:, cols])
        put_rows(put, total.astype(BF), width, cols)
    total = nn(atts[0][...], dresid[0:length].astype(BF))
    for row in range(1, rows):
        total = total + nn(atts[row][...], dresid[row * length : (row + 1) * length].astype(BF))
    put_rows(put, total.astype(BF), width, slice(3 * model, 4 * model))
    average = averages(length)
    gains = jnp.zeros((1, model), F32)
    shifts = jnp.zeros((1, model), F32)
    for row in range(rows):
        grad = nt(mixeds[row][...], w_in[...])
        grad = grad[:length] + tn(average, grad[length:].astype(BF))
        gains = gains + jnp.sum(grad * units[row], axis=0, keepdims=True)
        shifts = shifts + jnp.sum(grad, axis=0, keepdims=True)
        dnormed[row] = grad
    sums[0:1] = gains
    sums[1:2] = shifts
    sums[2:4] = wide_sum(*[part[...] for part in rear_sums])
    sums[4:8] = back_sums[...]
    sums[8:12] = gub[...]
    sums[12:16] = jnp.zeros((4, model), F32)
    if len(grads.shape) == 4:
        for device in range(model // width):
            block = [sums[0:8, device * width : (device + 1) * width]]
            for part in range(4):
                place = (device * 4 + part) * width
                row, low = 8 + place // model, place % model
                block.append(sums[row : row + 1, low : low + width])
            block.append(jnp.zeros((4, width), F32))
            block = jnp.concatenate(block, axis=0)
            block = jnp.concatenate([block, jnp.zeros((16, 128 - width), F32)], axis=1)
            put(None, None, block.astype(BF), device, (slice(0, 16), slice(4 * model, 4 * model + 128)))
            put(
                None,
                None,
                jnp.zeros((width - 16, 128), BF),
                device,
                (slice(16, width), slice(4 * model, 4 * model + 128)),
            )


def base(units, dresid, w_in, gub, back_sums, mixeds, rear_sums, wides, atts, width, fast):
    rows, length, model = units.shape
    shape = (2, 4, width, 4 * model + 128) if fast else (model, 4 * model)
    outs = [
        (full(shape, BF), False),
        (full((rows, length, model), F32), False),
        (full((16, model), F32), False),
    ]
    args = [units, dresid, w_in, gub, back_sums, *mixeds, *rear_sums, *wides, *atts]
    return call(functools.partial(base_body, rows, width), "base", 6, len(args), outs, [], args)


def shed_body(units, scales, dresid, vecs, dnormed, dx):
    rows, length, _ = units.shape
    for row in range(rows):
        own = dresid[row * length : (row + 1) * length]
        dx[row] = own + norm_back(dnormed[row] * vecs[0:1], units[row], scales[row, :, 0:1])


def shed(units, scales, dresid, vecs, dnormed):
    args = [units, scales, dresid, vecs, dnormed]
    return call(shed_body, "shed", 2, 5, [(full(units.shape, F32), False)], [], args)[0]


def finish_body(rows, vecs, hidden, down, *refs):
    resids = refs[:rows]
    out = refs[rows]
    length = resids[0].shape[0]
    step = length
    for chunk in range(hidden.shape[0] // step):
        rows = slice(chunk * step, (chunk + 1) * step)
        at = chunk * step % length
        resid = resids[chunk * step // length][at : at + step]
        out[rows] = (resid + nn(hidden[rows], down[...]) + vecs[7:8]).astype(BF)


def finish(vecs, hidden, down, resids):
    outs = [(full((hidden.shape[0], down.shape[1]), BF), False)]
    args = [vecs, hidden, down, *resids]
    return call(functools.partial(finish_body, len(resids)), "finish", 4, len(args), outs, [], args)[0]


def along(value, offset):
    return lax.ppermute(value, "fsdp", [(i, i ^ offset) for i in range(8)])


def across(value, offset, size):
    return lax.ppermute(value, "dp", [(i, i ^ offset) for i in range(size)])


def pack_body(*refs):
    sources, out = refs[:11], refs[11]
    w_in, w_out, *rows, sem = refs[12:]
    width, model = w_out.shape
    targets = [w_in, w_out, *rows]
    copies = [pltpu.make_async_copy(a, b, sem) for a, b in zip(sources, targets)]
    for copy in copies:
        copy.start()
    out[4 * width :] = jnp.zeros((EXTRA, model), BF)
    for copy in copies:
        copy.wait()
    for band in range(3):
        out[band * width : (band + 1) * width] = w_in[:, band * model : (band + 1) * model]
    out[3 * width : 4 * width] = w_out[...]
    lines = [row[...].astype(F32).reshape(1, width) for row in rows[:8]]
    bias = rows[8][...].astype(F32).reshape(1, 4 * width)
    lines += [bias[:, at * width : (at + 1) * width] for at in range(4)]
    lines += [jnp.zeros((4, width), F32)]
    out[4 * width :, 0:width] = jnp.concatenate(lines, axis=0).astype(BF)


def pack(project_in, project_out, vectors, up_bias):
    width, model = project_out.shape
    outs = [(full((4 * width + EXTRA, model), BF), False)]
    args = [project_in, project_out, *vectors, up_bias]
    scratch = [pltpu.VMEM(arg.shape, BF) for arg in args] + [pltpu.SemaphoreType.DMA]
    return call(pack_body, "pack", 2, 0, outs, scratch, args, 60 * 2**20)[0]


def settle_body(width, tall, small, *refs):
    me = lax.axis_index("fsdp")
    value = small[...]
    model = value.shape[1]
    turned = pltpu.roll(value, lax.rem(model - me * width, model), 1)
    for row, out in enumerate(refs[:8]):
        out[...] = turned[row : row + 1, 0:width].reshape(width)
    place = me * tall
    wide = jnp.zeros((1, model), F32)
    for row in range(4):
        wide = jnp.where(place // model == row, value[8 + row : 9 + row], wide)
    wide = jnp.concatenate([wide] * 8, axis=0)
    turned = pltpu.roll(wide, lax.rem(model - lax.rem(place, model), model), 1)
    refs[8][...] = turned[0:1, 0:tall].reshape(tall)


def settle(small, width, tall):
    outs = [(full((width,), F32), False)] * 8 + [(full((tall,), F32), False)]
    return call(functools.partial(settle_body, width, tall), "settle", 2, 1, outs, [], [small])


def wide_sum(*values):
    total = values[0].astype(F32)
    for value in values[1:]:
        total = total + value.astype(F32)
    return total


def plus(*values):
    def body(*refs):
        refs[-1][...] = wide_sum(*[ref[...] for ref in refs[:-1]]).astype(refs[-1].dtype)

    outs = [(full(values[0].shape, values[0].dtype), False)]
    return call(body, "plus", 1, len(values), outs, [], values)[0]


def plus_here(both, there):
    def body(both, there, out):
        out[...] = wide_sum(both[0], there[...]).astype(BF)

    return call(body, "plus", 1, 2, [(full(there.shape, BF), False)], [], [both, there])[0]


def own_sum(held, *others):
    return wide_sum(held[0], *[other[...] for other in others]).astype(BF)


def cross_halves(held):
    def body(held, to_x, to_y):
        half = held.shape[1] // 2
        to_x[0] = held[1, :half]
        to_x[1] = held[3, :half]
        to_y[0] = held[2, half:]
        to_y[1] = held[3, half:]

    _, rows, columns = held.shape
    outs = [(full((2, rows // 2, columns), BF), False)] * 2
    return call(body, "cross_halves", 1, 1, outs, [], [held])


def second(held, from_x, from_y):
    def body(held, from_x, from_y, to_x, to_y):
        half = held.shape[1] // 2
        to_x[...] = wide_sum(held[1, half:], from_y[1]).astype(BF)
        to_y[...] = wide_sum(held[2, :half], from_x[1]).astype(BF)

    outs = [(full(from_x.shape[1:], BF), False)] * 2
    return call(body, "second", 1, 3, outs, [], [held, from_x, from_y])


def hop_halves(*args):
    def body(held, from_x, from_y, last_x, last_y, keep, send):
        half = keep.shape[0]
        top = wide_sum(held[0, :half], from_x[0], last_y[...]).astype(BF)
        bottom = wide_sum(held[0, half:], from_y[0], last_x[...]).astype(BF)
        odd = odd_plane()

        @pl.when(odd)
        def _():
            keep[...] = bottom
            send[...] = top

        @pl.when(jnp.logical_not(odd))
        def _():
            keep[...] = top
            send[...] = bottom

    _, rows, columns = args[0].shape
    outs = [(full((rows // 2, columns), BF), False)] * 2
    return call(body, "hop_halves", 1, 5, outs, [], args)


def odd_plane():
    return lax.rem(lax.axis_index("dp"), 2) == 1


def by_halves(*args):
    def body(*refs):
        keep, send = refs[-2:]
        total = own_sum(*refs[:-2])
        half = keep.shape[0]
        odd = odd_plane()

        @pl.when(odd)
        def _():
            keep[...] = total[half:]
            send[...] = total[:half]

        @pl.when(jnp.logical_not(odd))
        def _():
            keep[...] = total[:half]
            send[...] = total[half:]

    rows, columns = args[1].shape
    outs = [(full((rows // 2, columns), BF), False)] * 2
    return call(body, "by_halves", 1, len(args), outs, [], args)


def by_quarters(*args):
    def body(*refs):
        outs = refs[-5:-1]
        whole = refs[-1]
        whole[...] = own_sum(*refs[:-5])
        rows = outs[0].shape[0]
        me = lax.axis_index("dp")
        for offset, out in enumerate(outs):
            place = pl.multiple_of(jnp.bitwise_xor(me, offset) * rows, rows)
            out[...] = whole[pl.ds(place, rows), :]

    rows, columns = args[1].shape
    outs = [(full((rows // 4, columns), BF), False)] * 4
    scratch = [pltpu.VMEM((rows, columns), BF)]
    return call(body, "by_quarters", 1, len(args), outs, scratch, args)


def last_down(keep, other):
    def body(keep, other, out):
        half = keep.shape[0]
        odd = odd_plane()

        @pl.when(odd)
        def _():
            out[:, :half] = other[...].astype(F32).T
            out[:, half:] = keep[...].astype(F32).T

        @pl.when(jnp.logical_not(odd))
        def _():
            out[:, :half] = keep[...].astype(F32).T
            out[:, half:] = other[...].astype(F32).T

    half, tall = keep.shape
    return call(body, "last_down", 1, 2, [(full((tall, 2 * half), F32), False)], [], [keep, other])[0]


def last_up(keep, other):
    def body(keep, other, out):
        half = keep.shape[0]
        odd = odd_plane()

        @pl.when(odd)
        def _():
            out[:half] = other[...].astype(F32)
            out[half:] = keep[...].astype(F32)

        @pl.when(jnp.logical_not(odd))
        def _():
            out[:half] = keep[...].astype(F32)
            out[half:] = other[...].astype(F32)

    half, ff = keep.shape
    return call(body, "last_up", 1, 2, [(full((2 * half, ff), F32), False)], [], [keep, other])[0]


def last_in(quarters, model, width, tall):
    def body(*refs):
        parts, g_in, g_out, small = refs[:4], refs[4], refs[5], refs[15]
        vectors = refs[6:15]
        rows = parts[0].shape[0]
        me = lax.axis_index("dp")
        for offset, part in enumerate(parts):
            place = pl.multiple_of(jnp.bitwise_xor(me, offset) * rows, rows)
            g_in[pl.ds(place, rows), :] = part[:, : 3 * model].astype(F32)
            g_out[pl.ds(place, rows), :] = part[:, 3 * model : 4 * model].astype(F32)
            small[pl.ds(place, rows), :] = part[:, 4 * model :].astype(F32)
        for row in range(8):
            vectors[row][...] = small[row : row + 1, 0:width].reshape(width)
        wide = jnp.concatenate([small[8 + part : 9 + part, 0:width] for part in range(4)], axis=1)
        vectors[8][...] = wide.reshape(tall)

    outs = [(full((width, 3 * model), F32), False), (full((width, model), F32), False)]
    outs += [(full((width,), F32), False)] * 8 + [(full((tall,), F32), False)]
    scratch = [pltpu.VMEM((width, 128), F32)]
    return call(body, "last_in", 1, 4, outs, scratch, quarters)


def after(value, *others):
    return lax.optimization_barrier((value,) + others)[0]


def whole_plan(rows, size):
    return [(0, False, 0, rows, size)]


def near_plan(rows):
    return [(offset, True, 0, rows, 1) for offset in (0, 1, 2, 4, 6, 3, 5, 7)]


def shards(
    group,
    frames,
    upstream,
    utterance,
    first_gain,
    first_shift,
    project_in,
    query_bias,
    value_bias,
    project_out,
    out_bias,
    second_gain,
    second_shift,
    up_weight,
    up_bias,
    down_weight,
    down_bias,
):
    micro, nrows, length, model = frames.shape
    rows = micro * nrows
    width = project_out.shape[0]
    size = model // width
    ff = up_weight.shape[1]
    tall = ff // size
    x = frames.reshape(rows, length, model)
    dy = upstream.reshape(rows * length, model)
    utter = utterance.reshape(rows, length // SEG)
    vectors = (first_gain, first_shift, query_bias, value_bias, out_bias, second_gain, second_shift, down_bias)
    fast = size == 8 and group == 4 and rows == 2
    packed = pack(project_in, project_out, vectors, up_bias)
    if fast:
        plan_a, plan_u, plan_d = near_plan(packed.shape[0]), near_plan(width), near_plan(tall)
        a2, a4, a6, a1 = [along(packed, offset) for offset in (2, 4, 6, 1)]
        units, scales, biases = early(after(utter, a1), x)
        a6, units = lax.optimization_barrier((a6, units))
        up_piece = after(up_weight, a6)
        dyt = turned(after(dy, a6))
        a2, a4, dyt = lax.optimization_barrier((a2, a4, dyt))
        u2, u4, u1 = along(up_piece, 2), along(up_piece, 4), along(up_piece, 1)
        parts_a = [packed, a1, a2, a4, a6, along(a2, 1), along(a4, 1)] + [along(a6, 1)]
        u6 = along(up_piece, 6)
        first = after(x, u1)
    else:
        plan_a, plan_u, plan_d = whole_plan(packed.shape[0], size), whole_plan(width, size), whole_plan(tall, size)
        parts_a = [lax.all_gather(packed, "fsdp", axis=0, tiled=True)]
        parts_u = [lax.all_gather(up_weight, "fsdp", axis=0, tiled=True)]
        parts_d = [lax.all_gather(down_weight, "fsdp", axis=0, tiled=True)]
        first = x
        units, scales, biases = early(utter, x)
        dyt = turned(dy)
    saved = []
    vecs, w_in, w_out, *first = front(0, first, units, biases, None, None, None, plan_a, parts_a, width)
    saved.append(first)
    held = vecs
    if fast:
        held = after(vecs, u2, u4)
        done = first[-1]
        u3, u5 = along(after(u2, done), 1), along(after(u4, done), 1)
    for row in range(1, rows):
        saved.append(front(row, x, units, biases, held, w_in, w_out, plan_a, None, width))
    qs, ks, vs, wides, ps, atts, resids, n2s, n2ts, unit2s, scale2s = zip(*saved)
    if fast:
        down_piece = after(down_weight, n2s[0])
        d2, d4 = along(down_piece, 2), along(down_piece, 4)
        u6, u3, u5, done = lax.optimization_barrier((u6, u3, u5, n2s[1]))
        parts_u = [up_piece, u1, u2, u4, u6, u3, u5, along(u6, 1)]
        down_piece, done = lax.optimization_barrier((down_piece, done))
        d6 = along(down_piece, 6)
        d2, d4, done = lax.optimization_barrier((d2, d4, done))
        held = after(vecs, d2, d4)
        d3, d5, d1 = along(d2, 1), along(d4, 1), along(after(down_piece, d2), 1)
    hidden, slopes, up, gdown = middle(n2s, dyt, held, parts_u, plan_u, width, ff, fast)
    if fast:
        d6 = after(d6, slopes)
        parts_d = [down_piece, d1, d2, d4, d6, d3, d5, along(d6, 1)]
    if fast:
        du, gub, down = turn(dy, slopes, parts_d, plan_d)
        d_core = along(after(gdown, gub)[1], 1)
        gup = rise(n2ts, du, width, fast)
        d_sum = plus_here(gdown, after(d_core, gup))
        to_x, to_y = cross_halves(d_sum)
        d_x, d_y = along(to_x, 2), along(to_y, 4)
        u_core = along(gup[1], 1)
        dresid, datt, sums2 = back(unit2s, scale2s, after(du, to_x), dy, vecs, up, w_out)
        u_core, done = lax.optimization_barrier((u_core, sums2))
        u_sum = plus_here(gup, u_core)
        to_x, to_y = cross_halves(u_sum)
        u_x, u_y = along(to_x, 2), along(to_y, 4)
        mixed0, sums0 = rear(0, after(qs[0], to_x), ks[0], vs[0], ps[0], datt)
        d_x, d_y, done = lax.optimization_barrier((d_x, d_y, sums0))
        to_x, to_y = second(d_sum, d_x, d_y)
        d_x2, d_y2 = along(to_x, 2), along(to_y, 4)
        mixed1, sums1 = rear(1, after(qs[1], to_x), ks[1], vs[1], ps[1], datt)
        u_x, u_y, d_x2, d_y2, done = lax.optimization_barrier((u_x, u_y, d_x2, d_y2, sums1))
        to_x, to_y = second(u_sum, u_x, u_y)
        u_x2, u_y2 = along(to_x, 2), along(to_y, 4)
        d_keep, d_send = hop_halves(d_sum, d_x, d_y, d_x2, d_y2)
        d_z = across(d_send, 1, group)
        mixeds = (mixed0, mixed1)
        gin, dnormed, small = base(
            units,
            after(dresid, to_x, d_send),
            w_in,
            gub,
            sums2,
            mixeds,
            (sums0, sums1),
            wides,
            atts,
            width,
            fast,
        )
        u_x2, u_y2, d_z, done = lax.optimization_barrier((u_x2, u_y2, d_z, small))
        u_keep, u_send = hop_halves(u_sum, u_x, u_y, u_x2, u_y2)
        u_z = across(u_send, 1, group)
        d_keep = plus(d_keep, d_z)
        d_z2 = across(d_keep, 2, group)
        i_core = along(after(gin, u_send, d_keep)[1], 1)
        i_sum = plus_here(gin, i_core)
        i_got = [along(i_sum[1], 2), along(i_sum[2], 4), along(i_sum[3], 6)]
        out = finish(after(vecs, i_sum), hidden, down, resids)
        dx = shed(units, scales, dresid, after(vecs, out), dnormed)
        *i_got, done = lax.optimization_barrier((*i_got, dx))
        u_z, d_z2, done = lax.optimization_barrier((u_z, d_z2, i_sum))
        u_keep = plus(u_keep, u_z)
        u_z2 = across(u_keep, 2, group)
        d_keep = plus(d_keep, d_z2)
        d_other = across(d_keep, 1, group)
        i_own, *i_send = by_quarters(i_sum, *i_got)
        i_got = [across(i_send[offset - 1], offset, group) for offset in (3, 2, 1)]
        u_keep = plus(u_keep, u_z2)
        u_other = across(u_keep, 1, group)
        i_own = plus(i_own, *i_got)
        i_got = [across(i_own, offset, group) for offset in (3, 2, 1)][::-1]
        gdown = last_down(after(d_keep, i_own), d_other)
        g_up = last_up(after(u_keep, i_own), u_other)
        g_in, g_out, *vectors = last_in([i_own, *i_got], model, width, tall)
    else:
        du, gub, down = turn(dy, slopes, parts_d, plan_d)
        dresid, datt, sums2 = back(unit2s, scale2s, du, dy, vecs, up, w_out)
        gup = rise(n2ts, du, width, fast)
        pairs = [rear(row, qs[row], ks[row], vs[row], ps[row], datt) for row in range(rows)]
        mixeds, rear_sums = zip(*pairs)
        gin, dnormed, small = base(
            units, dresid, w_in, gub, sums2, mixeds, rear_sums, wides, atts, width, fast
        )
        dx = shed(units, scales, dresid, vecs, dnormed)
        out = finish(vecs, hidden, down, resids)

        def total(value, dim):
            own = lax.psum_scatter(value, "fsdp", scatter_dimension=dim, tiled=True)
            return lax.psum(own, "dp").astype(F32)

        gdown = total(gdown, 1).T
        g_up = total(gup, 0)
        gin = total(gin, 0)
        g_in, g_out = gin[:, : 3 * model], gin[:, 3 * model :]
        vectors = settle(lax.psum(small, ("dp", "fsdp")), width, tall)
    return (
        out.reshape(frames.shape),
        dx.reshape(frames.shape),
        vectors[0],
        vectors[1],
        g_in,
        vectors[2],
        vectors[3],
        g_out,
        vectors[6],
        vectors[4],
        vectors[5],
        g_up,
        vectors[8],
        gdown,
        vectors[7],
    )


def solution(mesh):
    rows = P(None, ("dp", "fsdp"), None, None)
    vector = P("fsdp")
    matrix = P("fsdp", None)
    weights = (vector, vector, matrix, vector, vector, matrix, vector, vector, vector, matrix, vector, matrix, vector)
    return jax.shard_map(
        functools.partial(shards, mesh.shape["dp"]),
        mesh=mesh,
        in_specs=(rows, rows, P(None, ("dp", "fsdp"), None)) + weights,
        out_specs=(rows, rows) + weights,
        check_vma=False,
    )
```

```python
import functools

import jax
import jax.numpy as jnp
from jax import lax
from jax.experimental import pallas as pl
from jax.experimental.pallas import tpu as pltpu
from jax.sharding import PartitionSpec as P

HEADS = 8
SEG = 16
RIGHT = 4
LEFT = 30
MEMS = 4
QB = 128
WIN = 176
SLOTS = 16
KEYS = WIN + SLOTS
TILE = 512
EXTRA = 16
BF = jnp.bfloat16
F32 = jnp.float32
HBM = pl.BlockSpec(memory_space=pl.ANY)
VMEM = pl.BlockSpec(memory_space=pltpu.VMEM)
LIMIT = 16 * 2**20


def nn(a, b):
    return lax.dot_general(a, b, (((1,), (0,)), ((), ())), preferred_element_type=F32)


def nt(a, b):
    return lax.dot_general(a, b, (((1,), (1,)), ((), ())), preferred_element_type=F32)


def tn(a, b):
    return lax.dot_general(a, b, (((0,), (0,)), ((), ())), preferred_element_type=F32)


def params(limit=LIMIT):
    return pltpu.CompilerParams(vmem_limit_bytes=limit)


def cost(micros):
    return pl.CostEstimate(flops=int(micros * 0.1e9), bytes_accessed=0, transcendentals=0)


def window(block, length):
    first = min(max(block * QB - 32, 0), length - WIN)
    slot = min(max(block * QB // SEG - MEMS, 0), length // SEG - SLOTS)
    return first, slot


def full(shape, dtype):
    return jax.ShapeDtypeStruct(shape, dtype)


def assemble(plan, parts, segments):
    me = lax.axis_index("fsdp")
    for number, (offset, relative, first, rows, count) in enumerate(plan):
        for each in range(count):
            device = jnp.bitwise_xor(me, offset) if relative else each
            for start, height, target, column in segments:
                low, high = max(first, start), min(first + rows, start + height)
                if low < high:
                    place = pl.multiple_of(device * height, height) + low - start
                    at = each * rows + low - first
                    value = parts[number][at : at + high - low, :]
                    target[pl.ds(place, high - low), column : column + value.shape[1]] = value


def pieces_into(grads):
    if len(grads.shape) == 2:

        def put_whole(rows, columns, value, device, within):
            grads[rows, columns] = value

        return put_whole
    me = lax.axis_index("fsdp")
    chips = [jnp.bitwise_xor(me // 2, chip) for chip in range(4)]
    cores = [jnp.bitwise_xor(lax.rem(me, 2), core) for core in range(2)]

    def put(rows, columns, value, device, within):
        grads[cores[device % 2], chips[device // 2], within[0], within[1]] = value

    return put


def put_rows(put, value, width, columns):
    for device in range(value.shape[0] // width):
        rows = slice(device * width, (device + 1) * width)
        put(rows, columns, value[rows], device, (slice(0, width), columns))


def stats(value):
    mean = jnp.mean(value, axis=-1, keepdims=True)
    offset = value - mean
    spread = jnp.mean(offset * offset, axis=-1, keepdims=True)
    scale = lax.rsqrt(spread + 1e-05)
    return offset * scale, scale


def averages(length):
    blocks = length // QB
    rows = blocks * SLOTS
    row = lax.broadcasted_iota(jnp.int32, (rows, length), 0)
    seg = lax.broadcasted_iota(jnp.int32, (rows, length), 1) // SEG
    slot = row % SLOTS
    for block in range(blocks):
        first = window(block, length)[1]
        slot = slot + jnp.where(row // SLOTS == block, first, 0)
    return jnp.where(slot == seg, 1.0 / SEG, 0.0).astype(BF)


def head_pair(value):
    lane = lax.broadcasted_iota(jnp.int32, value.shape, 1)
    zero = jnp.zeros_like(value)
    half = value.shape[1] // 2
    return jnp.concatenate(
        [jnp.where(lane < half, value, zero), jnp.where(lane >= half, value, zero)], axis=0
    )


def diagonal(value):
    half = value.shape[0] // 2
    return jnp.concatenate([value[:half, :QB], value[half:, QB:]], axis=0)


def visible_bias(bias_ref, utter_ref, row, nsegs):
    length = nsegs * SEG
    key = lax.broadcasted_iota(jnp.int32, (KEYS, QB), 0)
    query = lax.broadcasted_iota(jnp.int32, (KEYS, QB), 1)
    segs = QB // SEG
    starts = [jnp.int32(0)]
    for seg in range(1, nsegs):
        same = utter_ref[row, seg] == utter_ref[row, seg - 1]
        starts.append(jnp.where(same, starts[-1], seg))
    for block in range(length // QB):
        first, slot = window(block, length)
        lower = jnp.zeros((KEYS, QB), jnp.int32)
        upper = jnp.zeros((KEYS, QB), jnp.int32)
        for part in range(segs):
            seg = block * segs + part
            more = jnp.int32(0)
            if seg + 1 < nsegs:
                more = jnp.where(utter_ref[row, seg + 1] == utter_ref[row, seg], RIGHT, 0)
            frame_low = jnp.maximum(seg * SEG - LEFT, starts[seg] * SEG) - first
            frame_high = seg * SEG + SEG + more - first
            slot_low = jnp.maximum(seg - MEMS, starts[seg]) - slot + WIN
            slot_high = jnp.int32(seg - slot + WIN)
            here = query // SEG == part
            lower = jnp.where(here, jnp.where(key < WIN, frame_low, slot_low), lower)
            upper = jnp.where(here, jnp.where(key < WIN, frame_high, slot_high), upper)
        seen = (key >= lower) & (key < upper)
        bias_ref[block] = jnp.where(seen, 0.0, -1e9)


def call(body, name, micros, ins, outs, scratch, args, limit=LIMIT):
    kinds = [HBM if by_copy else VMEM for _, by_copy in outs]
    return pl.pallas_call(
        body,
        in_specs=[VMEM] * ins + [HBM] * (len(args) - ins),
        out_specs=kinds,
        out_shape=[shape for shape, _ in outs],
        scratch_shapes=scratch,
        compiler_params=params(limit),
        name=name,
        cost_estimate=cost(micros),
    )(*args)


def attention(q_ref, k_ref, v_ref, p_ref, bias, att_ref, att, length):
    for block in range(length // QB):
        first, _ = window(block, length)
        rows = slice(block * QB, (block + 1) * QB)
        own = slice(length + block * SLOTS, length + (block + 1) * SLOTS)
        for pair in range(HEADS // 2):
            lanes = slice(pair * 128, (pair + 1) * 128)
            keys = jnp.concatenate([k_ref[first : first + WIN, lanes], k_ref[own, lanes]], axis=0)
            vals = jnp.concatenate([v_ref[first : first + WIN, lanes], v_ref[own, lanes]], axis=0)
            seen = bias[block]
            scores = nt(keys, head_pair(q_ref[rows, lanes]))
            scores = scores + jnp.concatenate([seen, seen], axis=1)
            top = jnp.max(scores, axis=0, keepdims=True)
            raised = jnp.exp(scores - top)
            probs = (raised * (1.0 / jnp.sum(raised, axis=0, keepdims=True))).astype(BF)
            p_ref[block, pair] = probs
            found = diagonal(tn(vals, probs))
            att_ref[lanes, rows] = found.astype(BF)
            att[rows, lanes] = found.T.astype(BF)


def early_body(utter, x, units, scales, biases):
    rows, length, _ = x.shape
    for row in range(rows):
        unit, scale = stats(x[row].astype(F32))
        units[row] = unit
        scales[row] = jnp.broadcast_to(scale, scales.shape[1:])
        visible_bias(biases.at[row], utter, row, length // SEG)


def turned(dy):
    def body(dy, out):
        out[...] = dy[...].T

    return call(body, "turned", 1, 1, [(full(dy.shape[::-1], BF), False)], [], [dy])[0]


def early(utter, x):
    rows, length, model = x.shape
    return pl.pallas_call(
        early_body,
        in_specs=[pl.BlockSpec(memory_space=pltpu.SMEM), VMEM],
        out_specs=[VMEM] * 3,
        out_shape=[
            full((rows, length, model), F32),
            full((rows, length, 128), F32),
            full((rows, length // QB, KEYS, QB), F32),
        ],
        compiler_params=params(),
        name="early",
        cost_estimate=cost(2),
    )(utter, x)


def front_body(row, first_call, plan, width, x, units, biases, vecs_in, w_in_in, w_out_in, *refs):
    nparts = len(plan) if first_call else 0
    parts = refs[:nparts]
    outs = refs[nparts:]
    if first_call:
        vecs, w_in, w_out, *outs = outs
    else:
        vecs, w_in, w_out = vecs_in, w_in_in, w_out_in
    (q_out, k_out, v_out, wide_out, p_out, att_out, resid_out) = outs[:7]
    (n2_out, n2t_out, unit_out, scale_out, att, *outs) = outs[7:]
    length, model = x.shape[1], x.shape[2]
    value = x[row].astype(F32)
    if first_call:
        (small,) = outs
        segments = [(band * width, width, w_in, band * model) for band in range(3)]
        segments += [(3 * width, width, w_out, 0), (4 * width, EXTRA, small, 0)]
        assemble(plan, parts, segments)
        total = jnp.zeros((8, model), F32)
        ups = [jnp.zeros((1, model), F32) for _ in range(4)]
        for piece in range(model // width):
            found = small[piece * EXTRA : (piece + 1) * EXTRA].astype(F32)
            total = total + pltpu.roll(found, piece * width, 1)[:8]
            for part in range(4):
                place = (piece * 4 + part) * width
                ups[place // model] += pltpu.roll(found, place % model, 1)[8 + part : 9 + part]
        vecs[0:8] = total
        for part in range(4):
            vecs[8 + part : 9 + part] = ups[part]
        vecs[12:16] = jnp.zeros((4, model), F32)
    normed = (units[row] * vecs[0:1] + vecs[1:2]).astype(BF)
    summary = nn(averages(length), normed).astype(BF)
    wide = jnp.concatenate([normed, summary], axis=0)
    wide_out[...] = wide.T
    q_out[...] = ((nn(normed, w_in[:, :model]) + vecs[2:3]).astype(BF).astype(F32) * 0.125).astype(BF)
    k_out[...] = nn(wide, w_in[:, model : 2 * model]).astype(BF)
    v_out[...] = (nn(wide, w_in[:, 2 * model :]) + vecs[3:4]).astype(BF)
    attention(q_out, k_out, v_out, p_out, biases.at[row], att_out, att, length)
    resid = value + nn(att[...], w_out[...]) + vecs[4:5]
    resid_out[...] = resid
    unit, scale = stats(resid)
    unit_out[...] = unit
    scale_out[...] = jnp.broadcast_to(scale, scale_out.shape)
    normed = (unit * vecs[5:6] + vecs[6:7]).astype(BF)
    n2_out[...] = normed
    n2t_out[...] = normed.T


def front(row, x, units, biases, vecs, w_in, w_out, plan, parts, width):
    _, length, model = x.shape
    blocks = length // QB
    wide = length + blocks * SLOTS
    first_call = vecs is None
    outs = [
        full((length, model), BF),
        full((wide, model), BF),
        full((wide, model), BF),
        full((model, wide), BF),
        full((blocks, HEADS // 2, KEYS, 2 * QB), BF),
        full((model, length), BF),
        full((length, model), F32),
        full((length, model), BF),
        full((model, length), BF),
        full((length, model), F32),
        full((length, 128), F32),
    ]
    scratch = [pltpu.VMEM((length, model), BF)]
    if first_call:
        outs = [full((16, model), F32), full((model, 3 * model), BF), full((model, model), BF)] + outs
        pieces = model // width
        scratch += [pltpu.VMEM((pieces * EXTRA, model), BF)]
        args = [x, units, biases] + list(parts)
        specs = [VMEM] * len(args)

        def body(x, units, biases, *refs):
            front_body(row, True, plan, width, x, units, biases, None, None, None, *refs)
    else:
        args = [x, units, biases, vecs, w_in, w_out]
        specs = [VMEM] * 6
        body = functools.partial(front_body, row, False, plan, width)
    return pl.pallas_call(
        body,
        in_specs=specs,
        out_specs=[VMEM] * len(outs),
        out_shape=outs,
        scratch_shapes=scratch,
        compiler_params=params(),
        name=f"front{row}",
        cost_estimate=cost(7),
    )(*args)


def gelu_both(v):
    c = 0.7978845608028654
    a = 0.044715
    square = v * v
    half = 0.5 + 0.5 * jnp.tanh(v * (c + (c * a) * square))
    value = v * half
    return value, half + value * (1.0 - half) * (2 * c + (6 * c * a) * square)


def middle_body(rows, plan, width, *refs):
    n2s = refs[:rows]
    dyt, vecs, *refs = refs[rows:]
    parts = refs[: len(plan)]
    hidden, slopes, up, grads = refs[len(plan) :]
    put = pieces_into(grads)
    model, tokens = dyt.shape
    ff = up.shape[1]
    tall = ff * width // model
    assemble(plan, parts, [(0, width, up, 0)])
    length = n2s[0].shape[0]
    step = length
    for tile in range(ff // TILE):
        cols = slice(tile * TILE, (tile + 1) * TILE)
        for chunk in range(tokens // step):
            rows = slice(chunk * step, (chunk + 1) * step)
            at = chunk * step % length
            u = nn(n2s[chunk * step // length][at : at + step], up[:, cols]) + vecs[8 + tile : 9 + tile]
            value, slope = gelu_both(u)
            hidden[rows, cols] = value.astype(BF)
            slopes[rows, cols] = slope.astype(BF)
    for tile in range(ff // TILE):
        cols = slice(tile * TILE, (tile + 1) * TILE)
        grad = nn(dyt[...], hidden[:, cols]).astype(BF)
        for part in range(TILE // tall):
            inner_cols = slice(part * tall, (part + 1) * tall)
            outer_cols = slice(tile * TILE + part * tall, tile * TILE + (part + 1) * tall)
            device = tile * TILE // tall + part
            rows = slice(0, model)
            put(rows, outer_cols, grad[:, inner_cols], device, (rows, slice(0, tall)))


def middle(n2s, dyt, vecs, parts, plan, width, ff, fast):
    model, tokens = dyt.shape
    tall = ff * width // model
    shape = (2, 4, model, tall) if fast else (model, ff)
    outs = [
        (full((tokens, ff), BF), False),
        (full((tokens, ff), BF), False),
        (full((model, ff), BF), False),
        (full(shape, BF), False),
    ]
    body = functools.partial(middle_body, len(n2s), plan, width)
    args = [*n2s, dyt, vecs, *parts]
    return call(body, "middle", 8, len(args), outs, [], args)


def turn_body(plan, dy, slopes, *refs):
    parts = refs[: len(plan)]
    du, ub, down = refs[len(plan) :]
    tokens, model = dy.shape
    ff = down.shape[0]
    tall = plan[0][3]
    length = dy.shape[0] // 2
    assemble(plan, parts, [(0, tall, down, 0)])
    step = length
    for tile in range(ff // TILE):
        cols = slice(tile * TILE, (tile + 1) * TILE)
        sums = jnp.zeros((1, TILE), F32)
        for chunk in range(tokens // step):
            rows = slice(chunk * step, (chunk + 1) * step)
            back = nt(dy[rows], down[cols]).astype(BF).astype(F32) * slopes[rows, cols].astype(F32)
            du[rows, cols] = back.astype(BF)
            sums = sums + jnp.sum(back, axis=0, keepdims=True)
        ub[tile : tile + 1] = sums


def turn(dy, slopes, parts, plan):
    tokens, model = dy.shape
    ff = slopes.shape[1]
    outs = [
        (full((tokens, ff), BF), False),
        (full((ff // TILE, TILE), F32), False),
        (full((ff, model), BF), False),
    ]
    args = [dy, slopes, *parts]
    return call(functools.partial(turn_body, plan), "turn", 5, len(args), outs, [], args)


def rise_body(rows, width, *refs):
    n2ts = refs[:rows]
    du, grads, turned = refs[rows:]
    length = n2ts[0].shape[1]
    put = pieces_into(grads)
    for row in range(rows):
        turned[:, row * length : (row + 1) * length] = n2ts[row][...]
    for tile in range(du.shape[1] // TILE):
        cols = slice(tile * TILE, (tile + 1) * TILE)
        put_rows(put, nn(turned[...], du[:, cols]).astype(BF), width, cols)


def rise(n2ts, du, width, fast):
    tokens, ff = du.shape
    model = n2ts[0].shape[0]
    shape = (2, 4, width, ff) if fast else (model, ff)
    body = functools.partial(rise_body, len(n2ts), width)
    args = [*n2ts, du]
    scratch = [pltpu.VMEM((model, tokens), BF)]
    return call(body, "rise", 4, len(args), [(full(shape, BF), False)], scratch, args)[0]


def norm_back(grad, unit, scale):
    first = jnp.mean(grad, axis=-1, keepdims=True)
    second = jnp.mean(grad * unit, axis=-1, keepdims=True)
    return scale * (grad - first - unit * second)


def back_body(rows, *refs):
    units = refs[:rows]
    scales = refs[rows : 2 * rows]
    du, dy, vecs, up, w_out, dresid, datt, sums = refs[2 * rows :]
    tokens, model = dy.shape
    length = units[0].shape[0]
    step = length
    gains = jnp.zeros((1, model), F32)
    shifts = jnp.zeros((1, model), F32)
    biases = jnp.zeros((1, model), F32)
    downs = jnp.zeros((1, model), F32)
    for chunk in range(tokens // step):
        rows = slice(chunk * step, (chunk + 1) * step)
        at = chunk * step % length
        grad = nt(du[rows], up[...])
        unit = units[chunk * step // length][at : at + step]
        scale = scales[chunk * step // length][at : at + step, 0:1]
        gains = gains + jnp.sum(grad * unit, axis=0, keepdims=True)
        shifts = shifts + jnp.sum(grad, axis=0, keepdims=True)
        top = dy[rows].astype(F32)
        downs = downs + jnp.sum(top, axis=0, keepdims=True)
        total = top + norm_back(grad * vecs[5:6], unit, scale)
        biases = biases + jnp.sum(total, axis=0, keepdims=True)
        dresid[rows] = total
        datt[rows] = nt(total.astype(BF), w_out[...]).astype(BF)
    sums[0:1] = gains
    sums[1:2] = shifts
    sums[2:3] = biases
    sums[3:4] = downs


def back(units, scales, du, dy, vecs, up, w_out):
    tokens, model = dy.shape
    outs = [
        (full((tokens, model), F32), False),
        (full((tokens, model), BF), False),
        (full((4, model), F32), False),
    ]
    args = [*units, *scales, du, dy, vecs, up, w_out]
    return call(functools.partial(back_body, len(units)), "back", 8, len(args), outs, [], args)


def rear_body(row, q, k, v, p, datt, mixed, sums, dk, dv):
    length, model = q.shape
    extent = k.shape[0]
    base = row * length
    done = 0
    mixed[length:extent, 0:model] = jnp.zeros((extent - length, model), BF)
    for block in range(length // QB):
        first, _ = window(block, length)
        rows = slice(block * QB, (block + 1) * QB)
        own = slice(length + block * SLOTS, length + (block + 1) * SLOTS)
        span = slice(first, first + WIN)
        for pair in range(HEADS // 2):
            lanes = slice(pair * 128, (pair + 1) * 128)
            keys = jnp.concatenate([k[span, lanes], k[own, lanes]], axis=0)
            vals = jnp.concatenate([v[span, lanes], v[own, lanes]], axis=0)
            queries = head_pair(q[rows, lanes])
            tops = head_pair(datt[base + block * QB : base + (block + 1) * QB, lanes])
            probs = p[block, pair]
            wides = probs.astype(F32)
            back = nt(vals, tops)
            inner = jnp.sum(wides * back, axis=0, keepdims=True)
            dscores = (wides * (back - inner)).astype(BF)
            gv = nn(probs, tops)
            gk = nn(dscores, queries)
            for total, part in ((dv, gv), (dk, gk)):
                if done > first:
                    total[first:done, lanes] += part[: done - first]
                total[max(first, done) : first + WIN, lanes] = part[max(done - first, 0) : WIN]
                total[own, lanes] = part[WIN:]
            gq = diagonal(tn(keys, dscores)).T * 0.125
            mixed[rows, lanes] = gq.astype(BF)
        done = first + WIN
    mixed[:, model : 2 * model] = dk[...].astype(BF)
    mixed[:, 2 * model :] = dv[...].astype(BF)
    sums[0:1] = jnp.sum(mixed[:, 0:model].astype(F32), axis=0, keepdims=True)
    sums[1:2] = jnp.sum(mixed[:, 2 * model :].astype(F32), axis=0, keepdims=True)


def rear(row, q, k, v, p, datt):
    length, model = q.shape
    extent = k.shape[0]
    outs = [(full((extent, 3 * model), BF), False), (full((2, model), F32), False)]
    scratch = [pltpu.VMEM((extent, model), F32), pltpu.VMEM((extent, model), F32)]
    body = functools.partial(rear_body, row)
    return call(body, f"rear{row}", 7, 5, outs, scratch, [q, k, v, p, datt])


def base_body(rows, width, units, dresid, w_in, gub, back_sums, *refs):
    mixeds = refs[:rows]
    rear_sums = refs[rows : 2 * rows]
    wides = refs[2 * rows : 3 * rows]
    atts = refs[3 * rows : 4 * rows]
    grads, dnormed, sums = refs[4 * rows :]
    length, model = units.shape[1], units.shape[2]
    put = pieces_into(grads)
    for tile in range(3):
        cols = slice(tile * model, (tile + 1) * model)
        total = nn(wides[0][...], mixeds[0][:, cols])
        for row in range(1, rows):
            total = total + nn(wides[row][...], mixeds[row][:, cols])
        put_rows(put, total.astype(BF), width, cols)
    total = nn(atts[0][...], dresid[0:length].astype(BF))
    for row in range(1, rows):
        total = total + nn(atts[row][...], dresid[row * length : (row + 1) * length].astype(BF))
    put_rows(put, total.astype(BF), width, slice(3 * model, 4 * model))
    average = averages(length)
    gains = jnp.zeros((1, model), F32)
    shifts = jnp.zeros((1, model), F32)
    for row in range(rows):
        grad = nt(mixeds[row][...], w_in[...])
        grad = grad[:length] + tn(average, grad[length:].astype(BF))
        gains = gains + jnp.sum(grad * units[row], axis=0, keepdims=True)
        shifts = shifts + jnp.sum(grad, axis=0, keepdims=True)
        dnormed[row] = grad
    sums[0:1] = gains
    sums[1:2] = shifts
    sums[2:4] = wide_sum(*[part[...] for part in rear_sums])
    sums[4:8] = back_sums[...]
    sums[8:12] = gub[...]
    sums[12:16] = jnp.zeros((4, model), F32)
    if len(grads.shape) == 4:
        for device in range(model // width):
            block = [sums[0:8, device * width : (device + 1) * width]]
            for part in range(4):
                place = (device * 4 + part) * width
                row, low = 8 + place // model, place % model
                block.append(sums[row : row + 1, low : low + width])
            block.append(jnp.zeros((4, width), F32))
            block = jnp.concatenate(block, axis=0)
            block = jnp.concatenate([block, jnp.zeros((16, 128 - width), F32)], axis=1)
            put(None, None, block.astype(BF), device, (slice(0, 16), slice(4 * model, 4 * model + 128)))
            put(
                None,
                None,
                jnp.zeros((width - 16, 128), BF),
                device,
                (slice(16, width), slice(4 * model, 4 * model + 128)),
            )


def base(units, dresid, w_in, gub, back_sums, mixeds, rear_sums, wides, atts, width, fast):
    rows, length, model = units.shape
    shape = (2, 4, width, 4 * model + 128) if fast else (model, 4 * model)
    outs = [
        (full(shape, BF), False),
        (full((rows, length, model), F32), False),
        (full((16, model), F32), False),
    ]
    args = [units, dresid, w_in, gub, back_sums, *mixeds, *rear_sums, *wides, *atts]
    return call(functools.partial(base_body, rows, width), "base", 6, len(args), outs, [], args)


def shed_body(units, scales, dresid, vecs, dnormed, dx):
    rows, length, _ = units.shape
    for row in range(rows):
        own = dresid[row * length : (row + 1) * length]
        dx[row] = own + norm_back(dnormed[row] * vecs[0:1], units[row], scales[row, :, 0:1])


def shed(units, scales, dresid, vecs, dnormed):
    args = [units, scales, dresid, vecs, dnormed]
    return call(shed_body, "shed", 2, 5, [(full(units.shape, F32), False)], [], args)[0]


def finish_body(rows, vecs, hidden, down, *refs):
    resids = refs[:rows]
    out = refs[rows]
    length = resids[0].shape[0]
    step = length
    for chunk in range(hidden.shape[0] // step):
        rows = slice(chunk * step, (chunk + 1) * step)
        at = chunk * step % length
        resid = resids[chunk * step // length][at : at + step]
        out[rows] = (resid + nn(hidden[rows], down[...]) + vecs[7:8]).astype(BF)


def finish(vecs, hidden, down, resids):
    outs = [(full((hidden.shape[0], down.shape[1]), BF), False)]
    args = [vecs, hidden, down, *resids]
    return call(functools.partial(finish_body, len(resids)), "finish", 4, len(args), outs, [], args)[0]


def along(value, offset):
    return lax.ppermute(value, "fsdp", [(i, i ^ offset) for i in range(8)])


def across(value, offset, size):
    return lax.ppermute(value, "dp", [(i, i ^ offset) for i in range(size)])


def pack_body(*refs):
    sources, out = refs[:11], refs[11]
    w_in, w_out, *rows, sem = refs[12:]
    width, model = w_out.shape
    targets = [w_in, w_out, *rows]
    copies = [pltpu.make_async_copy(a, b, sem) for a, b in zip(sources, targets)]
    for copy in copies:
        copy.start()
    out[4 * width :] = jnp.zeros((EXTRA, model), BF)
    for copy in copies:
        copy.wait()
    for band in range(3):
        out[band * width : (band + 1) * width] = w_in[:, band * model : (band + 1) * model]
    out[3 * width : 4 * width] = w_out[...]
    lines = [row[...].astype(F32).reshape(1, width) for row in rows[:8]]
    bias = rows[8][...].astype(F32).reshape(1, 4 * width)
    lines += [bias[:, at * width : (at + 1) * width] for at in range(4)]
    lines += [jnp.zeros((4, width), F32)]
    out[4 * width :, 0:width] = jnp.concatenate(lines, axis=0).astype(BF)


def pack(project_in, project_out, vectors, up_bias):
    width, model = project_out.shape
    outs = [(full((4 * width + EXTRA, model), BF), False)]
    args = [project_in, project_out, *vectors, up_bias]
    scratch = [pltpu.VMEM(arg.shape, BF) for arg in args] + [pltpu.SemaphoreType.DMA]
    return call(pack_body, "pack", 2, 0, outs, scratch, args, 60 * 2**20)[0]


def settle_body(width, tall, small, *refs):
    me = lax.axis_index("fsdp")
    value = small[...]
    model = value.shape[1]
    turned = pltpu.roll(value, lax.rem(model - me * width, model), 1)
    for row, out in enumerate(refs[:8]):
        out[...] = turned[row : row + 1, 0:width].reshape(width)
    place = me * tall
    wide = jnp.zeros((1, model), F32)
    for row in range(4):
        wide = jnp.where(place // model == row, value[8 + row : 9 + row], wide)
    wide = jnp.concatenate([wide] * 8, axis=0)
    turned = pltpu.roll(wide, lax.rem(model - lax.rem(place, model), model), 1)
    refs[8][...] = turned[0:1, 0:tall].reshape(tall)


def settle(small, width, tall):
    outs = [(full((width,), F32), False)] * 8 + [(full((tall,), F32), False)]
    return call(functools.partial(settle_body, width, tall), "settle", 2, 1, outs, [], [small])


def wide_sum(*values):
    total = values[0].astype(F32)
    for value in values[1:]:
        total = total + value.astype(F32)
    return total


def plus(*values):
    def body(*refs):
        refs[-1][...] = wide_sum(*[ref[...] for ref in refs[:-1]]).astype(refs[-1].dtype)

    outs = [(full(values[0].shape, values[0].dtype), False)]
    return call(body, "plus", 1, len(values), outs, [], values)[0]


def plus_here(both, there):
    def body(both, there, out):
        out[...] = wide_sum(both[0], there[...]).astype(BF)

    return call(body, "plus", 1, 2, [(full(there.shape, BF), False)], [], [both, there])[0]


def own_sum(held, *others):
    return wide_sum(held[0], *[other[...] for other in others]).astype(BF)


def cross_halves(held):
    def body(held, to_x, to_y):
        half = held.shape[1] // 2
        to_x[0] = held[1, :half]
        to_x[1] = held[3, :half]
        to_y[0] = held[2, half:]
        to_y[1] = held[3, half:]

    _, rows, columns = held.shape
    outs = [(full((2, rows // 2, columns), BF), False)] * 2
    return call(body, "cross_halves", 1, 1, outs, [], [held])


def second(held, from_x, from_y):
    def body(held, from_x, from_y, to_x, to_y):
        half = held.shape[1] // 2
        to_x[...] = wide_sum(held[1, half:], from_y[1]).astype(BF)
        to_y[...] = wide_sum(held[2, :half], from_x[1]).astype(BF)

    outs = [(full(from_x.shape[1:], BF), False)] * 2
    return call(body, "second", 1, 3, outs, [], [held, from_x, from_y])


def hop_halves(*args):
    def body(held, from_x, from_y, last_x, last_y, keep, send):
        half = keep.shape[0]
        top = wide_sum(held[0, :half], from_x[0], last_y[...]).astype(BF)
        bottom = wide_sum(held[0, half:], from_y[0], last_x[...]).astype(BF)
        odd = odd_plane()

        @pl.when(odd)
        def _():
            keep[...] = bottom
            send[...] = top

        @pl.when(jnp.logical_not(odd))
        def _():
            keep[...] = top
            send[...] = bottom

    _, rows, columns = args[0].shape
    outs = [(full((rows // 2, columns), BF), False)] * 2
    return call(body, "hop_halves", 1, 5, outs, [], args)


def odd_plane():
    return lax.rem(lax.axis_index("dp"), 2) == 1


def by_halves(*args):
    def body(*refs):
        keep, send = refs[-2:]
        total = own_sum(*refs[:-2])
        half = keep.shape[0]
        odd = odd_plane()

        @pl.when(odd)
        def _():
            keep[...] = total[half:]
            send[...] = total[:half]

        @pl.when(jnp.logical_not(odd))
        def _():
            keep[...] = total[:half]
            send[...] = total[half:]

    rows, columns = args[1].shape
    outs = [(full((rows // 2, columns), BF), False)] * 2
    return call(body, "by_halves", 1, len(args), outs, [], args)


def by_quarters(*args):
    def body(*refs):
        outs = refs[-5:-1]
        whole = refs[-1]
        whole[...] = own_sum(*refs[:-5])
        rows = outs[0].shape[0]
        me = lax.axis_index("dp")
        for offset, out in enumerate(outs):
            place = pl.multiple_of(jnp.bitwise_xor(me, offset) * rows, rows)
            out[...] = whole[pl.ds(place, rows), :]

    rows, columns = args[1].shape
    outs = [(full((rows // 4, columns), BF), False)] * 4
    scratch = [pltpu.VMEM((rows, columns), BF)]
    return call(body, "by_quarters", 1, len(args), outs, scratch, args)


def last_down(keep, other):
    def body(keep, other, out):
        half = keep.shape[0]
        odd = odd_plane()

        @pl.when(odd)
        def _():
            out[:, :half] = other[...].astype(F32).T
            out[:, half:] = keep[...].astype(F32).T

        @pl.when(jnp.logical_not(odd))
        def _():
            out[:, :half] = keep[...].astype(F32).T
            out[:, half:] = other[...].astype(F32).T

    half, tall = keep.shape
    return call(body, "last_down", 1, 2, [(full((tall, 2 * half), F32), False)], [], [keep, other])[0]


def last_up(keep, other):
    def body(keep, other, out):
        half = keep.shape[0]
        odd = odd_plane()

        @pl.when(odd)
        def _():
            out[:half] = other[...].astype(F32)
            out[half:] = keep[...].astype(F32)

        @pl.when(jnp.logical_not(odd))
        def _():
            out[:half] = keep[...].astype(F32)
            out[half:] = other[...].astype(F32)

    half, ff = keep.shape
    return call(body, "last_up", 1, 2, [(full((2 * half, ff), F32), False)], [], [keep, other])[0]


def last_in(quarters, model, width, tall):
    def body(*refs):
        parts, g_in, g_out, small = refs[:4], refs[4], refs[5], refs[15]
        vectors = refs[6:15]
        rows = parts[0].shape[0]
        me = lax.axis_index("dp")
        for offset, part in enumerate(parts):
            place = pl.multiple_of(jnp.bitwise_xor(me, offset) * rows, rows)
            g_in[pl.ds(place, rows), :] = part[:, : 3 * model].astype(F32)
            g_out[pl.ds(place, rows), :] = part[:, 3 * model : 4 * model].astype(F32)
            small[pl.ds(place, rows), :] = part[:, 4 * model :].astype(F32)
        for row in range(8):
            vectors[row][...] = small[row : row + 1, 0:width].reshape(width)
        wide = jnp.concatenate([small[8 + part : 9 + part, 0:width] for part in range(4)], axis=1)
        vectors[8][...] = wide.reshape(tall)

    outs = [(full((width, 3 * model), F32), False), (full((width, model), F32), False)]
    outs += [(full((width,), F32), False)] * 8 + [(full((tall,), F32), False)]
    scratch = [pltpu.VMEM((width, 128), F32)]
    return call(body, "last_in", 1, 4, outs, scratch, quarters)


def after(value, *others):
    return lax.optimization_barrier((value,) + others)[0]


def whole_plan(rows, size):
    return [(0, False, 0, rows, size)]


def near_plan(rows):
    return [(offset, True, 0, rows, 1) for offset in (0, 1, 2, 4, 6, 3, 5, 7)]


def shards(
    group,
    frames,
    upstream,
    utterance,
    first_gain,
    first_shift,
    project_in,
    query_bias,
    value_bias,
    project_out,
    out_bias,
    second_gain,
    second_shift,
    up_weight,
    up_bias,
    down_weight,
    down_bias,
):
    micro, nrows, length, model = frames.shape
    rows = micro * nrows
    width = project_out.shape[0]
    size = model // width
    ff = up_weight.shape[1]
    tall = ff // size
    x = frames.reshape(rows, length, model)
    dy = upstream.reshape(rows * length, model)
    utter = utterance.reshape(rows, length // SEG)
    vectors = (first_gain, first_shift, query_bias, value_bias, out_bias, second_gain, second_shift, down_bias)
    fast = size == 8 and group == 4 and rows == 2
    packed = pack(project_in, project_out, vectors, up_bias)
    if fast:
        plan_a, plan_u, plan_d = near_plan(packed.shape[0]), near_plan(width), near_plan(tall)
        a2, a4, a6, a1 = [along(packed, offset) for offset in (2, 4, 6, 1)]
        units, scales, biases = early(after(utter, a1), x)
        a6, units = lax.optimization_barrier((a6, units))
        up_piece = after(up_weight, a6)
        dyt = turned(after(dy, a6))
        a2, a4, dyt = lax.optimization_barrier((a2, a4, dyt))
        u2, u4, u1 = along(up_piece, 2), along(up_piece, 4), along(up_piece, 1)
        parts_a = [packed, a1, a2, a4, a6, along(a2, 1), along(a4, 1)] + [along(a6, 1)]
        u6 = along(up_piece, 6)
        first = after(x, u1)
    else:
        plan_a, plan_u, plan_d = whole_plan(packed.shape[0], size), whole_plan(width, size), whole_plan(tall, size)
        parts_a = [lax.all_gather(packed, "fsdp", axis=0, tiled=True)]
        parts_u = [lax.all_gather(up_weight, "fsdp", axis=0, tiled=True)]
        parts_d = [lax.all_gather(down_weight, "fsdp", axis=0, tiled=True)]
        first = x
        units, scales, biases = early(utter, x)
        dyt = turned(dy)
    saved = []
    vecs, w_in, w_out, *first = front(0, first, units, biases, None, None, None, plan_a, parts_a, width)
    saved.append(first)
    held = vecs
    if fast:
        held = after(vecs, u2, u4)
        done = first[-1]
        u3, u5 = along(after(u2, done), 1), along(after(u4, done), 1)
    for row in range(1, rows):
        saved.append(front(row, x, units, biases, held, w_in, w_out, plan_a, None, width))
    qs, ks, vs, wides, ps, atts, resids, n2s, n2ts, unit2s, scale2s = zip(*saved)
    if fast:
        down_piece = after(down_weight, n2s[0])
        d2, d4 = along(down_piece, 2), along(down_piece, 4)
        u6, u3, u5, done = lax.optimization_barrier((u6, u3, u5, n2s[1]))
        parts_u = [up_piece, u1, u2, u4, u6, u3, u5, along(u6, 1)]
        down_piece, done = lax.optimization_barrier((down_piece, done))
        d6 = along(down_piece, 6)
        d2, d4, done = lax.optimization_barrier((d2, d4, done))
        held = after(vecs, d2, d4)
        d3, d5, d1 = along(d2, 1), along(d4, 1), along(after(down_piece, d2), 1)
    hidden, slopes, up, gdown = middle(n2s, dyt, held, parts_u, plan_u, width, ff, fast)
    if fast:
        d6 = after(d6, slopes)
        parts_d = [down_piece, d1, d2, d4, d6, d3, d5, along(d6, 1)]
    if fast:
        du, gub, down = turn(dy, slopes, parts_d, plan_d)
        d_core = along(after(gdown, gub)[1], 1)
        gup = rise(n2ts, du, width, fast)
        d_sum = plus_here(gdown, after(d_core, gup))
        to_x, to_y = cross_halves(d_sum)
        d_x, d_y = along(to_x, 2), along(to_y, 4)
        u_core = along(gup[1], 1)
        dresid, datt, sums2 = back(unit2s, scale2s, after(du, to_x), dy, vecs, up, w_out)
        u_core, done = lax.optimization_barrier((u_core, sums2))
        u_sum = plus_here(gup, u_core)
        to_x, to_y = cross_halves(u_sum)
        u_x, u_y = along(to_x, 2), along(to_y, 4)
        mixed0, sums0 = rear(0, after(qs[0], to_x), ks[0], vs[0], ps[0], datt)
        d_x, d_y, done = lax.optimization_barrier((d_x, d_y, sums0))
        to_x, to_y = second(d_sum, d_x, d_y)
        d_x2, d_y2 = along(to_x, 2), along(to_y, 4)
        mixed1, sums1 = rear(1, after(qs[1], to_x), ks[1], vs[1], ps[1], datt)
        u_x, u_y, d_x2, d_y2, done = lax.optimization_barrier((u_x, u_y, d_x2, d_y2, sums1))
        to_x, to_y = second(u_sum, u_x, u_y)
        u_x2, u_y2 = along(to_x, 2), along(to_y, 4)
        d_keep, d_send = hop_halves(d_sum, d_x, d_y, d_x2, d_y2)
        d_z = across(d_send, 1, group)
        mixeds = (mixed0, mixed1)
        gin, dnormed, small = base(
            units,
            after(dresid, to_x, d_send),
            w_in,
            gub,
            sums2,
            mixeds,
            (sums0, sums1),
            wides,
            atts,
            width,
            fast,
        )
        u_x2, u_y2, d_z, done = lax.optimization_barrier((u_x2, u_y2, d_z, small))
        u_keep, u_send = hop_halves(u_sum, u_x, u_y, u_x2, u_y2)
        u_z = across(u_send, 1, group)
        d_keep = plus(d_keep, d_z)
        d_z2 = across(d_keep, 2, group)
        i_core = along(after(gin, u_send, d_keep)[1], 1)
        i_sum = plus_here(gin, i_core)
        i_got = [along(i_sum[1], 2), along(i_sum[2], 4), along(i_sum[3], 6)]
        out = finish(after(vecs, i_sum), hidden, down, resids)
        dx = shed(units, scales, dresid, after(vecs, out), dnormed)
        *i_got, done = lax.optimization_barrier((*i_got, dx))
        u_z, d_z2, done = lax.optimization_barrier((u_z, d_z2, i_sum))
        u_keep = plus(u_keep, u_z)
        u_z2 = across(u_keep, 2, group)
        d_keep = plus(d_keep, d_z2)
        d_other = across(d_keep, 1, group)
        i_own, *i_send = by_quarters(i_sum, *i_got)
        i_got = [across(i_send[offset - 1], offset, group) for offset in (3, 2, 1)]
        u_keep = plus(u_keep, u_z2)
        u_other = across(u_keep, 1, group)
        i_own = plus(i_own, *i_got)
        i_got = [across(i_own, offset, group) for offset in (3, 2, 1)][::-1]
        gdown = last_down(after(d_keep, i_own), d_other)
        g_up = last_up(after(u_keep, i_own), u_other)
        g_in, g_out, *vectors = last_in([i_own, *i_got], model, width, tall)
    else:
        du, gub, down = turn(dy, slopes, parts_d, plan_d)
        dresid, datt, sums2 = back(unit2s, scale2s, du, dy, vecs, up, w_out)
        gup = rise(n2ts, du, width, fast)
        pairs = [rear(row, qs[row], ks[row], vs[row], ps[row], datt) for row in range(rows)]
        mixeds, rear_sums = zip(*pairs)
        gin, dnormed, small = base(
            units, dresid, w_in, gub, sums2, mixeds, rear_sums, wides, atts, width, fast
        )
        dx = shed(units, scales, dresid, vecs, dnormed)
        out = finish(vecs, hidden, down, resids)

        def total(value, dim):
            own = lax.psum_scatter(value, "fsdp", scatter_dimension=dim, tiled=True)
            return lax.psum(own, "dp").astype(F32)

        gdown = total(gdown, 1).T
        g_up = total(gup, 0)
        gin = total(gin, 0)
        g_in, g_out = gin[:, : 3 * model], gin[:, 3 * model :]
        vectors = settle(lax.psum(small, ("dp", "fsdp")), width, tall)
    return (
        out.reshape(frames.shape),
        dx.reshape(frames.shape),
        vectors[0],
        vectors[1],
        g_in,
        vectors[2],
        vectors[3],
        g_out,
        vectors[6],
        vectors[4],
        vectors[5],
        g_up,
        vectors[8],
        gdown,
        vectors[7],
    )


def solution(mesh):
    rows = P(None, ("dp", "fsdp"), None, None)
    vector = P("fsdp")
    matrix = P("fsdp", None)
    weights = (vector, vector, matrix, vector, vector, matrix, vector, vector, vector, matrix, vector, matrix, vector)
    return jax.shard_map(
        functools.partial(shards, mesh.shape["dp"]),
        mesh=mesh,
        in_specs=(rows, rows, P(None, ("dp", "fsdp"), None)) + weights,
        out_specs=(rows, rows) + weights,
        check_vma=False,
    )
```
